32 devices in a mesh: pipe: 2 (over x), dp: 16 (over z, y, core).
Axes of the slice: x: 2, y: 2, z: 4, core: 2. Of those that a mesh axis runs over, the one named last changes fastest.
Arguments:
- inputs: bfloat16 [4, 8192, 768], P(None, 'dp'), may hold values from -6 to 6
- bucket: int32 [4], replicated, may hold values from 128 to 512, as said below
- plan: int32 [4], replicated, may hold values from 0 to 3, each once
- cotangent: bfloat16 [4, 8192, 768], P(None, 'dp'), may hold values from -6 to 6
- norm1_gain: float32 [2, 768], P('pipe'), may hold values from 0.25 to 1.75
- norm1_bias: float32 [2, 768], P('pipe'), may hold values from -2 to 2
- up_weight: bfloat16 [2, 768, 3072], P('pipe'), may hold values from -0.21875 to 0.21875
- up_bias: float32 [2, 3072], P('pipe'), may hold values from -3 to 3
- down_weight: bfloat16 [2, 3072, 768], P('pipe'), may hold values from -0.109375 to 0.109375
- down_bias: float32 [2, 768], P('pipe'), may hold values from -2 to 2
- norm2_gain: float32 [2, 768], P('pipe'), may hold values from 0.25 to 1.75
- norm2_bias: float32 [2, 768], P('pipe'), may hold values from -2 to 2
Outputs:
- activations: float32 [2, 4, 8192, 768], P('pipe', None, 'dp')
- input_grad: float32 [2, 4, 8192, 768], P('pipe', None, 'dp')
- norm1_gain_grad: float32 [2, 768], P('pipe')
- norm1_bias_grad: float32 [2, 768], P('pipe')
- up_weight_grad: float32 [2, 768, 3072], P('pipe')
- up_bias_grad: float32 [2, 3072], P('pipe')
- down_weight_grad: float32 [2, 3072, 768], P('pipe')
- down_bias_grad: float32 [2, 768], P('pipe')
- norm2_gain_grad: float32 [2, 768], P('pipe')
- norm2_bias_grad: float32 [2, 768], P('pipe')
The draws below stay inside these ranges and needn't reach their ends.
Inputs may be any that keep to these rules, and one draw needn't show every extreme that they name: `bucket`: each entry is 128, 256 or 512; at least one entry is 512. `plan`: a permutation of the slots.
All inputs are finite; a program needn't handle non-finite values.
Results may differ from the reference program's by a relative error of at most 0.01.
Values may be sent and summed in bfloat16 or wider, within the bound.
A program may use at most 256 MiB of HBM per device.

```python
import math
from functools import partial
import jax
import jax.numpy as jnp
from jax import lax

D = 768
FF = 3072
LMAX = 512
MB = 4
TOKENS = 8192


def draw_bucket(key, part):
    key = jax.random.fold_in(key, 7)
    level_key, forced_key = jax.random.split(key)
    levels = jax.random.randint(level_key, (MB,), 0, 3)
    forced = jax.random.randint(forced_key, (), 0, MB)
    levels = jnp.where(jnp.arange(MB) == forced, 2, levels)
    return jnp.where(levels == 0, LMAX // 4, jnp.where(levels == 1, LMAX // 2, LMAX)).astype(jnp.int32)


def block_levels(key, shape, cuts, smallest, top_value):
    def one(axis_at, parts):
        heights = jax.random.uniform(jax.random.fold_in(jax.random.fold_in(key, 6), axis_at), (parts,), jnp.float32, smallest / len(cuts), top_value / len(cuts))
        return jnp.repeat(jnp.exp(heights), shape[axis_at] // parts).reshape((-1,) + (1,) * (len(shape) - axis_at - 1))

    level = one(*cuts[0])
    for cut in cuts[1:]:
        level = level * one(*cut)
    return level


def noise(rng, extent, deviation, limit, shards=(), kind=jnp.bfloat16):
    loudness = block_levels(rng, extent, shards, -0.22, 0.18) if shards else 1.0
    array = jax.random.normal(rng, extent, jnp.float32) * deviation * loudness
    return jnp.minimum(jnp.maximum(array, -limit), limit).astype(kind)


def setup_inputs(seed: int = 0) -> dict:
    key_of = jax.random.split(jax.random.key(seed), 13)
    return {
        "inputs": noise(key_of[0], (MB, TOKENS, D), 1.0, 6.0, ((1, 16),)),
        "bucket": draw_bucket(jax.random.fold_in(key_of[12], 71), 0),
        "plan": jax.random.permutation(key_of[2], MB).astype(jnp.int32),
        "cotangent": noise(key_of[3], (MB, TOKENS, D), 1.0, 6.0, ((1, 16),)),
        "norm1_gain": jnp.clip(1.0 + 0.15 * jax.random.normal(key_of[4], (2, D), jnp.float32), 0.25, 1.75),
        "norm1_bias": noise(key_of[5], (2, D), 0.3, 2.0, ((0, 2),), jnp.float32),
        "up_weight": noise(key_of[6], (2, D, FF), D ** -0.5, 0.21875, ((0, 2),)),
        "up_bias": noise(key_of[7], (2, FF), 0.5, 3.0, ((0, 2),), jnp.float32),
        "down_weight": noise(key_of[8], (2, FF, D), FF ** -0.5, 0.109375, ((0, 2),)),
        "down_bias": noise(key_of[9], (2, D), 0.3, 2.0, ((0, 2),), jnp.float32),
        "norm2_gain": jnp.clip(1.0 + 0.15 * jax.random.normal(key_of[10], (2, D), jnp.float32), 0.25, 1.75),
        "norm2_bias": noise(key_of[11], (2, D), 0.3, 2.0, ((0, 2),), jnp.float32),
    }


@jax.custom_vjp
def low(v):
    return lax.optimization_barrier(v.astype(jnp.bfloat16)).astype(jnp.float32)

@jax.custom_vjp
def low_back(v):
    return v

def low_keep(v):
    return (low(v), None)

def low_pass(kept, grad):
    return (grad,)

def back_keep(v):
    return (v, None)

def back_low(kept, grad):
    return (low(grad),)
low.defvjp(low_keep, low_pass)
low_back.defvjp(back_keep, back_low)

def layer_norm(values, gain, offset):
    average = lax.optimization_barrier(jnp.mean(values, axis=-1, keepdims=True))
    centered = values - average
    variance = lax.optimization_barrier(jnp.mean(centered * centered, axis=-1, keepdims=True))
    return centered * lax.rsqrt(variance + 1e-06) * gain + offset

def seq_tables(length):
    positions = jnp.arange(LMAX, dtype=jnp.int32)
    row_pos = positions[:, None]
    col_pos = positions[None, :]
    same = row_pos // length == col_pos // length
    phase = row_pos % length * (col_pos % length) % length
    length_f = length.astype(jnp.float32)
    angle = 2.0 * math.pi * phase.astype(jnp.float32) / length_f
    scale = lax.rsqrt(length_f)
    cosine = jnp.where(same, jnp.cos(angle) * scale, 0.0)
    sine = jnp.where(same, jnp.sin(angle) * scale, 0.0)
    return (low(cosine), low(sine))

def hidden_tables():
    positions = jnp.arange(D, dtype=jnp.int32)
    phase = positions[:, None] * positions[None, :] % D
    width_f = jnp.float32(D)
    angle = 2.0 * math.pi * phase.astype(jnp.float32) / width_f
    scale = lax.rsqrt(width_f)
    return (low(jnp.cos(angle) * scale), low(jnp.sin(angle) * scale))

def matmul(left, right):
    return jnp.dot(left, right, preferred_element_type=jnp.float32, precision=lax.Precision.HIGHEST)

def seq_apply(table, values):
    blocks = values.reshape(-1, LMAX, values.shape[-1])
    result = jnp.einsum('ij,bjd->bid', table, blocks, precision=lax.Precision.HIGHEST)
    return result.reshape(values.shape)

def layer(values, length, weights, hidden_cos, hidden_sin):
    gain_one, bias_one, up_matrix, up_offset, down_matrix, down_offset, gain_two, bias_two = weights
    seq_cos, seq_sin = seq_tables(length)
    cos_part = low_back(low(matmul(values, hidden_cos)))
    sin_part = low_back(low(matmul(values, hidden_sin)))
    mixed = low_back(seq_apply(seq_cos, cos_part) - seq_apply(seq_sin, sin_part))
    normed = layer_norm(values + mixed, gain_one, bias_one)
    pre_act = low_back(matmul(low(normed), up_matrix) + up_offset)
    activated = low(jax.nn.gelu(pre_act, approximate=True))
    branch = low_back(matmul(activated, down_matrix) + down_offset)
    return layer_norm(normed + branch, gain_two, bias_two)

def reference(inputs, bucket, plan, cotangent, norm1_gain, norm1_bias, up_weight, up_bias, down_weight, down_bias, norm2_gain, norm2_bias):
    hidden_cos, hidden_sin = hidden_tables()
    first_in = inputs.astype(jnp.float32)[plan]
    params = (norm1_gain.astype(jnp.float32), norm1_bias.astype(jnp.float32), up_weight.astype(jnp.float32), up_bias.astype(jnp.float32), down_weight.astype(jnp.float32), down_bias.astype(jnp.float32), norm2_gain.astype(jnp.float32), norm2_bias.astype(jnp.float32))
    group_rows = 8 * LMAX
    blocks_per = TOKENS // group_rows
    lengths = jnp.repeat(bucket, blocks_per, total_repeat_length=MB * blocks_per)

    def block_pair(params_in, block, linkage, length):
        weights_zero = tuple((p[0] for p in params_in))
        weights_one = tuple((p[1] for p in params_in))
        out_zero = layer(block, length, weights_zero, hidden_cos, hidden_sin)
        carried = low_back(low(out_zero + linkage))
        out_one = layer(carried, length, weights_one, hidden_cos, hidden_sin)
        return (out_zero, out_one)

    def forward(first, linkage, params_in):
        runner = jax.checkpoint(partial(block_pair, params_in))

        def apply_one(element):
            return runner(element[0], element[1], element[2])
        shaped = first.reshape(MB * blocks_per, group_rows, D)
        link_shaped = linkage.reshape(MB * blocks_per, group_rows, D)
        out_zero, out_one = lax.map(apply_one, (shaped, link_shaped, lengths))
        return (out_zero.reshape(MB, TOKENS, D), out_one.reshape(MB, TOKENS, D))
    linkage = jnp.zeros_like(first_in)
    outputs, pullback = jax.vjp(forward, first_in, linkage, params)
    grad_first, grad_link, grad_params = pullback((jnp.zeros_like(outputs[0]), cotangent.astype(jnp.float32)))
    return (jnp.stack([outputs[0], outputs[1]]), jnp.stack([grad_first, grad_link]), grad_params[0], grad_params[1], grad_params[2], grad_params[3], grad_params[4], grad_params[5], grad_params[6], grad_params[7])
```

```python
import functools
import math

import jax
import jax.numpy as jnp
import ml_dtypes
import numpy as np
from jax import lax
from jax.experimental import pallas as pl
from jax.experimental.pallas import tpu as pltpu
from jax.sharding import PartitionSpec as P

BF = jnp.bfloat16
F32 = jnp.float32
TANH_IN = math.sqrt(2.0 / math.pi)
TANH_CUBE = TANH_IN * 0.044715
EPS = 1e-6
CHUNKS = 4


def hidden_tables(width):
    position = np.arange(width)
    angle = 2.0 * np.pi * (np.outer(position, position) % width) / width
    pair = np.stack([np.cos(angle), np.sin(angle)]) / np.sqrt(width)
    return pair.astype(ml_dtypes.bfloat16)


def seq_tables(rows):
    position = np.arange(rows)
    found = []
    for length in (rows // 4, rows // 2, rows):
        same = position[:, None] // length == position[None, :] // length
        phase = (position[:, None] % length) * (position[None, :] % length) % length
        angle = 2.0 * np.pi * phase / length
        found.append(
            np.stack(
                [
                    np.where(same, np.cos(angle), 0.0) / np.sqrt(length),
                    np.where(same, -np.sin(angle), 0.0) / np.sqrt(length),
                ]
            )
        )
    return np.stack(found).astype(ml_dtypes.bfloat16)


def dot(left, right):
    return jnp.dot(left, right, preferred_element_type=F32)


def dot_t(left, right):
    return lax.dot_general(left, right, (((1,), (1,)), ((), ())), preferred_element_type=F32)


def fold8(values):
    return jnp.sum(values.reshape(-1, 8, values.shape[-1]), axis=0)


def layers_kernel(
    count, rows, width, blocks, fb,
    bucket, plan, norm_ref, upb_ref, in_hbm, cot_hbm, wu_hbm, wd_hbm, htab_hbm, stab_hbm,
    act_hbm, grad_hbm, h_hbm, du_hbm, a_hbm, df_hbm, small_ref,
    wu, wd, htab, stab, inbuf, recv, sendbuf, deriv, xh1, xh2, rstd,
    hst, pq, u0, u1, acc, low, yst, xst, sums,
    w_sem, t_sem, o_sem, h_sem, send_sem, recv_sem,
):
    first = lax.axis_index("pipe") == 0
    partner = 1 - lax.axis_index("pipe")
    last = blocks - 1

    def wu_copy(b):
        return pltpu.make_async_copy(wu_hbm.at[0, :, pl.ds(b * fb, fb)], wu.at[b], w_sem.at[b])

    def wd_copy(b):
        return pltpu.make_async_copy(wd_hbm.at[0, pl.ds(b * fb, fb), :], wd.at[b], w_sem.at[blocks + b])

    in_copy = pltpu.make_async_copy(in_hbm, inbuf, t_sem.at[0])
    cot_copy = pltpu.make_async_copy(cot_hbm, inbuf, t_sem.at[0])
    htab_copy = pltpu.make_async_copy(htab_hbm, htab, t_sem.at[1])
    stab_copy = pltpu.make_async_copy(stab_hbm, stab, t_sem.at[2])

    @pl.when(first)
    def _():
        in_copy.start()

    htab_copy.start()
    stab_copy.start()
    for b in range(blocks):
        wu_copy(b).start()
        wd_copy(b).start()

    @pl.when(jnp.logical_not(first))
    def _():
        cot_copy.start()

    sums[...] = jnp.zeros_like(sums)

    barrier = pltpu.get_barrier_semaphore()
    pl.semaphore_signal(barrier, inc=1, device_id={"pipe": partner}, device_id_type=pl.DeviceIdType.MESH)
    pl.semaphore_wait(barrier, 1)

    span = rows // CHUNKS

    def chunk_copy(k, c):
        part = pl.ds(c * span, span)
        return pltpu.make_async_remote_copy(
            src_ref=sendbuf.at[k, part],
            dst_ref=recv.at[k, part],
            send_sem=send_sem.at[k, c],
            recv_sem=recv_sem.at[k, c],
            device_id={"pipe": partner},
            device_id_type=pl.DeviceIdType.MESH,
        )

    def act_copy(k):
        return pltpu.make_async_copy(yst, act_hbm.at[0, k], o_sem.at[0])

    def grad_copy(k):
        return pltpu.make_async_copy(xst, grad_hbm.at[0, k], o_sem.at[1])

    def a_copy(k):
        return pltpu.make_async_copy(low, a_hbm.at[k], o_sem.at[2])

    def df_copy(k):
        return pltpu.make_async_copy(low, df_hbm.at[k], o_sem.at[2])

    def h_copy(k, b):
        return pltpu.make_async_copy(hst.at[b], h_hbm.at[b, k], h_sem.at[b])

    def du_copy(k, b):
        return pltpu.make_async_copy(hst.at[b], du_hbm.at[b, k], h_sem.at[b])

    def arrived(k):
        for c in range(CHUNKS):
            chunk_copy(k, c).wait_recv()

    half = rows // 2
    halves = (slice(0, half), slice(half, rows))
    tiles = [slice(r, r + span) for r in range(0, rows, span)]
    g1 = norm_ref[0:1, :]
    b1 = norm_ref[1:2, :]
    g2 = norm_ref[2:3, :]
    b2 = norm_ref[3:4, :]
    bd = norm_ref[4:5, :]

    def normalized(values):
        centered = values - jnp.mean(values, axis=-1, keepdims=True)
        scale = lax.rsqrt(jnp.mean(centered * centered, axis=-1, keepdims=True) + EPS)
        return centered * scale, scale

    def norm_back(grad, gain, unit, scale):
        scaled = grad * gain
        mean_one = jnp.mean(scaled, axis=-1, keepdims=True)
        mean_two = jnp.mean(scaled * unit, axis=-1, keepdims=True)
        return scale * (scaled - mean_one - unit * mean_two)

    def forward(k, step):
        source = plan[k]
        length = bucket[k]
        level = jnp.where(length == rows, 2, jnp.where(length * 2 == rows, 1, 0))

        @pl.when(step == 0)
        def _():
            htab_copy.wait()

        @pl.when(jnp.logical_and(step == 0, first))
        def _():
            in_copy.wait()

        @pl.when(first)
        def _():
            recv[k] = inbuf[source]

        @pl.when(jnp.logical_not(first))
        def _():
            arrived(k)

        pq[0] = dot(recv[k], htab[0]).astype(BF)
        pq[1] = dot(recv[k], htab[1]).astype(BF)

        @pl.when(step == 0)
        def _():
            stab_copy.wait()

        @pl.when(step > 0)
        def _():
            a_copy(k).wait()
            for b in range(blocks):
                h_copy(k, b).wait()

        for part in halves:
            mixed = dot(stab[level, 0, part, :], pq[0]) + dot(stab[level, 1, part, :], pq[1])
            unit, scale = normalized(recv[k, part, :].astype(F32) + mixed)
            xh1[k, part, :] = unit.astype(BF)
            rstd[k, part, 0:1] = scale
            value = unit * g1 + b1
            low[part, :] = value.astype(BF)
            acc[part, :] = value + bd
        a_copy(k).start()

        @pl.when(step == 0)
        def _():
            for b in range(blocks):
                wu_copy(b).wait()
                wd_copy(b).wait()

        def up(b, u):
            u[...] = dot(low[...], wu[b])

        def activate(b, u):
            pre = u[...] + upb_ref[b]
            square = pre * pre
            level_half = 0.5 * jnp.tanh(pre * (TANH_IN + TANH_CUBE * square)) + 0.5
            value = pre * level_half
            slope = level_half + value * (1.0 - level_half) * (2.0 * TANH_IN + 6.0 * TANH_CUBE * square)
            hst[b] = value.astype(BF)
            deriv[k, b] = slope.astype(BF)

        def down(b):
            acc[...] += dot(hst[b], wd[b])

        buffers = (u0, u1)
        up(0, u0)
        for b in range(blocks):
            if b + 1 < blocks:
                up(b + 1, buffers[(b + 1) % 2])
            if b > 0:
                down(b - 1)
            activate(b, buffers[b % 2])
        down(last)
        for b in range(blocks):
            h_copy(k, b).start()

        @pl.when(k > 0)
        def _():
            act_copy(k).wait()

        for c, part in enumerate(tiles):
            unit, scale = normalized(acc[part, :])
            xh2[k, part, :] = unit.astype(BF)
            rstd[k, part, 1:2] = scale
            value = unit * g2 + b2
            yst[part, :] = value

            @pl.when(first)
            def _():
                sendbuf[k, part, :] = value.astype(BF)
                chunk_copy(k, c).start()

        act_copy(k).start()

    def backward(k, step):
        length = bucket[k]
        level = jnp.where(length == rows, 2, jnp.where(length * 2 == rows, 1, 0))

        @pl.when(jnp.logical_and(k == 0, jnp.logical_not(first)))
        def _():
            cot_copy.wait()

        df_copy(k).wait()
        for b in range(blocks):
            du_copy(k, b).wait()

        @pl.when(k > 0)
        def _():
            grad_copy(k).wait()

        @pl.when(first)
        def _():
            arrived(k)
            xst[...] = recv[k].astype(F32)

        @pl.when(jnp.logical_not(first))
        def _():
            xst[...] = inbuf[k].astype(F32)

        for part in tiles:
            grad = xst[part, :]
            unit = xh2[k, part, :].astype(F32)
            back = norm_back(grad, g2, unit, rstd[k, part, 1:2])
            rounded = back.astype(BF)
            low[part, :] = rounded
            acc[part, :] = back
            sums[2] += fold8(grad * unit)
            sums[3] += fold8(grad)
            sums[4] += fold8(rounded.astype(F32))
        df_copy(k).start()

        def up(b, u):
            u[...] = dot_t(low[...], wd[b])

        def activate(b, u):
            rounded = (u[...] * deriv[k, b].astype(F32)).astype(BF)
            hst[b] = rounded
            sums[5 + b] += fold8(rounded.astype(F32))

        def down(b):
            acc[...] += dot_t(hst[b], wu[b])

        buffers = (u0, u1)
        up(0, u0)
        for b in range(blocks):
            if b + 1 < blocks:
                up(b + 1, buffers[(b + 1) % 2])
            if b > 0:
                down(b - 1)
            activate(b, buffers[b % 2])
        down(last)
        for b in range(blocks):
            du_copy(k, b).start()

        for part in tiles:
            grad = acc[part, :]
            unit = xh1[k, part, :].astype(F32)
            back = norm_back(grad, g1, unit, rstd[k, part, 0:1])
            acc[part, :] = back
            recv[k, part, :] = back.astype(BF)
            sums[0] += fold8(grad * unit)
            sums[1] += fold8(grad)
        pq[0] = dot(stab[level, 0], recv[k]).astype(BF)
        pq[1] = dot(stab[level, 1], recv[k]).astype(BF)

        for i, part in enumerate(halves):
            value = acc[part, :] + dot(pq[0, part, :], htab[0]) + dot(pq[1, part, :], htab[1])
            rounded = value.astype(BF)
            xst[part, :] = jnp.where(first, value, rounded.astype(F32))

            @pl.when(jnp.logical_not(first))
            def _():
                sendbuf[k, part, :] = rounded
                for c in range(i * CHUNKS // 2, (i + 1) * CHUNKS // 2):
                    chunk_copy(k, c).start()

        grad_copy(k).start()

    def one(step, carry):
        forwards = jnp.where(first, step < count, lax.rem(step, 2) == 0)
        k = jnp.where(first, lax.rem(step, count), step // 2)

        @pl.when(forwards)
        def _():
            forward(k, step)

        @pl.when(jnp.logical_not(forwards))
        def _():
            backward(k, step)

        return carry

    lax.fori_loop(0, 2 * count, one, 0)

    end = count - 1

    for n in range(5 + blocks):
        small_ref[n : n + 1, :] = jnp.sum(sums[n], axis=0, keepdims=True)
    for n in range(5 + blocks, small_ref.shape[0]):
        small_ref[n : n + 1, :] = jnp.zeros((1, width), F32)
    act_copy(end).wait()
    grad_copy(end).wait()
    df_copy(end).wait()
    for b in range(blocks):
        du_copy(end, b).wait()
    for k in range(count):
        for c in range(CHUNKS):
            chunk_copy(k, c).wait_send()


def run_layers(bucket, plan, norms, up_bias, inputs, cotangent, up_weight, down_weight):
    count, rows, width = inputs.shape
    hidden = up_weight.shape[-1]
    fb = width
    blocks = hidden // fb
    htab = jnp.asarray(hidden_tables(width))
    stab = jnp.asarray(seq_tables(rows))
    any_spec = pl.BlockSpec(memory_space=pl.ANY)
    smem = pl.BlockSpec(memory_space=pltpu.SMEM)
    vmem = pl.BlockSpec(memory_space=pltpu.VMEM)
    shape = jax.ShapeDtypeStruct
    body = functools.partial(layers_kernel, count, rows, width, blocks, fb)
    flops = count * (12 * rows * width * hidden // 1 + 4 * rows * width * (2 * width + 2 * rows))
    return pl.pallas_call(
        body,
        out_shape=(
            shape((1, count, rows, width), F32),
            shape((1, count, rows, width), F32),
            shape((blocks, count, rows, fb), BF),
            shape((blocks, count, rows, fb), BF),
            shape((count, rows, width), BF),
            shape((count, rows, width), BF),
            shape((16, width), F32),
        ),
        in_specs=[smem, smem, vmem, vmem] + [any_spec] * 6,
        out_specs=(any_spec,) * 6 + (vmem,),
        scratch_shapes=[
            pltpu.VMEM((blocks, width, fb), BF),
            pltpu.VMEM((blocks, fb, width), BF),
            pltpu.VMEM((2, width, width), BF),
            pltpu.VMEM((3, 2, rows, rows), BF),
            pltpu.VMEM((count, rows, width), BF),
            pltpu.VMEM((count, rows, width), BF),
            pltpu.VMEM((count, rows, width), BF),
            pltpu.VMEM((count, blocks, rows, fb), BF),
            pltpu.VMEM((count, rows, width), BF),
            pltpu.VMEM((count, rows, width), BF),
            pltpu.VMEM((count, rows, 128), F32),
            pltpu.VMEM((blocks, rows, fb), BF),
            pltpu.VMEM((2, rows, width), BF),
            pltpu.VMEM((rows, fb), F32),
            pltpu.VMEM((rows, fb), F32),
            pltpu.VMEM((rows, width), F32),
            pltpu.VMEM((rows, width), BF),
            pltpu.VMEM((rows, width), F32),
            pltpu.VMEM((rows, width), F32),
            pltpu.VMEM((5 + blocks, 8, width), F32),
            pltpu.SemaphoreType.DMA((2 * blocks,)),
            pltpu.SemaphoreType.DMA((3,)),
            pltpu.SemaphoreType.DMA((3,)),
            pltpu.SemaphoreType.DMA((blocks,)),
            pltpu.SemaphoreType.DMA((count, CHUNKS)),
            pltpu.SemaphoreType.DMA((count, CHUNKS)),
        ],
        compiler_params=pltpu.CompilerParams(
            collective_id=0, has_side_effects=True, vmem_limit_bytes=63 * 2**20
        ),
        cost_estimate=pl.CostEstimate(flops=flops, bytes_accessed=60 * 2**20, transcendentals=0),
    )(bucket, plan, norms, up_bias, inputs, cotangent, up_weight, down_weight, htab, stab)


def per_device(
    inputs, bucket, plan, cotangent, norm1_gain, norm1_bias, up_weight, up_bias,
    down_weight, down_bias, norm2_gain, norm2_bias,
):
    count, rows, width = inputs.shape
    hidden = up_weight.shape[-1]
    norms = jnp.concatenate(
        [norm1_gain, norm1_bias, norm2_gain, norm2_bias, down_bias, jnp.zeros((3, width), F32)]
    )
    activations, input_grad, h, du, a, df, small = run_layers(
        bucket, plan, norms, up_bias.reshape(-1, 1, width), inputs, cotangent, up_weight, down_weight
    )
    up_grad = jnp.einsum("krd,bkrf->dbf", a, du, preferred_element_type=F32).reshape(1, width, hidden)
    down_grad = jnp.einsum("bkrf,krd->bfd", h, df, preferred_element_type=F32).reshape(1, hidden, width)
    up_grad, down_grad, small = lax.psum((up_grad, down_grad, small), "dp")
    blocks = hidden // width
    return (
        activations, input_grad, small[0:1], small[1:2], up_grad,
        small[5 : 5 + blocks].reshape(1, hidden), down_grad, small[4:5], small[2:3], small[3:4],
    )


def solution(mesh):
    row = P("pipe", None)
    weight = P("pipe", None, None)
    tokens = P(None, "dp", None)
    result = P("pipe", None, "dp", None)
    return jax.shard_map(
        per_device,
        mesh=mesh,
        in_specs=(tokens, P(), P(), tokens, row, row, weight, row, weight, row, row, row),
        out_specs=(result, result, row, row, weight, row, weight, row, row, row),
        check_vma=False,
    )
```

```python
import functools
import math

import jax
import jax.numpy as jnp
import ml_dtypes
import numpy as np
from jax import lax
from jax.experimental import pallas as pl
from jax.experimental.pallas import tpu as pltpu
from jax.sharding import PartitionSpec as P

BF = jnp.bfloat16
F32 = jnp.float32
TANH_IN = math.sqrt(2.0 / math.pi)
TANH_CUBE = TANH_IN * 0.044715
EPS = 1e-6
CHUNKS = 4


def hidden_tables(width):
    position = np.arange(width)
    angle = 2.0 * np.pi * (np.outer(position, position) % width) / width
    pair = np.stack([np.cos(angle), np.sin(angle)]) / np.sqrt(width)
    return pair.astype(ml_dtypes.bfloat16)


def seq_tables(rows):
    position = np.arange(rows)
    found = []
    for length in (rows // 4, rows // 2, rows):
        same = position[:, None] // length == position[None, :] // length
        phase = (position[:, None] % length) * (position[None, :] % length) % length
        angle = 2.0 * np.pi * phase / length
        found.append(
            np.stack(
                [
                    np.where(same, np.cos(angle), 0.0) / np.sqrt(length),
                    np.where(same, -np.sin(angle), 0.0) / np.sqrt(length),
                ]
            )
        )
    return np.stack(found).astype(ml_dtypes.bfloat16)


def dot(left, right):
    return jnp.dot(left, right, preferred_element_type=F32)


def dot_t(left, right):
    return lax.dot_general(left, right, (((1,), (1,)), ((), ())), preferred_element_type=F32)


def fold8(values):
    return jnp.sum(values.reshape(-1, 8, values.shape[-1]), axis=0)


def layers_kernel(
    count, rows, width, blocks, fb,
    bucket, plan, norm_ref, upb_ref, in_hbm, cot_hbm, wu_hbm, wd_hbm, htab_hbm, stab_hbm,
    act_hbm, grad_hbm, h_hbm, du_hbm, a_hbm, df_hbm, small_ref,
    wu, wd, htab, stab, inbuf, recv, sendbuf, deriv, xh1, xh2, rstd,
    hst, pq, u0, u1, acc, low, yst, xst, sums,
    w_sem, t_sem, o_sem, h_sem, send_sem, recv_sem,
):
    first = lax.axis_index("pipe") == 0
    partner = 1 - lax.axis_index("pipe")
    last = blocks - 1

    def wu_copy(b):
        return pltpu.make_async_copy(wu_hbm.at[0, :, pl.ds(b * fb, fb)], wu.at[b], w_sem.at[b])

    def wd_copy(b):
        return pltpu.make_async_copy(wd_hbm.at[0, pl.ds(b * fb, fb), :], wd.at[b], w_sem.at[blocks + b])

    in_copy = pltpu.make_async_copy(in_hbm, inbuf, t_sem.at[0])
    cot_copy = pltpu.make_async_copy(cot_hbm, inbuf, t_sem.at[0])
    htab_copy = pltpu.make_async_copy(htab_hbm, htab, t_sem.at[1])
    stab_copy = pltpu.make_async_copy(stab_hbm, stab, t_sem.at[2])

    @pl.when(first)
    def _():
        in_copy.start()

    htab_copy.start()
    stab_copy.start()
    for b in range(blocks):
        wu_copy(b).start()
        wd_copy(b).start()

    @pl.when(jnp.logical_not(first))
    def _():
        cot_copy.start()

    sums[...] = jnp.zeros_like(sums)

    barrier = pltpu.get_barrier_semaphore()
    pl.semaphore_signal(barrier, inc=1, device_id={"pipe": partner}, device_id_type=pl.DeviceIdType.MESH)
    pl.semaphore_wait(barrier, 1)

    span = rows // CHUNKS

    def chunk_copy(k, c):
        part = pl.ds(c * span, span)
        return pltpu.make_async_remote_copy(
            src_ref=sendbuf.at[k, part],
            dst_ref=recv.at[k, part],
            send_sem=send_sem.at[k, c],
            recv_sem=recv_sem.at[k, c],
            device_id={"pipe": partner},
            device_id_type=pl.DeviceIdType.MESH,
        )

    def act_copy(k):
        return pltpu.make_async_copy(yst, act_hbm.at[0, k], o_sem.at[0])

    def grad_copy(k):
        return pltpu.make_async_copy(xst, grad_hbm.at[0, k], o_sem.at[1])

    def a_copy(k):
        return pltpu.make_async_copy(low, a_hbm.at[k], o_sem.at[2])

    def df_copy(k):
        return pltpu.make_async_copy(low, df_hbm.at[k], o_sem.at[2])

    def h_copy(k, b):
        return pltpu.make_async_copy(hst.at[b], h_hbm.at[b, k], h_sem.at[b])

    def du_copy(k, b):
        return pltpu.make_async_copy(hst.at[b], du_hbm.at[b, k], h_sem.at[b])

    def arrived(k):
        for c in range(CHUNKS):
            chunk_copy(k, c).wait_recv()

    half = rows // 2
    halves = (slice(0, half), slice(half, rows))
    tiles = [slice(r, r + span) for r in range(0, rows, span)]
    g1 = norm_ref[0:1, :]
    b1 = norm_ref[1:2, :]
    g2 = norm_ref[2:3, :]
    b2 = norm_ref[3:4, :]
    bd = norm_ref[4:5, :]

    def normalized(values):
        centered = values - jnp.mean(values, axis=-1, keepdims=True)
        scale = lax.rsqrt(jnp.mean(centered * centered, axis=-1, keepdims=True) + EPS)
        return centered * scale, scale

    def norm_back(grad, gain, unit, scale):
        scaled = grad * gain
        mean_one = jnp.mean(scaled, axis=-1, keepdims=True)
        mean_two = jnp.mean(scaled * unit, axis=-1, keepdims=True)
        return scale * (scaled - mean_one - unit * mean_two)

    def forward(k, step):
        source = plan[k]
        length = bucket[k]
        level = jnp.where(length == rows, 2, jnp.where(length * 2 == rows, 1, 0))

        @pl.when(step == 0)
        def _():
            htab_copy.wait()

        @pl.when(jnp.logical_and(step == 0, first))
        def _():
            in_copy.wait()

        @pl.when(first)
        def _():
            recv[k] = inbuf[source]

        @pl.when(jnp.logical_not(first))
        def _():
            arrived(k)

        pq[0] = dot(recv[k], htab[0]).astype(BF)
        pq[1] = dot(recv[k], htab[1]).astype(BF)

        @pl.when(step == 0)
        def _():
            stab_copy.wait()

        @pl.when(step > 0)
        def _():
            a_copy(k).wait()
            for b in range(blocks):
                h_copy(k, b).wait()

        for part in halves:
            mixed = dot(stab[level, 0, part, :], pq[0]) + dot(stab[level, 1, part, :], pq[1])
            unit, scale = normalized(recv[k, part, :].astype(F32) + mixed)
            xh1[k, part, :] = unit.astype(BF)
            rstd[k, part, 0:1] = scale
            value = unit * g1 + b1
            low[part, :] = value.astype(BF)
            acc[part, :] = value + bd
        a_copy(k).start()

        @pl.when(step == 0)
        def _():
            for b in range(blocks):
                wu_copy(b).wait()
                wd_copy(b).wait()

        def up(b, u):
            u[...] = dot(low[...], wu[b])

        def activate(b, u):
            pre = u[...] + upb_ref[b]
            square = pre * pre
            level_half = 0.5 * jnp.tanh(pre * (TANH_IN + TANH_CUBE * square)) + 0.5
            value = pre * level_half
            slope = level_half + value * (1.0 - level_half) * (2.0 * TANH_IN + 6.0 * TANH_CUBE * square)
            hst[b] = value.astype(BF)
            deriv[k, b] = slope.astype(BF)

        def down(b):
            acc[...] += dot(hst[b], wd[b])

        buffers = (u0, u1)
        up(0, u0)
        for b in range(blocks):
            if b + 1 < blocks:
                up(b + 1, buffers[(b + 1) % 2])
            if b > 0:
                down(b - 1)
            activate(b, buffers[b % 2])
        down(last)
        for b in range(blocks):
            h_copy(k, b).start()

        @pl.when(k > 0)
        def _():
            act_copy(k).wait()

        for c, part in enumerate(tiles):
            unit, scale = normalized(acc[part, :])
            xh2[k, part, :] = unit.astype(BF)
            rstd[k, part, 1:2] = scale
            value = unit * g2 + b2
            yst[part, :] = value

            @pl.when(first)
            def _():
                sendbuf[k, part, :] = value.astype(BF)
                chunk_copy(k, c).start()

        act_copy(k).start()

    def backward(k, step):
        length = bucket[k]
        level = jnp.where(length == rows, 2, jnp.where(length * 2 == rows, 1, 0))

        @pl.when(jnp.logical_and(k == 0, jnp.logical_not(first)))
        def _():
            cot_copy.wait()

        df_copy(k).wait()
        for b in range(blocks):
            du_copy(k, b).wait()

        @pl.when(k > 0)
        def _():
            grad_copy(k).wait()

        @pl.when(first)
        def _():
            arrived(k)
            xst[...] = recv[k].astype(F32)

        @pl.when(jnp.logical_not(first))
        def _():
            xst[...] = inbuf[k].astype(F32)

        for part in tiles:
            grad = xst[part, :]
            unit = xh2[k, part, :].astype(F32)
            back = norm_back(grad, g2, unit, rstd[k, part, 1:2])
            rounded = back.astype(BF)
            low[part, :] = rounded
            acc[part, :] = back
            sums[2] += fold8(grad * unit)
            sums[3] += fold8(grad)
            sums[4] += fold8(rounded.astype(F32))
        df_copy(k).start()

        def up(b, u):
            u[...] = dot_t(low[...], wd[b])

        def activate(b, u):
            rounded = (u[...] * deriv[k, b].astype(F32)).astype(BF)
            hst[b] = rounded
            sums[5 + b] += fold8(rounded.astype(F32))

        def down(b):
            acc[...] += dot_t(hst[b], wu[b])

        buffers = (u0, u1)
        up(0, u0)
        for b in range(blocks):
            if b + 1 < blocks:
                up(b + 1, buffers[(b + 1) % 2])
            if b > 0:
                down(b - 1)
            activate(b, buffers[b % 2])
        down(last)
        for b in range(blocks):
            du_copy(k, b).start()

        for part in tiles:
            grad = acc[part, :]
            unit = xh1[k, part, :].astype(F32)
            back = norm_back(grad, g1, unit, rstd[k, part, 0:1])
            acc[part, :] = back
            recv[k, part, :] = back.astype(BF)
            sums[0] += fold8(grad * unit)
            sums[1] += fold8(grad)
        pq[0] = dot(stab[level, 0], recv[k]).astype(BF)
        pq[1] = dot(stab[level, 1], recv[k]).astype(BF)

        for i, part in enumerate(halves):
            value = acc[part, :] + dot(pq[0, part, :], htab[0]) + dot(pq[1, part, :], htab[1])
            rounded = value.astype(BF)
            xst[part, :] = jnp.where(first, value, rounded.astype(F32))

            @pl.when(jnp.logical_not(first))
            def _():
                sendbuf[k, part, :] = rounded
                for c in range(i * CHUNKS // 2, (i + 1) * CHUNKS // 2):
                    chunk_copy(k, c).start()

        grad_copy(k).start()

    def one(step, carry):
        forwards = jnp.where(first, step < count, lax.rem(step, 2) == 0)
        k = jnp.where(first, lax.rem(step, count), step // 2)

        @pl.when(forwards)
        def _():
            forward(k, step)

        @pl.when(jnp.logical_not(forwards))
        def _():
            backward(k, step)

        return carry

    lax.fori_loop(0, 2 * count, one, 0)

    end = count - 1

    for n in range(5 + blocks):
        small_ref[n : n + 1, :] = jnp.sum(sums[n], axis=0, keepdims=True)
    for n in range(5 + blocks, small_ref.shape[0]):
        small_ref[n : n + 1, :] = jnp.zeros((1, width), F32)
    act_copy(end).wait()
    grad_copy(end).wait()
    df_copy(end).wait()
    for b in range(blocks):
        du_copy(end, b).wait()
    for k in range(count):
        for c in range(CHUNKS):
            chunk_copy(k, c).wait_send()


def run_layers(bucket, plan, norms, up_bias, inputs, cotangent, up_weight, down_weight):
    count, rows, width = inputs.shape
    hidden = up_weight.shape[-1]
    fb = width
    blocks = hidden // fb
    htab = jnp.asarray(hidden_tables(width))
    stab = jnp.asarray(seq_tables(rows))
    any_spec = pl.BlockSpec(memory_space=pl.ANY)
    smem = pl.BlockSpec(memory_space=pltpu.SMEM)
    vmem = pl.BlockSpec(memory_space=pltpu.VMEM)
    shape = jax.ShapeDtypeStruct
    body = functools.partial(layers_kernel, count, rows, width, blocks, fb)
    flops = count * (12 * rows * width * hidden // 1 + 4 * rows * width * (2 * width + 2 * rows))
    return pl.pallas_call(
        body,
        out_shape=(
            shape((1, count, rows, width), F32),
            shape((1, count, rows, width), F32),
            shape((blocks, count, rows, fb), BF),
            shape((blocks, count, rows, fb), BF),
            shape((count, rows, width), BF),
            shape((count, rows, width), BF),
            shape((16, width), F32),
        ),
        in_specs=[smem, smem, vmem, vmem] + [any_spec] * 6,
        out_specs=(any_spec,) * 6 + (vmem,),
        scratch_shapes=[
            pltpu.VMEM((blocks, width, fb), BF),
            pltpu.VMEM((blocks, fb, width), BF),
            pltpu.VMEM((2, width, width), BF),
            pltpu.VMEM((3, 2, rows, rows), BF),
            pltpu.VMEM((count, rows, width), BF),
            pltpu.VMEM((count, rows, width), BF),
            pltpu.VMEM((count, rows, width), BF),
            pltpu.VMEM((count, blocks, rows, fb), BF),
            pltpu.VMEM((count, rows, width), BF),
            pltpu.VMEM((count, rows, width), BF),
            pltpu.VMEM((count, rows, 128), F32),
            pltpu.VMEM((blocks, rows, fb), BF),
            pltpu.VMEM((2, rows, width), BF),
            pltpu.VMEM((rows, fb), F32),
            pltpu.VMEM((rows, fb), F32),
            pltpu.VMEM((rows, width), F32),
            pltpu.VMEM((rows, width), BF),
            pltpu.VMEM((rows, width), F32),
            pltpu.VMEM((rows, width), F32),
            pltpu.VMEM((5 + blocks, 8, width), F32),
            pltpu.SemaphoreType.DMA((2 * blocks,)),
            pltpu.SemaphoreType.DMA((3,)),
            pltpu.SemaphoreType.DMA((3,)),
            pltpu.SemaphoreType.DMA((blocks,)),
            pltpu.SemaphoreType.DMA((count, CHUNKS)),
            pltpu.SemaphoreType.DMA((count, CHUNKS)),
        ],
        compiler_params=pltpu.CompilerParams(
            collective_id=0, has_side_effects=True, vmem_limit_bytes=63 * 2**20
        ),
        cost_estimate=pl.CostEstimate(flops=flops, bytes_accessed=60 * 2**20, transcendentals=0),
    )(bucket, plan, norms, up_bias, inputs, cotangent, up_weight, down_weight, htab, stab)


KINDS = 13
C1, Y1, CHY, INY, RY, Y2, CHZ, INZ, YZ, RZH, RZF, SY, SZ = range(KINDS)
RING = 4
LAG = 7


def grads_kernel(
    dp, count, rows, width, units, wide, per_block,
    a_hbm, df_hbm, h_hbm, du_hbm, small_ref,
    out_hbm, small_out,
    at, abuf, dfb, xb, prod, cur, res, c1in, y1in, chy, iny, chz, inz, yz, sm, smin,
    in_sem, x_sem, out_sem, send_sem, recv_sem, sm_send, sm_recv,
):
    me = lax.axis_index("dp")
    n = dp // 4
    core = me % 2
    side = (me // 2) % 2
    z = me // 4
    low = z < n // 2
    inner = jnp.logical_or(z == n // 2 - 1, z == n // 2)
    outer = jnp.logical_not(inner)
    has_out = jnp.logical_and(z > 0, z < n - 1)
    edge = jnp.logical_not(has_out)
    toward = jnp.where(low, 4, -4)
    inward = me + toward
    outward = me - toward
    sibling = me + 1 - 2 * core
    across = me + 2 - 4 * side
    keep = jnp.where(low, 0, 1)
    half = units // 2
    steps = dp.bit_length() - 1
    home = core * 4

    def x_start(u):
        slot = u % 3
        j = u % half
        block = j // per_block
        part = pl.ds(pl.multiple_of((j % per_block) * wide, wide), wide)

        @pl.when(u < half)
        def _():
            pltpu.make_async_copy(h_hbm.at[block, :, :, part], xb.at[slot], x_sem.at[slot]).start()

        @pl.when(u >= half)
        def _():
            pltpu.make_async_copy(du_hbm.at[block, :, :, part], xb.at[slot], x_sem.at[slot]).start()

    def x_wait(u):
        slot = u % 3
        pltpu.make_async_copy(h_hbm.at[0, :, :, pl.ds(0, wide)], xb.at[slot], x_sem.at[slot]).wait()

    df_copy = pltpu.make_async_copy(df_hbm, dfb, in_sem.at[0])
    a_copy = pltpu.make_async_copy(a_hbm, abuf, in_sem.at[1])
    df_copy.start()
    x_start(0)
    x_start(1)
    a_copy.start()

    def partner(s):
        return me + 2**s - 2 ** (s + 1) * ((me // 2**s) % 2)

    barrier = pltpu.get_barrier_semaphore()
    for s in range(steps):
        pl.semaphore_signal(barrier, inc=1, device_id={"dp": partner(s)}, device_id_type=pl.DeviceIdType.MESH)
    pl.semaphore_signal(barrier, inc=1, device_id={"dp": inward}, device_id_type=pl.DeviceIdType.MESH)

    @pl.when(has_out)
    def _():
        pl.semaphore_signal(barrier, inc=1, device_id={"dp": outward}, device_id_type=pl.DeviceIdType.MESH)
        pl.semaphore_wait(barrier, steps + 2)

    @pl.when(edge)
    def _():
        pl.semaphore_wait(barrier, steps + 1)

    def small_copy(s):
        return pltpu.make_async_remote_copy(
            src_ref=sm.at[s], dst_ref=smin.at[s], send_sem=sm_send.at[s], recv_sem=sm_recv.at[s],
            device_id={"dp": partner(s)}, device_id_type=pl.DeviceIdType.MESH,
        )

    sm[0] = small_ref[...]
    small_copy(0).start()

    def message(kind, u, src, dst, target):
        return pltpu.make_async_remote_copy(
            src_ref=src, dst_ref=dst, send_sem=send_sem.at[kind, u % RING], recv_sem=recv_sem.at[kind, u],
            device_id={"dp": target}, device_id_type=pl.DeviceIdType.MESH,
        )

    def c1(u):
        return message(C1, u, prod.at[u % RING, pl.ds(4 - home, 4)], c1in.at[u], sibling)

    def y1(u):
        return message(Y1, u, cur.at[u, 1 - side], y1in.at[u], across)

    def ch_y(u):
        return message(CHY, u, cur.at[u, side], chy.at[u], inward)

    def in_y(u):
        return message(INY, u, cur.at[u, side], iny.at[u], inward)

    def r_y(u):
        return message(RY, u, res.at[u, home + side], res.at[u, home + side], outward)

    def y2(u):
        return message(Y2, u, res.at[u, home + side], res.at[u, home + side], across)

    def ch_z(u):
        return message(CHZ, u, cur.at[u, pl.ds(2, 2)], chz.at[u], inward)

    def in_z(u):
        return message(INZ, u, cur.at[u, 3 - keep], inz.at[u], inward)

    def y_z(u):
        return message(YZ, u, cur.at[u, 2 + keep], yz.at[u], across)

    def r_zh(u):
        return message(RZH, u, res.at[u, home + 2 + keep], res.at[u, home + 2 + keep], inward)

    def r_zf(u):
        return message(RZF, u, res.at[u, pl.ds(home + 2, 2)], res.at[u, pl.ds(home + 2, 2)], outward)

    def s_y(u):
        return message(SY, u, res.at[u, pl.ds(home, 2)], res.at[u, pl.ds(home, 2)], sibling)

    def s_z(u):
        return message(SZ, u, res.at[u, pl.ds(home + 2, 2)], res.at[u, pl.ds(home + 2, 2)], sibling)

    def out_copy(u):
        return pltpu.make_async_copy(res.at[u], out_hbm.at[u], out_sem.at[u % RING])

    def send(make, u):
        @pl.when(u >= RING)
        def _():
            make(u - RING).wait_send()

        make(u).start()

    def plus(left, right):
        return (left.astype(F32) + right.astype(F32)).astype(BF)

    def compute(u):
        slot = u % RING
        x_wait(u)

        @pl.when(u + 2 < units)
        def _():
            x_start(u + 2)

        @pl.when(u >= RING)
        def _():
            c1(u - RING).wait_send()

        @pl.when(u == 0)
        def _():
            df_copy.wait()

        @pl.when(u == half)
        def _():
            a_copy.wait()
            for k in range(count):
                at[:, k * rows : (k + 1) * rows] = abuf[k].T

        block = xb.at[u % 3]

        @pl.when(u < half)
        def _():
            value = lax.dot_general(
                block[...].reshape(count * rows, wide), dfb[...].reshape(count * rows, width),
                (((0,), (0,)), ((), ())), preferred_element_type=F32,
            )
            value = jnp.concatenate([value[:, t : t + wide] for t in range(0, width, wide)], axis=0)
            prod[slot] = value.astype(BF).reshape(8, width // 8, wide)

        @pl.when(u >= half)
        def _():
            value = dot(at[...], block[...].reshape(count * rows, wide))
            prod[slot] = value.astype(BF).reshape(8, width // 8, wide)

        c1(u).start()

    def stage1(u):
        c1(u).wait_recv()
        cur[u] = plus(prod[u % RING, pl.ds(home, 4)], c1in[u])
        send(y1, u)

        @pl.when(edge)
        def _():
            send(ch_z, u)

    def stage2(u):
        y1(u).wait_recv()
        cur[u, side] = plus(cur[u, side], y1in[u])

        @pl.when(edge)
        def _():
            send(ch_y, u)

        @pl.when(has_out)
        def _():
            ch_z(u).wait_recv()
            cur[u, 2:4] = plus(cur[u, 2:4], chz[u])

        @pl.when(inner)
        def _():
            send(in_z, u)

        @pl.when(jnp.logical_and(outer, has_out))
        def _():
            send(ch_z, u)

    def stage3(u):
        @pl.when(has_out)
        def _():
            ch_y(u).wait_recv()
            cur[u, side] = plus(cur[u, side], chy[u])

        @pl.when(inner)
        def _():
            send(in_y, u)
            in_z(u).wait_recv()
            cur[u, 2 + keep] = plus(cur[u, 2 + keep], inz[u])
            send(y_z, u)

        @pl.when(jnp.logical_and(outer, has_out))
        def _():
            send(ch_y, u)

    def stage4(u):
        @pl.when(inner)
        def _():
            in_y(u).wait_recv()
            res[u, home + side] = plus(cur[u, side], iny[u])
            send(r_y, u)
            send(y2, u)
            y_z(u).wait_recv()
            res[u, home + 2 + keep] = plus(cur[u, 2 + keep], yz[u])
            send(r_zh, u)

    def stage5(u):
        @pl.when(outer)
        def _():
            r_y(u).wait_recv()

            @pl.when(has_out)
            def _():
                send(r_y, u)

            send(y2, u)

        @pl.when(inner)
        def _():
            message(
                RZH, u, res.at[u, home + 3 - keep], res.at[u, home + 3 - keep], inward
            ).wait_recv()
            send(r_zf, u)
            send(s_z, u)

    def stage6(u):
        message(Y2, u, res.at[u, home + 1 - side], res.at[u, home + 1 - side], across).wait_recv()
        send(s_y, u)

        @pl.when(outer)
        def _():
            r_zf(u).wait_recv()

            @pl.when(has_out)
            def _():
                send(r_zf, u)

            send(s_z, u)

    def stage7(u):
        away = 4 - home
        message(SY, u, res.at[u, pl.ds(away, 2)], res.at[u, pl.ds(away, 2)], sibling).wait_recv()
        message(SZ, u, res.at[u, pl.ds(away + 2, 2)], res.at[u, pl.ds(away + 2, 2)], sibling).wait_recv()

        @pl.when(u >= RING)
        def _():
            out_copy(u - RING).wait()

        out_copy(u).start()

    stages = (stage1, stage2, stage3, stage4, stage5, stage6, stage7)

    def one(i, carry):
        @pl.when(i < units)
        def _():
            compute(i)

        for lag in range(LAG, 0, -1):
            u = i - lag

            @pl.when(jnp.logical_and(u >= 0, u < units))
            def _():
                stages[lag - 1](u)

        for s in range(steps):

            @pl.when(i == s + 1)
            def _():
                small_copy(s).wait_recv()
                sm[s + 1] = sm[s] + smin[s]
                if s + 1 < steps:
                    small_copy(s + 1).start()

        return carry

    lax.fori_loop(0, units + LAG, one, 0)

    small_out[...] = sm[steps]
    for s in range(steps):
        small_copy(s).wait_send()

    def drain(u, carry):
        for make in (c1, y1, y2, s_y, s_z):
            make(u).wait_send()
        out_copy(u).wait()

        @pl.when(inner)
        def _():
            for make in (in_z, in_y, y_z, r_zh):
                make(u).wait_send()

        @pl.when(has_out)
        def _():
            for make in (r_y, r_zf):
                make(u).wait_send()

        @pl.when(outer)
        def _():
            for make in (ch_y, ch_z):
                make(u).wait_send()

        return carry

    lax.fori_loop(units - RING, units, drain, 0)


def run_grads(dp, a, df, h, du, small):
    count, rows, width = a.shape
    blocks, fb = h.shape[0], h.shape[-1]
    wide = fb // 3
    half = blocks * 3
    units = 2 * half
    steps = dp.bit_length() - 1
    piece = width // 8
    any_spec = pl.BlockSpec(memory_space=pl.ANY)
    vmem = pl.BlockSpec(memory_space=pltpu.VMEM)
    shape = jax.ShapeDtypeStruct
    body = functools.partial(grads_kernel, dp, count, rows, width, units, wide, 3)
    return pl.pallas_call(
        body,
        out_shape=(shape((units, 8, piece, wide), BF), shape(small.shape, F32)),
        in_specs=[any_spec] * 4 + [vmem],
        out_specs=(any_spec, vmem),
        scratch_shapes=[
            pltpu.VMEM((width, count * rows), BF),
            pltpu.VMEM((count, rows, width), BF),
            pltpu.VMEM((count, rows, width), BF),
            pltpu.VMEM((3, count, rows, wide), BF),
            pltpu.VMEM((RING, 8, piece, wide), BF),
            pltpu.VMEM((units, 4, piece, wide), BF),
            pltpu.VMEM((units, 8, piece, wide), BF),
            pltpu.VMEM((units, 4, piece, wide), BF),
            pltpu.VMEM((units, piece, wide), BF),
            pltpu.VMEM((units, piece, wide), BF),
            pltpu.VMEM((units, piece, wide), BF),
            pltpu.VMEM((units, 2, piece, wide), BF),
            pltpu.VMEM((units, piece, wide), BF),
            pltpu.VMEM((units, piece, wide), BF),
            pltpu.VMEM((steps + 1,) + small.shape, F32),
            pltpu.VMEM((steps,) + small.shape, F32),
            pltpu.SemaphoreType.DMA((2,)),
            pltpu.SemaphoreType.DMA((3,)),
            pltpu.SemaphoreType.DMA((RING,)),
            pltpu.SemaphoreType.DMA((KINDS, RING)),
            pltpu.SemaphoreType.DMA((KINDS, units)),
            pltpu.SemaphoreType.DMA((steps,)),
            pltpu.SemaphoreType.DMA((steps,)),
        ],
        compiler_params=pltpu.CompilerParams(
            collective_id=1, has_side_effects=True, vmem_limit_bytes=60 * 2**20
        ),
    )(a, df, h, du, small)


def per_device(
    inputs, bucket, plan, cotangent, norm1_gain, norm1_bias, up_weight, up_bias,
    down_weight, down_bias, norm2_gain, norm2_bias,
):
    count, rows, width = inputs.shape
    hidden = up_weight.shape[-1]
    norms = jnp.concatenate(
        [norm1_gain, norm1_bias, norm2_gain, norm2_bias, down_bias, jnp.zeros((3, width), F32)]
    )
    activations, input_grad, h, du, a, df, small = run_layers(
        bucket, plan, norms, up_bias.reshape(-1, 1, width), inputs, cotangent, up_weight, down_weight
    )
    total, small = run_grads(lax.axis_size("dp"), a, df, h, du, small)
    units, wide = total.shape[0], total.shape[-1]
    total = total.reshape(2, units // 2, width // wide, wide, wide)
    down_grad = total[0].transpose(0, 2, 1, 3).reshape(1, hidden, width).astype(F32)
    up_grad = total[1].transpose(1, 2, 0, 3).reshape(1, width, hidden).astype(F32)
    blocks = hidden // width
    return (
        activations, input_grad, small[0:1], small[1:2], up_grad,
        small[5 : 5 + blocks].reshape(1, hidden), down_grad, small[4:5], small[2:3], small[3:4],
    )


def solution(mesh):
    row = P("pipe", None)
    weight = P("pipe", None, None)
    tokens = P(None, "dp", None)
    result = P("pipe", None, "dp", None)
    return jax.shard_map(
        per_device,
        mesh=mesh,
        in_specs=(tokens, P(), P(), tokens, row, row, weight, row, weight, row, row, row),
        out_specs=(result, result, row, row, weight, row, weight, row, row, row),
        check_vma=False,
    )
```

```python
import functools
import math

import jax
import jax.numpy as jnp
import ml_dtypes
import numpy as np
from jax import lax
from jax.experimental import pallas as pl
from jax.experimental.pallas import tpu as pltpu
from jax.sharding import PartitionSpec as P

BF = jnp.bfloat16
F32 = jnp.float32
TANH_IN = math.sqrt(2.0 / math.pi)
TANH_CUBE = TANH_IN * 0.044715
EPS = 1e-6
CHUNKS = 4


def hidden_tables(width):
    position = np.arange(width)
    angle = 2.0 * np.pi * (np.outer(position, position) % width) / width
    pair = np.stack([np.cos(angle), np.sin(angle)]) / np.sqrt(width)
    return pair.astype(ml_dtypes.bfloat16)


def seq_tables(rows):
    position = np.arange(rows)
    found = []
    for length in (rows // 4, rows // 2, rows):
        same = position[:, None] // length == position[None, :] // length
        phase = (position[:, None] % length) * (position[None, :] % length) % length
        angle = 2.0 * np.pi * phase / length
        found.append(
            np.stack(
                [
                    np.where(same, np.cos(angle), 0.0) / np.sqrt(length),
                    np.where(same, -np.sin(angle), 0.0) / np.sqrt(length),
                ]
            )
        )
    return np.stack(found).astype(ml_dtypes.bfloat16)


def dot(left, right):
    return jnp.dot(left, right, preferred_element_type=F32)


def dot_t(left, right):
    return lax.dot_general(left, right, (((1,), (1,)), ((), ())), preferred_element_type=F32)


def fold8(values):
    return jnp.sum(values.reshape(-1, 8, values.shape[-1]), axis=0)


def layers_kernel(
    count, rows, width, blocks, fb,
    bucket, plan, norm_ref, upb_ref, in_hbm, cot_hbm, wu_hbm, wd_hbm, htab_hbm, stab_hbm,
    act_hbm, grad_hbm, h_hbm, du_hbm, a_hbm, df_hbm, small_ref,
    wu, wd, htab, stab, inbuf, recv, sendbuf, deriv, xh1, xh2, rstd,
    hst, pq, u0, u1, acc, alow, dlow, yst, xst, sums,
    w_sem, t_sem, o_sem, h_sem, send_sem, recv_sem,
):
    first = lax.axis_index("pipe") == 0
    partner = 1 - lax.axis_index("pipe")
    last = blocks - 1

    def wu_copy(b):
        return pltpu.make_async_copy(wu_hbm.at[0, :, pl.ds(b * fb, fb)], wu.at[b], w_sem.at[b])

    def wd_copy(b):
        return pltpu.make_async_copy(wd_hbm.at[0, pl.ds(b * fb, fb), :], wd.at[b], w_sem.at[blocks + b])

    in_copy = pltpu.make_async_copy(in_hbm, inbuf, t_sem.at[0])
    cot_copy = pltpu.make_async_copy(cot_hbm, inbuf, t_sem.at[0])
    htab_copy = pltpu.make_async_copy(htab_hbm, htab, t_sem.at[1])
    stab_copy = pltpu.make_async_copy(stab_hbm, stab, t_sem.at[2])

    @pl.when(first)
    def _():
        in_copy.start()

    htab_copy.start()
    stab_copy.start()
    for b in range(blocks):
        wu_copy(b).start()
        wd_copy(b).start()

    @pl.when(jnp.logical_not(first))
    def _():
        cot_copy.start()

    sums[...] = jnp.zeros_like(sums)

    barrier = pltpu.get_barrier_semaphore()
    pl.semaphore_signal(barrier, inc=1, device_id={"pipe": partner}, device_id_type=pl.DeviceIdType.MESH)
    pl.semaphore_wait(barrier, 1)

    span = rows // CHUNKS

    def chunk_copy(k, c):
        part = pl.ds(c * span, span)
        return pltpu.make_async_remote_copy(
            src_ref=sendbuf.at[k, part],
            dst_ref=recv.at[k, part],
            send_sem=send_sem.at[k, c],
            recv_sem=recv_sem.at[k, c],
            device_id={"pipe": partner},
            device_id_type=pl.DeviceIdType.MESH,
        )

    def act_copy(k):
        return pltpu.make_async_copy(yst, act_hbm.at[0, k], o_sem.at[0])

    def grad_copy(k):
        return pltpu.make_async_copy(xst, grad_hbm.at[0, k], o_sem.at[1])

    def a_copy(k):
        return pltpu.make_async_copy(alow, a_hbm.at[k], o_sem.at[2])

    def df_copy(k):
        return pltpu.make_async_copy(dlow, df_hbm.at[k], o_sem.at[3])

    def h_copy(k, b):
        return pltpu.make_async_copy(hst.at[b], h_hbm.at[b, k], h_sem.at[b])

    def du_copy(k, b):
        return pltpu.make_async_copy(hst.at[b], du_hbm.at[b, k], h_sem.at[b])

    def arrived(k, i):
        for c in range(i * CHUNKS // 2, (i + 1) * CHUNKS // 2):
            chunk_copy(k, c).wait_recv()

    def leave(k, i):
        for c in range(i * CHUNKS // 2, (i + 1) * CHUNKS // 2):
            chunk_copy(k, c).start()

    half = rows // 2
    halves = (slice(0, half), slice(half, rows))
    tiles = [[slice(r, r + span) for r in range(h.start, h.stop, span)] for h in halves]
    order = [(i, b) for i in range(2) for b in range(blocks)]
    buffers = (u0, u1)
    g1 = norm_ref[0:1, :]
    b1 = norm_ref[1:2, :]
    g2 = norm_ref[2:3, :]
    b2 = norm_ref[3:4, :]
    bd = norm_ref[4:5, :]

    def normalized(values):
        centered = values - jnp.mean(values, axis=-1, keepdims=True)
        scale = lax.rsqrt(jnp.mean(centered * centered, axis=-1, keepdims=True) + EPS)
        return centered * scale, scale

    def norm_back(grad, gain, unit, scale):
        scaled = grad * gain
        mean_one = jnp.mean(scaled, axis=-1, keepdims=True)
        mean_two = jnp.mean(scaled * unit, axis=-1, keepdims=True)
        return scale * (scaled - mean_one - unit * mean_two)

    def pipelined(up, activate, down, before, after):
        before(0)
        up(*order[0], u0)
        for n, (i, b) in enumerate(order):
            if n + 1 < len(order):
                if order[n + 1][1] == 0:
                    before(order[n + 1][0])
                up(*order[n + 1], buffers[(n + 1) % 2])
            if n > 0:
                down(*order[n - 1])
            activate(i, b, buffers[n % 2])
            if n > 0 and order[n - 1][1] == last:
                after(order[n - 1][0])
        down(*order[-1])
        after(1)

    def forward(k, step):
        source = plan[k]
        length = bucket[k]
        level = jnp.where(length == rows, 2, jnp.where(length * 2 == rows, 1, 0))

        @pl.when(step == 0)
        def _():
            htab_copy.wait()

        @pl.when(jnp.logical_and(step == 0, first))
        def _():
            in_copy.wait()

        @pl.when(first)
        def _():
            recv[k] = inbuf[source]

        for i, part in enumerate(halves):

            @pl.when(jnp.logical_not(first))
            def _():
                arrived(k, i)

            pq[0, part] = dot(recv[k, part], htab[0]).astype(BF)
            pq[1, part] = dot(recv[k, part], htab[1]).astype(BF)

        @pl.when(step == 0)
        def _():
            stab_copy.wait()

        @pl.when(step > 0)
        def _():
            for b in range(blocks):
                h_copy(k, b).wait()

        @pl.when(k > 0)
        def _():
            a_copy(k).wait()

        for part in halves:
            mixed = dot(stab[level, 0, part, :], pq[0]) + dot(stab[level, 1, part, :], pq[1])
            unit, scale = normalized(recv[k, part, :].astype(F32) + mixed)
            xh1[k, part, :] = unit.astype(BF)
            rstd[k, part, 0:1] = scale
            value = unit * g1 + b1
            alow[part, :] = value.astype(BF)
            acc[part, :] = value + bd
        a_copy(k).start()

        @pl.when(step == 0)
        def _():
            for b in range(blocks):
                wu_copy(b).wait()
                wd_copy(b).wait()

        @pl.when(k > 0)
        def _():
            act_copy(k).wait()

        def up(i, b, u):
            u[...] = dot(alow[halves[i], :], wu[b])

        def activate(i, b, u):
            pre = u[...] + upb_ref[b]
            square = pre * pre
            level_half = 0.5 * jnp.tanh(pre * (TANH_IN + TANH_CUBE * square)) + 0.5
            value = pre * level_half
            slope = level_half + value * (1.0 - level_half) * (2.0 * TANH_IN + 6.0 * TANH_CUBE * square)
            hst[b, halves[i], :] = value.astype(BF)
            deriv[k, b, halves[i], :] = slope.astype(BF)

        def down(i, b):
            acc[halves[i], :] += dot(hst[b, halves[i], :], wd[b])

        def before(i):
            pass

        def after(i):
            for part in tiles[i]:
                unit, scale = normalized(acc[part, :])
                xh2[k, part, :] = unit.astype(BF)
                rstd[k, part, 1:2] = scale
                value = unit * g2 + b2
                yst[part, :] = value
                sendbuf[k, part, :] = value.astype(BF)

            @pl.when(first)
            def _():
                leave(k, i)

        pipelined(up, activate, down, before, after)
        for b in range(blocks):
            h_copy(k, b).start()
        act_copy(k).start()

    def backward(k, step):
        length = bucket[k]
        level = jnp.where(length == rows, 2, jnp.where(length * 2 == rows, 1, 0))

        @pl.when(jnp.logical_and(k == 0, jnp.logical_not(first)))
        def _():
            cot_copy.wait()

        @pl.when(first)
        def _():
            for c in range(CHUNKS):
                chunk_copy(k, c).wait_send()

        @pl.when(k > 0)
        def _():
            df_copy(k).wait()
            grad_copy(k).wait()

        def before(i):
            @pl.when(first)
            def _():
                arrived(k, i)

            for part in tiles[i]:
                grad = jnp.where(first, recv[k, part, :], inbuf[k, part, :]).astype(F32)
                unit = xh2[k, part, :].astype(F32)
                back = norm_back(grad, g2, unit, rstd[k, part, 1:2])
                rounded = back.astype(BF)
                dlow[part, :] = rounded
                acc[part, :] = back
                sums[2] += fold8(grad * unit)
                sums[3] += fold8(grad)
                sums[4] += fold8(rounded.astype(F32))
            if i == 0:
                for b in range(blocks):
                    du_copy(k, b).wait()

        def up(i, b, u):
            u[...] = dot_t(dlow[halves[i], :], wd[b])

        def activate(i, b, u):
            rounded = (u[...] * deriv[k, b, halves[i], :].astype(F32)).astype(BF)
            hst[b, halves[i], :] = rounded
            sums[5 + b] += fold8(rounded.astype(F32))

        def down(i, b):
            acc[halves[i], :] += dot_t(hst[b, halves[i], :], wu[b])

        def after(i):
            for part in tiles[i]:
                grad = acc[part, :]
                unit = xh1[k, part, :].astype(F32)
                back = norm_back(grad, g1, unit, rstd[k, part, 0:1])
                acc[part, :] = back
                recv[k, part, :] = back.astype(BF)
                sums[0] += fold8(grad * unit)
                sums[1] += fold8(grad)

        pipelined(up, activate, down, before, after)
        df_copy(k).start()
        for b in range(blocks):
            du_copy(k, b).start()

        pq[0] = dot(stab[level, 0], recv[k]).astype(BF)
        pq[1] = dot(stab[level, 1], recv[k]).astype(BF)

        for i, part in enumerate(halves):
            value = acc[part, :] + dot(pq[0, part, :], htab[0]) + dot(pq[1, part, :], htab[1])
            rounded = value.astype(BF)
            xst[part, :] = jnp.where(first, value, rounded.astype(F32))
            sendbuf[k, part, :] = rounded

            @pl.when(jnp.logical_not(first))
            def _():
                leave(k, i)

        grad_copy(k).start()

    def one(step, carry):
        forwards = jnp.where(first, step < count, lax.rem(step, 2) == 0)
        k = jnp.where(first, lax.rem(step, count), step // 2)

        @pl.when(forwards)
        def _():
            forward(k, step)

        @pl.when(jnp.logical_not(forwards))
        def _():
            backward(k, step)

        return carry

    lax.fori_loop(0, 2 * count, one, 0)

    end = count - 1

    for n in range(5 + blocks):
        small_ref[n : n + 1, :] = jnp.sum(sums[n], axis=0, keepdims=True)
    for n in range(5 + blocks, small_ref.shape[0]):
        small_ref[n : n + 1, :] = jnp.zeros((1, width), F32)
    act_copy(end).wait()
    grad_copy(end).wait()
    a_copy(end).wait()
    df_copy(end).wait()
    for b in range(blocks):
        du_copy(end, b).wait()

    @pl.when(jnp.logical_not(first))
    def _():
        for k in range(count):
            for c in range(CHUNKS):
                chunk_copy(k, c).wait_send()


def run_layers(bucket, plan, norms, up_bias, inputs, cotangent, up_weight, down_weight):
    count, rows, width = inputs.shape
    hidden = up_weight.shape[-1]
    fb = width
    blocks = hidden // fb
    htab = jnp.asarray(hidden_tables(width))
    stab = jnp.asarray(seq_tables(rows))
    any_spec = pl.BlockSpec(memory_space=pl.ANY)
    smem = pl.BlockSpec(memory_space=pltpu.SMEM)
    vmem = pl.BlockSpec(memory_space=pltpu.VMEM)
    shape = jax.ShapeDtypeStruct
    body = functools.partial(layers_kernel, count, rows, width, blocks, fb)
    flops = count * (12 * rows * width * hidden // 1 + 4 * rows * width * (2 * width + 2 * rows))
    return pl.pallas_call(
        body,
        out_shape=(
            shape((1, count, rows, width), F32),
            shape((1, count, rows, width), F32),
            shape((blocks, count, rows, fb), BF),
            shape((blocks, count, rows, fb), BF),
            shape((count, rows, width), BF),
            shape((count, rows, width), BF),
            shape((16, width), F32),
        ),
        in_specs=[smem, smem, vmem, vmem] + [any_spec] * 6,
        out_specs=(any_spec,) * 6 + (vmem,),
        scratch_shapes=[
            pltpu.VMEM((blocks, width, fb), BF),
            pltpu.VMEM((blocks, fb, width), BF),
            pltpu.VMEM((2, width, width), BF),
            pltpu.VMEM((3, 2, rows, rows), BF),
            pltpu.VMEM((count, rows, width), BF),
            pltpu.VMEM((count, rows, width), BF),
            pltpu.VMEM((count, rows, width), BF),
            pltpu.VMEM((count, blocks, rows, fb), BF),
            pltpu.VMEM((count, rows, width), BF),
            pltpu.VMEM((count, rows, width), BF),
            pltpu.VMEM((count, rows, 128), F32),
            pltpu.VMEM((blocks, rows, fb), BF),
            pltpu.VMEM((2, rows, width), BF),
            pltpu.VMEM((rows // 2, fb), F32),
            pltpu.VMEM((rows // 2, fb), F32),
            pltpu.VMEM((rows, width), F32),
            pltpu.VMEM((rows, width), BF),
            pltpu.VMEM((rows, width), BF),
            pltpu.VMEM((rows, width), F32),
            pltpu.VMEM((rows, width), F32),
            pltpu.VMEM((5 + blocks, 8, width), F32),
            pltpu.SemaphoreType.DMA((2 * blocks,)),
            pltpu.SemaphoreType.DMA((3,)),
            pltpu.SemaphoreType.DMA((4,)),
            pltpu.SemaphoreType.DMA((blocks,)),
            pltpu.SemaphoreType.DMA((count, CHUNKS)),
            pltpu.SemaphoreType.DMA((count, CHUNKS)),
        ],
        compiler_params=pltpu.CompilerParams(
            collective_id=0, has_side_effects=True, vmem_limit_bytes=63 * 2**20
        ),
        cost_estimate=pl.CostEstimate(flops=flops, bytes_accessed=60 * 2**20, transcendentals=0),
    )(bucket, plan, norms, up_bias, inputs, cotangent, up_weight, down_weight, htab, stab)


KINDS = 13
C1, Y1, CHY, INY, RY, Y2, CHZ, INZ, YZ, RZH, RZF, SY, SZ = range(KINDS)
RING = 4
LAGS = (1, 3, 5, 7, 9, 11, 12)


def grads_kernel(
    dp, count, rows, width, units, wide, per_block,
    a_hbm, df_hbm, h_hbm, du_hbm, small_ref,
    down_hbm, up_hbm, small_out,
    at, abuf, dfb, xb, prod, cur, res, stage, c1in, y1in, chy, iny, chz, inz, yz, sm, smin,
    in_sem, x_sem, out_sem, send_sem, recv_sem, sm_send, sm_recv,
):
    me = lax.axis_index("dp")
    n = dp // 4
    core = me % 2
    side = (me // 2) % 2
    z = me // 4
    low = z < n // 2
    inner = jnp.logical_or(z == n // 2 - 1, z == n // 2)
    outer = jnp.logical_not(inner)
    has_out = jnp.logical_and(z > 0, z < n - 1)
    edge = jnp.logical_not(has_out)
    toward = jnp.where(low, 4, -4)
    inward = me + toward
    outward = me - toward
    sibling = me + 1 - 2 * core
    across = me + 2 - 4 * side
    keep = jnp.where(low, 0, 1)
    half = units // 2
    steps = dp.bit_length() - 1
    home = core * 4

    def x_start(u):
        slot = u % 3
        j = u % half
        block = j // per_block
        part = pl.ds(pl.multiple_of((j % per_block) * wide, wide), wide)

        @pl.when(u < half)
        def _():
            pltpu.make_async_copy(h_hbm.at[block, :, :, part], xb.at[slot], x_sem.at[slot]).start()

        @pl.when(u >= half)
        def _():
            pltpu.make_async_copy(du_hbm.at[block, :, :, part], xb.at[slot], x_sem.at[slot]).start()

    def x_wait(u):
        slot = u % 3
        pltpu.make_async_copy(h_hbm.at[0, :, :, pl.ds(0, wide)], xb.at[slot], x_sem.at[slot]).wait()

    df_copy = pltpu.make_async_copy(df_hbm, dfb, in_sem.at[0])
    a_copy = pltpu.make_async_copy(a_hbm, abuf, in_sem.at[1])
    df_copy.start()
    x_start(0)
    x_start(1)
    a_copy.start()

    def partner(s):
        return me + 2**s - 2 ** (s + 1) * ((me // 2**s) % 2)

    barrier = pltpu.get_barrier_semaphore()
    for s in range(steps):
        pl.semaphore_signal(barrier, inc=1, device_id={"dp": partner(s)}, device_id_type=pl.DeviceIdType.MESH)
    pl.semaphore_signal(barrier, inc=1, device_id={"dp": inward}, device_id_type=pl.DeviceIdType.MESH)

    @pl.when(has_out)
    def _():
        pl.semaphore_signal(barrier, inc=1, device_id={"dp": outward}, device_id_type=pl.DeviceIdType.MESH)
        pl.semaphore_wait(barrier, steps + 2)

    @pl.when(edge)
    def _():
        pl.semaphore_wait(barrier, steps + 1)

    def small_copy(s):
        return pltpu.make_async_remote_copy(
            src_ref=sm.at[s], dst_ref=smin.at[s], send_sem=sm_send.at[s], recv_sem=sm_recv.at[s],
            device_id={"dp": partner(s)}, device_id_type=pl.DeviceIdType.MESH,
        )

    sm[0] = small_ref[...]
    small_copy(0).start()

    def message(kind, u, src, dst, target):
        return pltpu.make_async_remote_copy(
            src_ref=src, dst_ref=dst, send_sem=send_sem.at[kind, u % RING], recv_sem=recv_sem.at[kind, u],
            device_id={"dp": target}, device_id_type=pl.DeviceIdType.MESH,
        )

    def c1(u):
        return message(C1, u, prod.at[u % RING, pl.ds(4 - home, 4)], c1in.at[u], sibling)

    def y1(u):
        return message(Y1, u, cur.at[u, 1 - side], y1in.at[u], across)

    def ch_y(u):
        return message(CHY, u, cur.at[u, side], chy.at[u], inward)

    def in_y(u):
        return message(INY, u, cur.at[u, side], iny.at[u], inward)

    def r_y(u):
        return message(RY, u, res.at[u, home + side], res.at[u, home + side], outward)

    def y2(u):
        return message(Y2, u, res.at[u, home + side], res.at[u, home + side], across)

    def ch_z(u):
        return message(CHZ, u, cur.at[u, pl.ds(2, 2)], chz.at[u], inward)

    def in_z(u):
        return message(INZ, u, cur.at[u, 3 - keep], inz.at[u], inward)

    def y_z(u):
        return message(YZ, u, cur.at[u, 2 + keep], yz.at[u], across)

    def r_zh(u):
        return message(RZH, u, res.at[u, home + 2 + keep], res.at[u, home + 2 + keep], inward)

    def r_zf(u):
        return message(RZF, u, res.at[u, pl.ds(home + 2, 2)], res.at[u, pl.ds(home + 2, 2)], outward)

    def s_y(u):
        return message(SY, u, res.at[u, pl.ds(home, 2)], res.at[u, pl.ds(home, 2)], sibling)

    def s_z(u):
        return message(SZ, u, res.at[u, pl.ds(home + 2, 2)], res.at[u, pl.ds(home + 2, 2)], sibling)

    def down_copy(u, t):
        part = pl.ds(pl.multiple_of(u * wide, wide), wide)
        return pltpu.make_async_copy(
            stage.at[u % 2, pl.ds(t * wide, wide)], down_hbm.at[0, part, pl.ds(t * wide, wide)],
            out_sem.at[u % 2, t],
        )

    def up_copy(u, t, slot):
        part = pl.ds(pl.multiple_of((u - half) * wide, wide), wide)
        return pltpu.make_async_copy(
            stage.at[slot, pl.ds(t * wide, wide)], up_hbm.at[0, pl.ds(t * wide, wide), part],
            out_sem.at[slot, t],
        )

    def send(make, u):
        @pl.when(u >= RING)
        def _():
            make(u - RING).wait_send()

        make(u).start()

    def plus(left, right):
        return (left.astype(F32) + right.astype(F32)).astype(BF)

    def compute(u):
        slot = u % RING
        x_wait(u)

        @pl.when(u + 2 < units)
        def _():
            x_start(u + 2)

        @pl.when(u >= RING)
        def _():
            c1(u - RING).wait_send()

        @pl.when(u == 0)
        def _():
            df_copy.wait()

        @pl.when(u == half)
        def _():
            a_copy.wait()
            for k in range(count):
                at[:, k * rows : (k + 1) * rows] = abuf[k].T

        block = xb.at[u % 3]

        @pl.when(u < half)
        def _():
            value = lax.dot_general(
                block[...].reshape(count * rows, wide), dfb[...].reshape(count * rows, width),
                (((0,), (0,)), ((), ())), preferred_element_type=F32,
            )
            value = jnp.concatenate([value[:, t : t + wide] for t in range(0, width, wide)], axis=0)
            prod[slot] = value.astype(BF).reshape(8, width // 8, wide)

        @pl.when(u >= half)
        def _():
            value = dot(at[...], block[...].reshape(count * rows, wide))
            prod[slot] = value.astype(BF).reshape(8, width // 8, wide)

        c1(u).start()

    def stage1(u):
        c1(u).wait_recv()
        cur[u] = plus(prod[u % RING, pl.ds(home, 4)], c1in[u])
        send(y1, u)

        @pl.when(edge)
        def _():
            send(ch_z, u)

    def stage2(u):
        y1(u).wait_recv()
        cur[u, side] = plus(cur[u, side], y1in[u])

        @pl.when(edge)
        def _():
            send(ch_y, u)

        @pl.when(has_out)
        def _():
            ch_z(u).wait_recv()
            cur[u, 2:4] = plus(cur[u, 2:4], chz[u])

        @pl.when(inner)
        def _():
            send(in_z, u)

        @pl.when(jnp.logical_and(outer, has_out))
        def _():
            send(ch_z, u)

    def stage3(u):
        @pl.when(has_out)
        def _():
            ch_y(u).wait_recv()
            cur[u, side] = plus(cur[u, side], chy[u])

        @pl.when(inner)
        def _():
            send(in_y, u)
            in_z(u).wait_recv()
            cur[u, 2 + keep] = plus(cur[u, 2 + keep], inz[u])
            send(y_z, u)

        @pl.when(jnp.logical_and(outer, has_out))
        def _():
            send(ch_y, u)

    def stage4(u):
        @pl.when(inner)
        def _():
            in_y(u).wait_recv()
            res[u, home + side] = plus(cur[u, side], iny[u])
            send(r_y, u)
            send(y2, u)
            y_z(u).wait_recv()
            res[u, home + 2 + keep] = plus(cur[u, 2 + keep], yz[u])
            send(r_zh, u)

    def stage5(u):
        @pl.when(outer)
        def _():
            r_y(u).wait_recv()

            @pl.when(has_out)
            def _():
                send(r_y, u)

            send(y2, u)

        @pl.when(inner)
        def _():
            message(
                RZH, u, res.at[u, home + 3 - keep], res.at[u, home + 3 - keep], inward
            ).wait_recv()
            send(r_zf, u)
            send(s_z, u)

    def stage6(u):
        message(Y2, u, res.at[u, home + 1 - side], res.at[u, home + 1 - side], across).wait_recv()
        send(s_y, u)

        @pl.when(outer)
        def _():
            r_zf(u).wait_recv()

            @pl.when(has_out)
            def _():
                send(r_zf, u)

            send(s_z, u)

    def stage7(u):
        away = 4 - home
        message(SY, u, res.at[u, pl.ds(away, 2)], res.at[u, pl.ds(away, 2)], sibling).wait_recv()
        message(SZ, u, res.at[u, pl.ds(away + 2, 2)], res.at[u, pl.ds(away + 2, 2)], sibling).wait_recv()

        @pl.when(u >= 2)
        def _():
            for t in range(width // wide):
                up_copy(half, t, u % 2).wait()

        stage[u % 2] = res[u].reshape(width, wide).astype(F32)

        @pl.when(u < half)
        def _():
            for t in range(width // wide):
                down_copy(u, t).start()

        @pl.when(u >= half)
        def _():
            for t in range(width // wide):
                up_copy(u, t, u % 2).start()

    stages = (stage1, stage2, stage3, stage4, stage5, stage6, stage7)

    def one(i, carry):
        @pl.when(i < units)
        def _():
            compute(i)

        for work, lag in reversed(list(zip(stages, LAGS))):
            u = i - lag

            @pl.when(jnp.logical_and(u >= 0, u < units))
            def _():
                work(u)

        for s in range(steps):

            @pl.when(i == s + 1)
            def _():
                small_copy(s).wait_recv()
                sm[s + 1] = sm[s] + smin[s]
                if s + 1 < steps:
                    small_copy(s + 1).start()

        return carry

    lax.fori_loop(0, units + LAGS[-1], one, 0)

    small_out[...] = sm[steps]
    for s in range(steps):
        small_copy(s).wait_send()

    def drain(u, carry):
        for make in (c1, y1, y2, s_y, s_z):
            make(u).wait_send()

        @pl.when(inner)
        def _():
            for make in (in_z, in_y, y_z, r_zh):
                make(u).wait_send()

        @pl.when(has_out)
        def _():
            for make in (r_y, r_zf):
                make(u).wait_send()

        @pl.when(outer)
        def _():
            for make in (ch_y, ch_z):
                make(u).wait_send()

        return carry

    lax.fori_loop(units - RING, units, drain, 0)
    for slot in range(2):
        for t in range(width // wide):
            up_copy(half, t, slot).wait()


def run_grads(dp, a, df, h, du, small):
    count, rows, width = a.shape
    blocks, fb = h.shape[0], h.shape[-1]
    wide = fb // 3
    half = blocks * 3
    units = 2 * half
    steps = dp.bit_length() - 1
    piece = width // 8
    hidden = blocks * fb
    any_spec = pl.BlockSpec(memory_space=pl.ANY)
    vmem = pl.BlockSpec(memory_space=pltpu.VMEM)
    shape = jax.ShapeDtypeStruct
    body = functools.partial(grads_kernel, dp, count, rows, width, units, wide, 3)
    return pl.pallas_call(
        body,
        out_shape=(shape((1, hidden, width), F32), shape((1, width, hidden), F32), shape(small.shape, F32)),
        in_specs=[any_spec] * 4 + [vmem],
        out_specs=(any_spec, any_spec, vmem),
        scratch_shapes=[
            pltpu.VMEM((width, count * rows), BF),
            pltpu.VMEM((count, rows, width), BF),
            pltpu.VMEM((count, rows, width), BF),
            pltpu.VMEM((3, count, rows, wide), BF),
            pltpu.VMEM((RING, 8, piece, wide), BF),
            pltpu.VMEM((units, 4, piece, wide), BF),
            pltpu.VMEM((units, 8, piece, wide), BF),
            pltpu.VMEM((2, width, wide), F32),
            pltpu.VMEM((units, 4, piece, wide), BF),
            pltpu.VMEM((units, piece, wide), BF),
            pltpu.VMEM((units, piece, wide), BF),
            pltpu.VMEM((units, piece, wide), BF),
            pltpu.VMEM((units, 2, piece, wide), BF),
            pltpu.VMEM((units, piece, wide), BF),
            pltpu.VMEM((units, piece, wide), BF),
            pltpu.VMEM((steps + 1,) + small.shape, F32),
            pltpu.VMEM((steps,) + small.shape, F32),
            pltpu.SemaphoreType.DMA((2,)),
            pltpu.SemaphoreType.DMA((3,)),
            pltpu.SemaphoreType.DMA((2, 3)),
            pltpu.SemaphoreType.DMA((KINDS, RING)),
            pltpu.SemaphoreType.DMA((KINDS, units)),
            pltpu.SemaphoreType.DMA((steps,)),
            pltpu.SemaphoreType.DMA((steps,)),
        ],
        compiler_params=pltpu.CompilerParams(
            collective_id=1, has_side_effects=True, vmem_limit_bytes=60 * 2**20
        ),
    )(a, df, h, du, small)


def per_device(
    inputs, bucket, plan, cotangent, norm1_gain, norm1_bias, up_weight, up_bias,
    down_weight, down_bias, norm2_gain, norm2_bias,
):
    count, rows, width = inputs.shape
    hidden = up_weight.shape[-1]
    norms = jnp.concatenate(
        [norm1_gain, norm1_bias, norm2_gain, norm2_bias, down_bias, jnp.zeros((3, width), F32)]
    )
    activations, input_grad, h, du, a, df, small = run_layers(
        bucket, plan, norms, up_bias.reshape(-1, 1, width), inputs, cotangent, up_weight, down_weight
    )
    down_grad, up_grad, small = run_grads(lax.axis_size("dp"), a, df, h, du, small)
    blocks = hidden // width
    return (
        activations, input_grad, small[0:1], small[1:2], up_grad,
        small[5 : 5 + blocks].reshape(1, hidden), down_grad, small[4:5], small[2:3], small[3:4],
    )


def solution(mesh):
    row = P("pipe", None)
    weight = P("pipe", None, None)
    tokens = P(None, "dp", None)
    result = P("pipe", None, "dp", None)
    return jax.shard_map(
        per_device,
        mesh=mesh,
        in_specs=(tokens, P(), P(), tokens, row, row, weight, row, weight, row, row, row),
        out_specs=(result, result, row, row, weight, row, weight, row, row, row),
        check_vma=False,
    )
```

```python
import functools
import math

import jax
import jax.numpy as jnp
import ml_dtypes
import numpy as np
from jax import lax
from jax.experimental import pallas as pl
from jax.experimental.pallas import tpu as pltpu
from jax.sharding import PartitionSpec as P

BF = jnp.bfloat16
F32 = jnp.float32
TANH_IN = math.sqrt(2.0 / math.pi)
TANH_CUBE = TANH_IN * 0.044715
EPS = 1e-6
CHUNKS = 4


def hidden_tables(width):
    position = np.arange(width)
    angle = 2.0 * np.pi * (np.outer(position, position) % width) / width
    pair = np.stack([np.cos(angle), np.sin(angle)]) / np.sqrt(width)
    return pair.astype(ml_dtypes.bfloat16)


def seq_tables(rows):
    position = np.arange(rows)
    found = []
    for length in (rows // 4, rows // 2, rows):
        same = position[:, None] // length == position[None, :] // length
        phase = (position[:, None] % length) * (position[None, :] % length) % length
        angle = 2.0 * np.pi * phase / length
        found.append(
            np.stack(
                [
                    np.where(same, np.cos(angle), 0.0) / np.sqrt(length),
                    np.where(same, -np.sin(angle), 0.0) / np.sqrt(length),
                ]
            )
        )
    return np.stack(found).astype(ml_dtypes.bfloat16)


def dot(left, right):
    return jnp.dot(left, right, preferred_element_type=F32)


def dot_t(left, right):
    return lax.dot_general(left, right, (((1,), (1,)), ((), ())), preferred_element_type=F32)


def fold8(values):
    return jnp.sum(values.reshape(-1, 8, values.shape[-1]), axis=0)


def layers_kernel(
    count, rows, width, blocks, fb,
    bucket, plan, g1_ref, b1_ref, g2_ref, b2_ref, bd_ref, upb_ref, in_hbm, cot_hbm, wu_hbm, wd_hbm, htab_hbm, stab_hbm,
    act_hbm, grad_hbm, h_hbm, du_hbm, a_hbm, df_hbm, small_ref,
    wu, wd, htab, stab, inbuf, recv, sendbuf, deriv, xh1, xh2, rstd,
    hst, pq, u0, u1, acc, alow, dlow, yst, xst, sums,
    w_sem, t_sem, o_sem, h_sem, send_sem, recv_sem,
):
    first = lax.axis_index("pipe") == 0
    partner = 1 - lax.axis_index("pipe")
    last = blocks - 1

    def wu_copy(b):
        return pltpu.make_async_copy(wu_hbm.at[0, :, pl.ds(b * fb, fb)], wu.at[b], w_sem.at[b])

    def wd_copy(b):
        return pltpu.make_async_copy(wd_hbm.at[0, pl.ds(b * fb, fb), :], wd.at[b], w_sem.at[blocks + b])

    in_copy = pltpu.make_async_copy(in_hbm, inbuf, t_sem.at[0])
    cot_copy = pltpu.make_async_copy(cot_hbm, inbuf, t_sem.at[0])
    htab_copy = pltpu.make_async_copy(htab_hbm, htab, t_sem.at[1])
    stab_copy = pltpu.make_async_copy(stab_hbm, stab, t_sem.at[2])

    def start_weights():
        for b in range(blocks):
            wu_copy(b).start()
            wd_copy(b).start()

    @pl.when(first)
    def _():
        in_copy.start()

    htab_copy.start()
    stab_copy.start()

    @pl.when(jnp.logical_not(first))
    def _():
        start_weights()
        cot_copy.start()

    sums[...] = jnp.zeros_like(sums)

    barrier = pltpu.get_barrier_semaphore()
    pl.semaphore_signal(barrier, inc=1, device_id={"pipe": partner}, device_id_type=pl.DeviceIdType.MESH)
    pl.semaphore_wait(barrier, 1)

    span = rows // CHUNKS

    def chunk_copy(k, c):
        part = pl.ds(c * span, span)
        return pltpu.make_async_remote_copy(
            src_ref=sendbuf.at[k, part],
            dst_ref=recv.at[k, part],
            send_sem=send_sem.at[k, c],
            recv_sem=recv_sem.at[k, c],
            device_id={"pipe": partner},
            device_id_type=pl.DeviceIdType.MESH,
        )

    def act_copy(k):
        return pltpu.make_async_copy(yst, act_hbm.at[0, k], o_sem.at[0])

    def grad_copy(k):
        return pltpu.make_async_copy(xst, grad_hbm.at[0, k], o_sem.at[1])

    def a_copy(k):
        return pltpu.make_async_copy(alow, a_hbm.at[k], o_sem.at[2])

    def df_copy(k):
        return pltpu.make_async_copy(dlow, df_hbm.at[k], o_sem.at[3])

    def h_copy(k, b):
        return pltpu.make_async_copy(hst.at[b], h_hbm.at[b, k], h_sem.at[b])

    def du_copy(k, b):
        return pltpu.make_async_copy(hst.at[b], du_hbm.at[b, k], h_sem.at[b])

    def arrived(k, i):
        for c in range(i * CHUNKS // 2, (i + 1) * CHUNKS // 2):
            chunk_copy(k, c).wait_recv()

    def leave(k, i):
        for c in range(i * CHUNKS // 2, (i + 1) * CHUNKS // 2):
            chunk_copy(k, c).start()

    half = rows // 2
    halves = (slice(0, half), slice(half, rows))
    tiles = [[slice(r, r + span) for r in range(h.start, h.stop, span)] for h in halves]
    order = [(i, b) for i in range(2) for b in range(blocks)]
    buffers = (u0, u1)
    g1, b1, g2, b2, bd = (ref[...] for ref in (g1_ref, b1_ref, g2_ref, b2_ref, bd_ref))

    def normalized(values):
        centered = values - jnp.mean(values, axis=-1, keepdims=True)
        scale = lax.rsqrt(jnp.mean(centered * centered, axis=-1, keepdims=True) + EPS)
        return centered * scale, scale

    def norm_back(grad, gain, unit, scale):
        scaled = grad * gain
        mean_one = jnp.mean(scaled, axis=-1, keepdims=True)
        mean_two = jnp.mean(scaled * unit, axis=-1, keepdims=True)
        return scale * (scaled - mean_one - unit * mean_two)

    def pipelined(up, activate, down, before, after):
        before(0)
        up(*order[0], u0)
        for n, (i, b) in enumerate(order):
            if n + 1 < len(order):
                if order[n + 1][1] == 0:
                    before(order[n + 1][0])
                up(*order[n + 1], buffers[(n + 1) % 2])
            if n > 0:
                down(*order[n - 1])
            activate(i, b, buffers[n % 2])
            if n > 0 and order[n - 1][1] == last:
                after(order[n - 1][0])
        down(*order[-1])
        after(1)

    def forward(k, step):
        source = plan[k]
        length = bucket[k]
        level = jnp.where(length == rows, 2, jnp.where(length * 2 == rows, 1, 0))

        @pl.when(step == 0)
        def _():
            htab_copy.wait()

        @pl.when(jnp.logical_and(step == 0, first))
        def _():
            in_copy.wait()
            start_weights()

        @pl.when(first)
        def _():
            recv[k] = inbuf[source]

        for i, part in enumerate(halves):

            @pl.when(jnp.logical_not(first))
            def _():
                arrived(k, i)

            pq[0, part] = dot(recv[k, part], htab[0]).astype(BF)
            pq[1, part] = dot(recv[k, part], htab[1]).astype(BF)

        @pl.when(step == 0)
        def _():
            stab_copy.wait()

        @pl.when(step > 0)
        def _():
            for b in range(blocks):
                h_copy(k, b).wait()

        @pl.when(k > 0)
        def _():
            a_copy(k).wait()

        for part in halves:
            mixed = dot(stab[level, 0, part, :], pq[0]) + dot(stab[level, 1, part, :], pq[1])
            unit, scale = normalized(recv[k, part, :].astype(F32) + mixed)
            xh1[k, part, :] = unit.astype(BF)
            rstd[k, part, 0:1] = scale
            value = unit * g1 + b1
            alow[part, :] = value.astype(BF)
            acc[part, :] = value + bd
        a_copy(k).start()

        @pl.when(step == 0)
        def _():
            for b in range(blocks):
                wu_copy(b).wait()
                wd_copy(b).wait()

        @pl.when(k > 0)
        def _():
            act_copy(k).wait()

        def up(i, b, u):
            u[...] = dot(alow[halves[i], :], wu[b])

        def activate(i, b, u):
            pre = u[...] + upb_ref[b]
            square = pre * pre
            level_half = 0.5 * jnp.tanh(pre * (TANH_IN + TANH_CUBE * square)) + 0.5
            value = pre * level_half
            slope = level_half + value * (1.0 - level_half) * (2.0 * TANH_IN + 6.0 * TANH_CUBE * square)
            hst[b, halves[i], :] = value.astype(BF)
            deriv[k, b, halves[i], :] = slope.astype(BF)

        def down(i, b):
            acc[halves[i], :] += dot(hst[b, halves[i], :], wd[b])

        def before(i):
            pass

        def after(i):
            for part in tiles[i]:
                unit, scale = normalized(acc[part, :])
                xh2[k, part, :] = unit.astype(BF)
                rstd[k, part, 1:2] = scale
                value = unit * g2 + b2
                rounded = value.astype(BF)
                yst[part, :] = rounded
                sendbuf[k, part, :] = rounded

            @pl.when(first)
            def _():
                leave(k, i)

        pipelined(up, activate, down, before, after)
        for b in range(blocks):
            h_copy(k, b).start()
        act_copy(k).start()

    def backward(k, step):
        length = bucket[k]
        level = jnp.where(length == rows, 2, jnp.where(length * 2 == rows, 1, 0))

        @pl.when(jnp.logical_and(k == 0, jnp.logical_not(first)))
        def _():
            cot_copy.wait()

        @pl.when(first)
        def _():
            for c in range(CHUNKS):
                chunk_copy(k, c).wait_send()

        @pl.when(k > 0)
        def _():
            df_copy(k).wait()
            grad_copy(k).wait()

        def before(i):
            @pl.when(first)
            def _():
                arrived(k, i)

            for part in tiles[i]:
                grad = jnp.where(first, recv[k, part, :], inbuf[k, part, :]).astype(F32)
                unit = xh2[k, part, :].astype(F32)
                back = norm_back(grad, g2, unit, rstd[k, part, 1:2])
                rounded = back.astype(BF)
                dlow[part, :] = rounded
                acc[part, :] = back
                sums[2] += fold8(grad * unit)
                sums[3] += fold8(grad)
                sums[4] += fold8(rounded.astype(F32))
            if i == 0:
                for b in range(blocks):
                    du_copy(k, b).wait()

        def up(i, b, u):
            u[...] = dot_t(dlow[halves[i], :], wd[b])

        def activate(i, b, u):
            rounded = (u[...] * deriv[k, b, halves[i], :].astype(F32)).astype(BF)
            hst[b, halves[i], :] = rounded
            sums[5 + b] += fold8(rounded.astype(F32))

        def down(i, b):
            acc[halves[i], :] += dot_t(hst[b, halves[i], :], wu[b])

        def after(i):
            for part in tiles[i]:
                grad = acc[part, :]
                unit = xh1[k, part, :].astype(F32)
                back = norm_back(grad, g1, unit, rstd[k, part, 0:1])
                acc[part, :] = back
                recv[k, part, :] = back.astype(BF)
                sums[0] += fold8(grad * unit)
                sums[1] += fold8(grad)

        pipelined(up, activate, down, before, after)
        df_copy(k).start()
        for b in range(blocks):
            du_copy(k, b).start()

        pq[0] = dot(stab[level, 0], recv[k]).astype(BF)
        pq[1] = dot(stab[level, 1], recv[k]).astype(BF)

        for i, part in enumerate(halves):
            value = acc[part, :] + dot(pq[0, part, :], htab[0]) + dot(pq[1, part, :], htab[1])
            rounded = value.astype(BF)
            xst[part, :] = rounded
            sendbuf[k, part, :] = rounded

            @pl.when(jnp.logical_not(first))
            def _():
                leave(k, i)

        grad_copy(k).start()

    def one(step, carry):
        forwards = jnp.where(first, step < count, lax.rem(step, 2) == 0)
        k = jnp.where(first, lax.rem(step, count), step // 2)

        @pl.when(forwards)
        def _():
            forward(k, step)

        @pl.when(jnp.logical_not(forwards))
        def _():
            backward(k, step)

        return carry

    lax.fori_loop(0, 2 * count, one, 0)

    end = count - 1

    for n in range(5 + blocks):
        small_ref[n : n + 1, :] = jnp.sum(sums[n], axis=0, keepdims=True)
    for n in range(5 + blocks, small_ref.shape[0]):
        small_ref[n : n + 1, :] = jnp.zeros((1, width), F32)
    act_copy(end).wait()
    grad_copy(end).wait()
    a_copy(end).wait()
    df_copy(end).wait()
    for b in range(blocks):
        du_copy(end, b).wait()

    @pl.when(jnp.logical_not(first))
    def _():
        for k in range(count):
            for c in range(CHUNKS):
                chunk_copy(k, c).wait_send()


def run_layers(bucket, plan, norms, up_bias, inputs, cotangent, up_weight, down_weight):
    count, rows, width = inputs.shape
    hidden = up_weight.shape[-1]
    fb = width
    blocks = hidden // fb
    htab = jnp.asarray(hidden_tables(width))
    stab = jnp.asarray(seq_tables(rows))
    any_spec = pl.BlockSpec(memory_space=pl.ANY)
    smem = pl.BlockSpec(memory_space=pltpu.SMEM)
    vmem = pl.BlockSpec(memory_space=pltpu.VMEM)
    shape = jax.ShapeDtypeStruct
    body = functools.partial(layers_kernel, count, rows, width, blocks, fb)
    flops = count * (12 * rows * width * hidden // 1 + 4 * rows * width * (2 * width + 2 * rows))
    return pl.pallas_call(
        body,
        out_shape=(
            shape((1, count, rows, width), BF),
            shape((1, count, rows, width), BF),
            shape((blocks, count, rows, fb), BF),
            shape((blocks, count, rows, fb), BF),
            shape((count, rows, width), BF),
            shape((count, rows, width), BF),
            shape((16, width), F32),
        ),
        in_specs=[smem, smem] + [vmem] * 6 + [any_spec] * 6,
        out_specs=(any_spec,) * 6 + (vmem,),
        scratch_shapes=[
            pltpu.VMEM((blocks, width, fb), BF),
            pltpu.VMEM((blocks, fb, width), BF),
            pltpu.VMEM((2, width, width), BF),
            pltpu.VMEM((3, 2, rows, rows), BF),
            pltpu.VMEM((count, rows, width), BF),
            pltpu.VMEM((count, rows, width), BF),
            pltpu.VMEM((count, rows, width), BF),
            pltpu.VMEM((count, blocks, rows, fb), BF),
            pltpu.VMEM((count, rows, width), BF),
            pltpu.VMEM((count, rows, width), BF),
            pltpu.VMEM((count, rows, 128), F32),
            pltpu.VMEM((blocks, rows, fb), BF),
            pltpu.VMEM((2, rows, width), BF),
            pltpu.VMEM((rows // 2, fb), F32),
            pltpu.VMEM((rows // 2, fb), F32),
            pltpu.VMEM((rows, width), F32),
            pltpu.VMEM((rows, width), BF),
            pltpu.VMEM((rows, width), BF),
            pltpu.VMEM((rows, width), BF),
            pltpu.VMEM((rows, width), BF),
            pltpu.VMEM((5 + blocks, 8, width), F32),
            pltpu.SemaphoreType.DMA((2 * blocks,)),
            pltpu.SemaphoreType.DMA((3,)),
            pltpu.SemaphoreType.DMA((4,)),
            pltpu.SemaphoreType.DMA((blocks,)),
            pltpu.SemaphoreType.DMA((count, CHUNKS)),
            pltpu.SemaphoreType.DMA((count, CHUNKS)),
        ],
        compiler_params=pltpu.CompilerParams(
            collective_id=0, has_side_effects=True, vmem_limit_bytes=63 * 2**20
        ),
        cost_estimate=pl.CostEstimate(flops=flops, bytes_accessed=60 * 2**20, transcendentals=0),
    )(bucket, plan, *norms, up_bias, inputs, cotangent, up_weight, down_weight, htab, stab)


KINDS = 13
C1, Y1, CHY, INY, RY, Y2, CHZ, INZ, YZ, RZH, RZF, SY, SZ = range(KINDS)
RING = 4
LAGS = (1, 3, 5, 7, 9, 11, 12)


def grads_kernel(
    dp, count, rows, width, units, wide, per_block,
    a_hbm, df_hbm, h_hbm, du_hbm, small_ref,
    down_hbm, up_hbm, small_out,
    at, abuf, dfb, xb, prod, cur, res, stage, c1in, y1in, chy, iny, chz, inz, yz, sm, smin,
    in_sem, x_sem, out_sem, send_sem, recv_sem, sm_send, sm_recv,
):
    me = lax.axis_index("dp")
    n = dp // 4
    core = me % 2
    side = (me // 2) % 2
    z = me // 4
    low = z < n // 2
    inner = jnp.logical_or(z == n // 2 - 1, z == n // 2)
    outer = jnp.logical_not(inner)
    has_out = jnp.logical_and(z > 0, z < n - 1)
    edge = jnp.logical_not(has_out)
    toward = jnp.where(low, 4, -4)
    inward = me + toward
    outward = me - toward
    sibling = me + 1 - 2 * core
    across = me + 2 - 4 * side
    keep = jnp.where(low, 0, 1)
    half = units // 2
    steps = dp.bit_length() - 1
    home = core * 4

    def x_start(u):
        slot = u % 3
        j = u % half
        block = j // per_block
        part = pl.ds(pl.multiple_of((j % per_block) * wide, wide), wide)

        @pl.when(u < half)
        def _():
            pltpu.make_async_copy(h_hbm.at[block, :, :, part], xb.at[slot], x_sem.at[slot]).start()

        @pl.when(u >= half)
        def _():
            pltpu.make_async_copy(du_hbm.at[block, :, :, part], xb.at[slot], x_sem.at[slot]).start()

    def x_wait(u):
        slot = u % 3
        pltpu.make_async_copy(h_hbm.at[0, :, :, pl.ds(0, wide)], xb.at[slot], x_sem.at[slot]).wait()

    df_copy = pltpu.make_async_copy(df_hbm, dfb, in_sem.at[0])
    a_copy = pltpu.make_async_copy(a_hbm, abuf, in_sem.at[1])
    df_copy.start()
    x_start(0)
    x_start(1)
    a_copy.start()

    def partner(s):
        return me + 2**s - 2 ** (s + 1) * ((me // 2**s) % 2)

    barrier = pltpu.get_barrier_semaphore()
    for s in range(steps):
        pl.semaphore_signal(barrier, inc=1, device_id={"dp": partner(s)}, device_id_type=pl.DeviceIdType.MESH)
    pl.semaphore_signal(barrier, inc=1, device_id={"dp": inward}, device_id_type=pl.DeviceIdType.MESH)

    @pl.when(has_out)
    def _():
        pl.semaphore_signal(barrier, inc=1, device_id={"dp": outward}, device_id_type=pl.DeviceIdType.MESH)

    def small_copy(s):
        return pltpu.make_async_remote_copy(
            src_ref=sm.at[s], dst_ref=smin.at[s], send_sem=sm_send.at[s], recv_sem=sm_recv.at[s],
            device_id={"dp": partner(s)}, device_id_type=pl.DeviceIdType.MESH,
        )

    def message(kind, u, src, dst, target):
        return pltpu.make_async_remote_copy(
            src_ref=src, dst_ref=dst, send_sem=send_sem.at[kind, u % RING], recv_sem=recv_sem.at[kind, u],
            device_id={"dp": target}, device_id_type=pl.DeviceIdType.MESH,
        )

    def c1(u):
        return message(C1, u, prod.at[u % RING, pl.ds(4 - home, 4)], c1in.at[u], sibling)

    def y1(u):
        return message(Y1, u, cur.at[u, 1 - side], y1in.at[u], across)

    def ch_y(u):
        return message(CHY, u, cur.at[u, side], chy.at[u], inward)

    def in_y(u):
        return message(INY, u, cur.at[u, side], iny.at[u], inward)

    def r_y(u):
        return message(RY, u, res.at[u, home + side], res.at[u, home + side], outward)

    def y2(u):
        return message(Y2, u, res.at[u, home + side], res.at[u, home + side], across)

    def ch_z(u):
        return message(CHZ, u, cur.at[u, pl.ds(2, 2)], chz.at[u], inward)

    def in_z(u):
        return message(INZ, u, cur.at[u, 3 - keep], inz.at[u], inward)

    def y_z(u):
        return message(YZ, u, cur.at[u, 2 + keep], yz.at[u], across)

    def r_zh(u):
        return message(RZH, u, res.at[u, home + 2 + keep], res.at[u, home + 2 + keep], inward)

    def r_zf(u):
        return message(RZF, u, res.at[u, pl.ds(home + 2, 2)], res.at[u, pl.ds(home + 2, 2)], outward)

    def s_y(u):
        return message(SY, u, res.at[u, pl.ds(home, 2)], res.at[u, pl.ds(home, 2)], sibling)

    def s_z(u):
        return message(SZ, u, res.at[u, pl.ds(home + 2, 2)], res.at[u, pl.ds(home + 2, 2)], sibling)

    def down_copy(u, t):
        part = pl.ds(pl.multiple_of(u * wide, wide), wide)
        return pltpu.make_async_copy(
            stage.at[u % 2, pl.ds(t * wide, wide)], down_hbm.at[0, part, pl.ds(t * wide, wide)],
            out_sem.at[u % 2, t],
        )

    def up_copy(u, t, slot):
        part = pl.ds(pl.multiple_of((u - half) * wide, wide), wide)
        return pltpu.make_async_copy(
            stage.at[slot, pl.ds(t * wide, wide)], up_hbm.at[0, pl.ds(t * wide, wide), part],
            out_sem.at[slot, t],
        )

    def send(make, u):
        @pl.when(u >= RING)
        def _():
            make(u - RING).wait_send()

        make(u).start()

    def plus(left, right):
        return (left.astype(F32) + right.astype(F32)).astype(BF)

    def product(u):
        slot = u % RING
        block = xb.at[u % 3]

        @pl.when(u < half)
        def _():
            value = lax.dot_general(
                block[...].reshape(count * rows, wide), dfb[...].reshape(count * rows, width),
                (((0,), (0,)), ((), ())), preferred_element_type=F32,
            )
            value = jnp.concatenate([value[:, t : t + wide] for t in range(0, width, wide)], axis=0)
            prod[slot] = value.astype(BF).reshape(8, width // 8, wide)

        @pl.when(u >= half)
        def _():
            value = dot(at[...], block[...].reshape(count * rows, wide))
            prod[slot] = value.astype(BF).reshape(8, width // 8, wide)

    def compute(u):
        x_wait(u)

        @pl.when(u + 2 < units)
        def _():
            x_start(u + 2)

        @pl.when(u >= RING)
        def _():
            c1(u - RING).wait_send()

        @pl.when(u == 1)
        def _():
            a_copy.wait()

        for k in range(count):

            @pl.when(u == 2 * k + 2)
            def _():
                at[:, k * rows : (k + 1) * rows] = abuf[k].T

        product(u)
        c1(u).start()

    def stage1(u):
        c1(u).wait_recv()
        cur[u] = plus(prod[u % RING, pl.ds(home, 4)], c1in[u])
        send(y1, u)

        @pl.when(edge)
        def _():
            send(ch_z, u)

    def stage2(u):
        y1(u).wait_recv()
        cur[u, side] = plus(cur[u, side], y1in[u])

        @pl.when(edge)
        def _():
            send(ch_y, u)

        @pl.when(has_out)
        def _():
            ch_z(u).wait_recv()
            cur[u, 2:4] = plus(cur[u, 2:4], chz[u])

        @pl.when(inner)
        def _():
            send(in_z, u)

        @pl.when(jnp.logical_and(outer, has_out))
        def _():
            send(ch_z, u)

    def stage3(u):
        @pl.when(has_out)
        def _():
            ch_y(u).wait_recv()
            cur[u, side] = plus(cur[u, side], chy[u])

        @pl.when(inner)
        def _():
            send(in_y, u)
            in_z(u).wait_recv()
            cur[u, 2 + keep] = plus(cur[u, 2 + keep], inz[u])
            send(y_z, u)

        @pl.when(jnp.logical_and(outer, has_out))
        def _():
            send(ch_y, u)

    def stage4(u):
        @pl.when(inner)
        def _():
            in_y(u).wait_recv()
            res[u, home + side] = plus(cur[u, side], iny[u])
            send(r_y, u)
            send(y2, u)
            y_z(u).wait_recv()
            res[u, home + 2 + keep] = plus(cur[u, 2 + keep], yz[u])
            send(r_zh, u)

    def stage5(u):
        @pl.when(outer)
        def _():
            r_y(u).wait_recv()

            @pl.when(has_out)
            def _():
                send(r_y, u)

            send(y2, u)

        @pl.when(inner)
        def _():
            message(
                RZH, u, res.at[u, home + 3 - keep], res.at[u, home + 3 - keep], inward
            ).wait_recv()
            send(r_zf, u)
            send(s_z, u)

    def stage6(u):
        message(Y2, u, res.at[u, home + 1 - side], res.at[u, home + 1 - side], across).wait_recv()
        send(s_y, u)

        @pl.when(outer)
        def _():
            r_zf(u).wait_recv()

            @pl.when(has_out)
            def _():
                send(r_zf, u)

            send(s_z, u)

    def stage7(u):
        away = 4 - home
        message(SY, u, res.at[u, pl.ds(away, 2)], res.at[u, pl.ds(away, 2)], sibling).wait_recv()
        message(SZ, u, res.at[u, pl.ds(away + 2, 2)], res.at[u, pl.ds(away + 2, 2)], sibling).wait_recv()

        @pl.when(u >= 2)
        def _():
            for t in range(width // wide):
                up_copy(half, t, u % 2).wait()

        stage[u % 2] = res[u].reshape(width, wide)

        @pl.when(u < half)
        def _():
            for t in range(width // wide):
                down_copy(u, t).start()

        @pl.when(u >= half)
        def _():
            for t in range(width // wide):
                up_copy(u, t, u % 2).start()

    stages = (stage1, stage2, stage3, stage4, stage5, stage6, stage7)

    def one(i, carry):
        @pl.when(jnp.logical_and(i > 0, i < units))
        def _():
            compute(i)

        for work, lag in reversed(list(zip(stages, LAGS))):
            u = i - lag

            @pl.when(jnp.logical_and(u >= 0, u < units))
            def _():
                work(u)

        for s in range(steps):

            @pl.when(i == s + 1)
            def _():
                small_copy(s).wait_recv()
                sm[s + 1] = sm[s] + smin[s]
                if s + 1 < steps:
                    small_copy(s + 1).start()

        return carry

    df_copy.wait()
    x_wait(0)
    x_start(2)
    product(0)
    sm[0] = small_ref[...]

    @pl.when(has_out)
    def _():
        pl.semaphore_wait(barrier, steps + 2)

    @pl.when(edge)
    def _():
        pl.semaphore_wait(barrier, steps + 1)

    c1(0).start()
    small_copy(0).start()
    lax.fori_loop(0, units + LAGS[-1], one, 0)

    small_out[...] = sm[steps]
    for s in range(steps):
        small_copy(s).wait_send()

    def drain(u, carry):
        for make in (c1, y1, y2, s_y, s_z):
            make(u).wait_send()

        @pl.when(inner)
        def _():
            for make in (in_z, in_y, y_z, r_zh):
                make(u).wait_send()

        @pl.when(has_out)
        def _():
            for make in (r_y, r_zf):
                make(u).wait_send()

        @pl.when(outer)
        def _():
            for make in (ch_y, ch_z):
                make(u).wait_send()

        return carry

    lax.fori_loop(units - RING, units, drain, 0)
    for slot in range(2):
        for t in range(width // wide):
            up_copy(half, t, slot).wait()


def run_grads(dp, a, df, h, du, small):
    count, rows, width = a.shape
    blocks, fb = h.shape[0], h.shape[-1]
    wide = fb // 3
    half = blocks * 3
    units = 2 * half
    steps = dp.bit_length() - 1
    piece = width // 8
    hidden = blocks * fb
    any_spec = pl.BlockSpec(memory_space=pl.ANY)
    vmem = pl.BlockSpec(memory_space=pltpu.VMEM)
    shape = jax.ShapeDtypeStruct
    body = functools.partial(grads_kernel, dp, count, rows, width, units, wide, 3)
    return pl.pallas_call(
        body,
        out_shape=(shape((1, hidden, width), BF), shape((1, width, hidden), BF), shape(small.shape, F32)),
        in_specs=[any_spec] * 4 + [vmem],
        out_specs=(any_spec, any_spec, vmem),
        scratch_shapes=[
            pltpu.VMEM((width, count * rows), BF),
            pltpu.VMEM((count, rows, width), BF),
            pltpu.VMEM((count, rows, width), BF),
            pltpu.VMEM((3, count, rows, wide), BF),
            pltpu.VMEM((RING, 8, piece, wide), BF),
            pltpu.VMEM((units, 4, piece, wide), BF),
            pltpu.VMEM((units, 8, piece, wide), BF),
            pltpu.VMEM((2, width, wide), BF),
            pltpu.VMEM((units, 4, piece, wide), BF),
            pltpu.VMEM((units, piece, wide), BF),
            pltpu.VMEM((units, piece, wide), BF),
            pltpu.VMEM((units, piece, wide), BF),
            pltpu.VMEM((units, 2, piece, wide), BF),
            pltpu.VMEM((units, piece, wide), BF),
            pltpu.VMEM((units, piece, wide), BF),
            pltpu.VMEM((steps + 1,) + small.shape, F32),
            pltpu.VMEM((steps,) + small.shape, F32),
            pltpu.SemaphoreType.DMA((2,)),
            pltpu.SemaphoreType.DMA((3,)),
            pltpu.SemaphoreType.DMA((2, 3)),
            pltpu.SemaphoreType.DMA((KINDS, RING)),
            pltpu.SemaphoreType.DMA((KINDS, units)),
            pltpu.SemaphoreType.DMA((steps,)),
            pltpu.SemaphoreType.DMA((steps,)),
        ],
        compiler_params=pltpu.CompilerParams(
            collective_id=1, has_side_effects=True, vmem_limit_bytes=60 * 2**20
        ),
    )(a, df, h, du, small)


def widen_kernel(act, grad, down, up, small, act_out, grad_out, g1, b1, up_out, upb, down_out, bd, g2, b2):
    act_out[...] = act[...].astype(F32)
    grad_out[...] = grad[...].astype(F32)
    up_out[...] = up[...].astype(F32)
    down_out[...] = down[...].astype(F32)

    @pl.when(pl.program_id(0) == 0)
    def _():
        width = small.shape[-1]
        for n, out in enumerate((g1, b1, g2, b2, bd)):
            out[...] = small[n : n + 1, :]
        for b in range(upb.shape[-1] // width):
            upb[:, b * width : (b + 1) * width] = small[5 + b : 6 + b, :]


def run_widen(act, grad, down, up, small):
    count, rows, width = act.shape[1:]
    hidden = down.shape[1]
    grid = 4 * count
    token = pl.BlockSpec((1, 1, rows // 4, width), lambda i: (0, i // 4, i % 4, 0))
    tall = pl.BlockSpec((1, hidden // grid, width), lambda i: (0, i, 0))
    flat = pl.BlockSpec((1, width // grid, hidden), lambda i: (0, i, 0))

    def whole(*extent):
        return pl.BlockSpec(extent, lambda i: (0, 0))

    shape = jax.ShapeDtypeStruct
    row = shape((1, width), F32)
    line = whole(1, width)
    return pl.pallas_call(
        widen_kernel,
        grid=(grid,),
        in_specs=[token, token, tall, flat, whole(*small.shape)],
        out_specs=(token, token, line, line, flat, whole(1, hidden), tall, line, line, line),
        out_shape=(
            shape(act.shape, F32), shape(grad.shape, F32), row, row, shape(up.shape, F32),
            shape((1, hidden), F32), shape(down.shape, F32), row, row, row,
        ),
        compiler_params=pltpu.CompilerParams(
            dimension_semantics=("arbitrary",), vmem_limit_bytes=60 * 2**20
        ),
    )(act, grad, down, up, small)


def per_device(
    inputs, bucket, plan, cotangent, norm1_gain, norm1_bias, up_weight, up_bias,
    down_weight, down_bias, norm2_gain, norm2_bias,
):
    count, rows, width = inputs.shape
    hidden = up_weight.shape[-1]
    norms = (norm1_gain, norm1_bias, norm2_gain, norm2_bias, down_bias)
    activations, input_grad, h, du, a, df, small = run_layers(
        bucket, plan, norms, up_bias.reshape(-1, 1, width), inputs, cotangent, up_weight, down_weight
    )
    down_grad, up_grad, small = run_grads(lax.axis_size("dp"), a, df, h, du, small)
    return run_widen(activations, input_grad, down_grad, up_grad, small)


def solution(mesh):
    row = P("pipe", None)
    weight = P("pipe", None, None)
    tokens = P(None, "dp", None)
    result = P("pipe", None, "dp", None)
    return jax.shard_map(
        per_device,
        mesh=mesh,
        in_specs=(tokens, P(), P(), tokens, row, row, weight, row, weight, row, row, row),
        out_specs=(result, result, row, row, weight, row, weight, row, row, row),
        check_vma=False,
    )
```

```python
import functools
import math

import jax
import jax.numpy as jnp
import ml_dtypes
import numpy as np
from jax import lax
from jax.experimental import pallas as pl
from jax.experimental.pallas import tpu as pltpu
from jax.sharding import PartitionSpec as P

BF = jnp.bfloat16
F32 = jnp.float32
TANH_IN = math.sqrt(2.0 / math.pi)
TANH_CUBE = TANH_IN * 0.044715
EPS = 1e-6
CHUNKS = 4


def hidden_tables(width):
    position = np.arange(width)
    angle = 2.0 * np.pi * (np.outer(position, position) % width) / width
    pair = np.stack([np.cos(angle), np.sin(angle)]) / np.sqrt(width)
    return pair.astype(ml_dtypes.bfloat16)


def seq_tables(rows):
    position = np.arange(rows)
    found = []
    for length in (rows // 4, rows // 2, rows):
        same = position[:, None] // length == position[None, :] // length
        phase = (position[:, None] % length) * (position[None, :] % length) % length
        angle = 2.0 * np.pi * phase / length
        found.append(
            np.stack(
                [
                    np.where(same, np.cos(angle), 0.0) / np.sqrt(length),
                    np.where(same, -np.sin(angle), 0.0) / np.sqrt(length),
                ]
            )
        )
    return np.stack(found).astype(ml_dtypes.bfloat16)


def dot(left, right):
    return jnp.dot(left, right, preferred_element_type=F32)


def dot_t(left, right):
    return lax.dot_general(left, right, (((1,), (1,)), ((), ())), preferred_element_type=F32)


def fold8(values):
    return jnp.sum(values.reshape(-1, 8, values.shape[-1]), axis=0)


def layers_kernel(
    count, rows, width, blocks, fb,
    bucket, plan, g1_ref, b1_ref, g2_ref, b2_ref, bd_ref, upb_ref, in_hbm, cot_hbm, wu_hbm, wd_hbm, htab_hbm, stab_hbm,
    act_hbm, grad_hbm, h_hbm, du_hbm, a_hbm, df_hbm, small_ref,
    wu, wd, htab, stab, inbuf, recv, sendbuf, deriv, xh1, xh2, rstd,
    hst, pq, u0, u1, acc, alow, dlow, yst, xst, sums,
    w_sem, t_sem, o_sem, h_sem, send_sem, recv_sem, turn_sem,
):
    first = lax.axis_index("pipe") == 0
    partner = 1 - lax.axis_index("pipe")
    core = lax.axis_index("dp") % 2
    sibling = lax.axis_index("dp") + 1 - 2 * core
    last = blocks - 1

    def wu_copy(b):
        return pltpu.make_async_copy(wu_hbm.at[0, :, pl.ds(b * fb, fb)], wu.at[b], w_sem.at[b])

    def wd_copy(b):
        return pltpu.make_async_copy(wd_hbm.at[0, pl.ds(b * fb, fb), :], wd.at[b], w_sem.at[blocks + b])

    in_copy = pltpu.make_async_copy(in_hbm, inbuf, t_sem.at[0])
    cot_copy = pltpu.make_async_copy(cot_hbm, inbuf, t_sem.at[0])
    htab_copy = pltpu.make_async_copy(htab_hbm, htab, t_sem.at[1])
    stab_copy = pltpu.make_async_copy(stab_hbm, stab, t_sem.at[2])

    def start_weights():
        for b in range(blocks):
            wu_copy(b).start()
            wd_copy(b).start()

    @pl.when(first)
    def _():
        in_copy.start()

    htab_copy.start()
    stab_copy.start()

    @pl.when(jnp.logical_not(first))
    def _():
        start_weights()
        cot_copy.start()

    sums[...] = jnp.zeros_like(sums)

    barrier = pltpu.get_barrier_semaphore()
    pl.semaphore_signal(barrier, inc=1, device_id={"pipe": partner}, device_id_type=pl.DeviceIdType.MESH)
    pl.semaphore_signal(barrier, inc=1, device_id={"dp": sibling}, device_id_type=pl.DeviceIdType.MESH)
    pl.semaphore_wait(barrier, 2)

    span = rows // CHUNKS

    def chunk_copy(k, c):
        part = pl.ds(c * span, span)
        return pltpu.make_async_remote_copy(
            src_ref=sendbuf.at[k, part],
            dst_ref=recv.at[k, part],
            send_sem=send_sem.at[k, c],
            recv_sem=recv_sem.at[k, c],
            device_id={"pipe": partner},
            device_id_type=pl.DeviceIdType.MESH,
        )

    def act_copy(k):
        return pltpu.make_async_copy(yst, act_hbm.at[0, k], o_sem.at[0])

    def grad_copy(k):
        return pltpu.make_async_copy(xst, grad_hbm.at[0, k], o_sem.at[1])

    def a_copy(k):
        return pltpu.make_async_copy(alow, a_hbm.at[k], o_sem.at[2])

    def df_copy(k):
        return pltpu.make_async_copy(dlow, df_hbm.at[k], o_sem.at[3])

    def h_copy(k, b):
        return pltpu.make_async_copy(hst.at[b], h_hbm.at[b, k], h_sem.at[b])

    def du_copy(k, b):
        return pltpu.make_async_copy(hst.at[b], du_hbm.at[b, k], h_sem.at[b])

    def arrived(k, i):
        for c in range(i * CHUNKS // 2, (i + 1) * CHUNKS // 2):
            chunk_copy(k, c).wait_recv()

    def leave(k, i):
        for c in range(i * CHUNKS // 2, (i + 1) * CHUNKS // 2):
            chunk_copy(k, c).start()

    half = rows // 2
    halves = (slice(0, half), slice(half, rows))
    tiles = [[slice(r, r + span) for r in range(h.start, h.stop, span)] for h in halves]
    order = [(i, b) for i in range(2) for b in range(blocks)]
    buffers = (u0, u1)
    g1, b1, g2, b2, bd = (ref[...] for ref in (g1_ref, b1_ref, g2_ref, b2_ref, bd_ref))

    def normalized(values):
        centered = values - jnp.mean(values, axis=-1, keepdims=True)
        scale = lax.rsqrt(jnp.mean(centered * centered, axis=-1, keepdims=True) + EPS)
        return centered * scale, scale

    def norm_back(grad, gain, unit, scale):
        scaled = grad * gain
        mean_one = jnp.mean(scaled, axis=-1, keepdims=True)
        mean_two = jnp.mean(scaled * unit, axis=-1, keepdims=True)
        return scale * (scaled - mean_one - unit * mean_two)

    def pipelined(up, activate, down, before, after):
        before(0)
        up(*order[0], u0)
        for n, (i, b) in enumerate(order):
            if n + 1 < len(order):
                if order[n + 1][1] == 0:
                    before(order[n + 1][0])
                up(*order[n + 1], buffers[(n + 1) % 2])
            if n > 0:
                down(*order[n - 1])
            activate(i, b, buffers[n % 2])
            if n > 0 and order[n - 1][1] == last:
                after(order[n - 1][0])
        down(*order[-1])
        after(1)

    def forward(k, step):
        source = plan[k]
        length = bucket[k]
        level = jnp.where(length == rows, 2, jnp.where(length * 2 == rows, 1, 0))

        @pl.when(step == 0)
        def _():
            htab_copy.wait()

        @pl.when(jnp.logical_and(step == 0, first))
        def _():
            in_copy.wait()
            start_weights()

        @pl.when(first)
        def _():
            recv[k] = inbuf[source]

        for i, part in enumerate(halves):

            @pl.when(jnp.logical_not(first))
            def _():
                arrived(k, i)

            pq[0, part] = dot(recv[k, part], htab[0]).astype(BF)
            pq[1, part] = dot(recv[k, part], htab[1]).astype(BF)

        @pl.when(step == 0)
        def _():
            stab_copy.wait()

        @pl.when(step > 0)
        def _():
            for b in range(blocks):
                h_copy(k, b).wait()

        @pl.when(k > 0)
        def _():
            a_copy(k).wait()

        for part in halves:
            mixed = dot(stab[level, 0, part, :], pq[0]) + dot(stab[level, 1, part, :], pq[1])
            unit, scale = normalized(recv[k, part, :].astype(F32) + mixed)
            xh1[k, part, :] = unit.astype(BF)
            rstd[k, part, 0:1] = scale
            value = unit * g1 + b1
            alow[part, :] = value.astype(BF)
            acc[part, :] = value + bd
        a_copy(k).start()

        @pl.when(step == 0)
        def _():
            for b in range(blocks):
                wu_copy(b).wait()
                wd_copy(b).wait()

        @pl.when(k > 0)
        def _():
            act_copy(k).wait()

        def up(i, b, u):
            u[...] = dot(alow[halves[i], :], wu[b])

        def activate(i, b, u):
            pre = u[...] + upb_ref[b]
            square = pre * pre
            level_half = 0.5 * jnp.tanh(pre * (TANH_IN + TANH_CUBE * square)) + 0.5
            value = pre * level_half
            slope = level_half + value * (1.0 - level_half) * (2.0 * TANH_IN + 6.0 * TANH_CUBE * square)
            hst[b, halves[i], :] = value.astype(BF)
            deriv[k, b, halves[i], :] = slope.astype(BF)

        def down(i, b):
            acc[halves[i], :] += dot(hst[b, halves[i], :], wd[b])

        def before(i):
            pass

        def after(i):
            for part in tiles[i]:
                unit, scale = normalized(acc[part, :])
                xh2[k, part, :] = unit.astype(BF)
                rstd[k, part, 1:2] = scale
                value = unit * g2 + b2
                rounded = value.astype(BF)
                yst[part, :] = rounded
                sendbuf[k, part, :] = rounded

            if i == 0:

                @pl.when(jnp.logical_and(first, core + k > 0))
                def _():
                    pl.semaphore_wait(turn_sem, 1)

            @pl.when(first)
            def _():
                leave(k, i)

            if i == 1:

                @pl.when(jnp.logical_and(first, k + core < count))
                def _():
                    for c in range(CHUNKS):
                        chunk_copy(k, c).wait_send()
                    pl.semaphore_signal(
                        turn_sem, inc=1, device_id={"dp": sibling}, device_id_type=pl.DeviceIdType.MESH
                    )

        pipelined(up, activate, down, before, after)
        for b in range(blocks):
            h_copy(k, b).start()
        act_copy(k).start()

    def backward(k, step):
        length = bucket[k]
        level = jnp.where(length == rows, 2, jnp.where(length * 2 == rows, 1, 0))

        @pl.when(jnp.logical_and(k == 0, jnp.logical_not(first)))
        def _():
            cot_copy.wait()

        @pl.when(jnp.logical_and(first, k + core == count))
        def _():
            for c in range(CHUNKS):
                chunk_copy(k, c).wait_send()

        @pl.when(k > 0)
        def _():
            df_copy(k).wait()
            grad_copy(k).wait()

        def before(i):
            @pl.when(first)
            def _():
                arrived(k, i)

            for part in tiles[i]:
                grad = jnp.where(first, recv[k, part, :], inbuf[k, part, :]).astype(F32)
                unit = xh2[k, part, :].astype(F32)
                back = norm_back(grad, g2, unit, rstd[k, part, 1:2])
                rounded = back.astype(BF)
                dlow[part, :] = rounded
                acc[part, :] = back
                sums[2] += fold8(grad * unit)
                sums[3] += fold8(grad)
                sums[4] += fold8(rounded.astype(F32))
            if i == 0:
                for b in range(blocks):
                    du_copy(k, b).wait()

        def up(i, b, u):
            u[...] = dot_t(dlow[halves[i], :], wd[b])

        def activate(i, b, u):
            rounded = (u[...] * deriv[k, b, halves[i], :].astype(F32)).astype(BF)
            hst[b, halves[i], :] = rounded
            sums[5 + b] += fold8(rounded.astype(F32))

        def down(i, b):
            acc[halves[i], :] += dot_t(hst[b, halves[i], :], wu[b])

        def after(i):
            for part in tiles[i]:
                grad = acc[part, :]
                unit = xh1[k, part, :].astype(F32)
                back = norm_back(grad, g1, unit, rstd[k, part, 0:1])
                acc[part, :] = back
                recv[k, part, :] = back.astype(BF)
                sums[0] += fold8(grad * unit)
                sums[1] += fold8(grad)

        pipelined(up, activate, down, before, after)
        df_copy(k).start()
        for b in range(blocks):
            du_copy(k, b).start()

        pq[0] = dot(stab[level, 0], recv[k]).astype(BF)
        pq[1] = dot(stab[level, 1], recv[k]).astype(BF)

        for i, part in enumerate(halves):
            value = acc[part, :] + dot(pq[0, part, :], htab[0]) + dot(pq[1, part, :], htab[1])
            rounded = value.astype(BF)
            xst[part, :] = rounded
            sendbuf[k, part, :] = rounded

            @pl.when(jnp.logical_not(first))
            def _():
                leave(k, i)

        grad_copy(k).start()

    def one(step, carry):
        forwards = jnp.where(first, step < count, lax.rem(step, 2) == 0)
        k = jnp.where(first, lax.rem(step, count), step // 2)

        @pl.when(forwards)
        def _():
            forward(k, step)

        @pl.when(jnp.logical_not(forwards))
        def _():
            backward(k, step)

        return carry

    lax.fori_loop(0, 2 * count, one, 0)

    end = count - 1

    for n in range(5 + blocks):
        small_ref[n : n + 1, :] = jnp.sum(sums[n], axis=0, keepdims=True)
    for n in range(5 + blocks, small_ref.shape[0]):
        small_ref[n : n + 1, :] = jnp.zeros((1, width), F32)
    act_copy(end).wait()
    grad_copy(end).wait()
    a_copy(end).wait()
    df_copy(end).wait()
    for b in range(blocks):
        du_copy(end, b).wait()

    @pl.when(jnp.logical_not(first))
    def _():
        for k in range(count):
            for c in range(CHUNKS):
                chunk_copy(k, c).wait_send()


def run_layers(bucket, plan, norms, up_bias, inputs, cotangent, up_weight, down_weight):
    count, rows, width = inputs.shape
    hidden = up_weight.shape[-1]
    fb = width
    blocks = hidden // fb
    htab = jnp.asarray(hidden_tables(width))
    stab = jnp.asarray(seq_tables(rows))
    any_spec = pl.BlockSpec(memory_space=pl.ANY)
    smem = pl.BlockSpec(memory_space=pltpu.SMEM)
    vmem = pl.BlockSpec(memory_space=pltpu.VMEM)
    shape = jax.ShapeDtypeStruct
    body = functools.partial(layers_kernel, count, rows, width, blocks, fb)
    flops = count * (12 * rows * width * hidden // 1 + 4 * rows * width * (2 * width + 2 * rows))
    return pl.pallas_call(
        body,
        out_shape=(
            shape((1, count, rows, width), BF),
            shape((1, count, rows, width), BF),
            shape((blocks, count, rows, fb), BF),
            shape((blocks, count, rows, fb), BF),
            shape((count, rows, width), BF),
            shape((count, rows, width), BF),
            shape((16, width), F32),
        ),
        in_specs=[smem, smem] + [vmem] * 6 + [any_spec] * 6,
        out_specs=(any_spec,) * 6 + (vmem,),
        scratch_shapes=[
            pltpu.VMEM((blocks, width, fb), BF),
            pltpu.VMEM((blocks, fb, width), BF),
            pltpu.VMEM((2, width, width), BF),
            pltpu.VMEM((3, 2, rows, rows), BF),
            pltpu.VMEM((count, rows, width), BF),
            pltpu.VMEM((count, rows, width), BF),
            pltpu.VMEM((count, rows, width), BF),
            pltpu.VMEM((count, blocks, rows, fb), BF),
            pltpu.VMEM((count, rows, width), BF),
            pltpu.VMEM((count, rows, width), BF),
            pltpu.VMEM((count, rows, 128), F32),
            pltpu.VMEM((blocks, rows, fb), BF),
            pltpu.VMEM((2, rows, width), BF),
            pltpu.VMEM((rows // 2, fb), F32),
            pltpu.VMEM((rows // 2, fb), F32),
            pltpu.VMEM((rows, width), F32),
            pltpu.VMEM((rows, width), BF),
            pltpu.VMEM((rows, width), BF),
            pltpu.VMEM((rows, width), BF),
            pltpu.VMEM((rows, width), BF),
            pltpu.VMEM((5 + blocks, 8, width), F32),
            pltpu.SemaphoreType.DMA((2 * blocks,)),
            pltpu.SemaphoreType.DMA((3,)),
            pltpu.SemaphoreType.DMA((4,)),
            pltpu.SemaphoreType.DMA((blocks,)),
            pltpu.SemaphoreType.DMA((count, CHUNKS)),
            pltpu.SemaphoreType.DMA((count, CHUNKS)),
            pltpu.SemaphoreType.REGULAR,
        ],
        compiler_params=pltpu.CompilerParams(
            collective_id=0, has_side_effects=True, vmem_limit_bytes=63 * 2**20
        ),
        cost_estimate=pl.CostEstimate(flops=flops, bytes_accessed=60 * 2**20, transcendentals=0),
    )(bucket, plan, *norms, up_bias, inputs, cotangent, up_weight, down_weight, htab, stab)


KINDS = 13
C1, Y1, CHY, INY, RY, Y2, CHZ, INZ, YZ, RZH, RZF, SY, SZ = range(KINDS)
RING = 4
LAGS = (1, 3, 5, 7, 9, 11, 12)


def grads_kernel(
    dp, count, rows, width, units, wide, per_block,
    a_hbm, df_hbm, h_hbm, du_hbm, small_ref,
    down_hbm, up_hbm, small_out,
    at, abuf, dfb, xb, prod, cur, res, stage, c1in, y1in, chy, iny, chz, inz, yz, sm, smin,
    in_sem, x_sem, out_sem, send_sem, recv_sem, sm_send, sm_recv,
):
    me = lax.axis_index("dp")
    n = dp // 4
    core = me % 2
    side = (me // 2) % 2
    z = me // 4
    low = z < n // 2
    inner = jnp.logical_or(z == n // 2 - 1, z == n // 2)
    outer = jnp.logical_not(inner)
    has_out = jnp.logical_and(z > 0, z < n - 1)
    edge = jnp.logical_not(has_out)
    toward = jnp.where(low, 4, -4)
    inward = me + toward
    outward = me - toward
    sibling = me + 1 - 2 * core
    across = me + 2 - 4 * side
    keep = jnp.where(low, 0, 1)
    half = units // 2
    steps = dp.bit_length() - 1
    home = core * 4

    def x_start(u):
        slot = u % 3
        j = u % half
        block = j // per_block
        part = pl.ds(pl.multiple_of((j % per_block) * wide, wide), wide)

        @pl.when(u < half)
        def _():
            pltpu.make_async_copy(h_hbm.at[block, :, :, part], xb.at[slot], x_sem.at[slot]).start()

        @pl.when(u >= half)
        def _():
            pltpu.make_async_copy(du_hbm.at[block, :, :, part], xb.at[slot], x_sem.at[slot]).start()

    def x_wait(u):
        slot = u % 3
        pltpu.make_async_copy(h_hbm.at[0, :, :, pl.ds(0, wide)], xb.at[slot], x_sem.at[slot]).wait()

    df_copy = pltpu.make_async_copy(df_hbm, dfb, in_sem.at[0])
    a_copy = pltpu.make_async_copy(a_hbm, abuf, in_sem.at[1])
    df_copy.start()
    x_start(0)
    x_start(1)
    a_copy.start()

    def partner(s):
        return me + 2**s - 2 ** (s + 1) * ((me // 2**s) % 2)

    barrier = pltpu.get_barrier_semaphore()
    for s in range(steps):
        pl.semaphore_signal(barrier, inc=1, device_id={"dp": partner(s)}, device_id_type=pl.DeviceIdType.MESH)
    pl.semaphore_signal(barrier, inc=1, device_id={"dp": inward}, device_id_type=pl.DeviceIdType.MESH)

    @pl.when(has_out)
    def _():
        pl.semaphore_signal(barrier, inc=1, device_id={"dp": outward}, device_id_type=pl.DeviceIdType.MESH)

    def small_copy(s):
        return pltpu.make_async_remote_copy(
            src_ref=sm.at[s], dst_ref=smin.at[s], send_sem=sm_send.at[s], recv_sem=sm_recv.at[s],
            device_id={"dp": partner(s)}, device_id_type=pl.DeviceIdType.MESH,
        )

    def message(kind, u, src, dst, target):
        return pltpu.make_async_remote_copy(
            src_ref=src, dst_ref=dst, send_sem=send_sem.at[kind, u % RING], recv_sem=recv_sem.at[kind, u],
            device_id={"dp": target}, device_id_type=pl.DeviceIdType.MESH,
        )

    def c1(u):
        return message(C1, u, prod.at[u % RING, pl.ds(4 - home, 4)], c1in.at[u], sibling)

    def y1(u):
        return message(Y1, u, cur.at[u, 1 - side], y1in.at[u], across)

    def ch_y(u):
        return message(CHY, u, cur.at[u, side], chy.at[u], inward)

    def in_y(u):
        return message(INY, u, cur.at[u, side], iny.at[u], inward)

    def r_y(u):
        return message(RY, u, res.at[u, home + side], res.at[u, home + side], outward)

    def y2(u):
        return message(Y2, u, res.at[u, home + side], res.at[u, home + side], across)

    def ch_z(u):
        return message(CHZ, u, cur.at[u, pl.ds(2, 2)], chz.at[u], inward)

    def in_z(u):
        return message(INZ, u, cur.at[u, 3 - keep], inz.at[u], inward)

    def y_z(u):
        return message(YZ, u, cur.at[u, 2 + keep], yz.at[u], across)

    def r_zh(u):
        return message(RZH, u, res.at[u, home + 2 + keep], res.at[u, home + 2 + keep], inward)

    def r_zf(u):
        return message(RZF, u, res.at[u, pl.ds(home + 2, 2)], res.at[u, pl.ds(home + 2, 2)], outward)

    def s_y(u):
        return message(SY, u, res.at[u, pl.ds(home, 2)], res.at[u, pl.ds(home, 2)], sibling)

    def s_z(u):
        return message(SZ, u, res.at[u, pl.ds(home + 2, 2)], res.at[u, pl.ds(home + 2, 2)], sibling)

    def down_copy(u, t):
        part = pl.ds(pl.multiple_of(u * wide, wide), wide)
        return pltpu.make_async_copy(
            stage.at[u % 2, pl.ds(t * wide, wide)], down_hbm.at[0, part, pl.ds(t * wide, wide)],
            out_sem.at[u % 2, t],
        )

    def up_copy(u, t, slot):
        part = pl.ds(pl.multiple_of((u - half) * wide, wide), wide)
        return pltpu.make_async_copy(
            stage.at[slot, pl.ds(t * wide, wide)], up_hbm.at[0, pl.ds(t * wide, wide), part],
            out_sem.at[slot, t],
        )

    def send(make, u):
        @pl.when(u >= RING)
        def _():
            make(u - RING).wait_send()

        make(u).start()

    def plus(left, right):
        return (left.astype(F32) + right.astype(F32)).astype(BF)

    def product(u):
        slot = u % RING
        block = xb.at[u % 3]

        @pl.when(u < half)
        def _():
            value = lax.dot_general(
                block[...].reshape(count * rows, wide), dfb[...].reshape(count * rows, width),
                (((0,), (0,)), ((), ())), preferred_element_type=F32,
            )
            value = jnp.concatenate([value[:, t : t + wide] for t in range(0, width, wide)], axis=0)
            prod[slot] = value.astype(BF).reshape(8, width // 8, wide)

        @pl.when(u >= half)
        def _():
            value = dot(at[...], block[...].reshape(count * rows, wide))
            prod[slot] = value.astype(BF).reshape(8, width // 8, wide)

    def compute(u):
        x_wait(u)

        @pl.when(u + 2 < units)
        def _():
            x_start(u + 2)

        @pl.when(u >= RING)
        def _():
            c1(u - RING).wait_send()

        @pl.when(u == 1)
        def _():
            a_copy.wait()

        for k in range(count):

            @pl.when(u == 2 * k + 2)
            def _():
                at[:, k * rows : (k + 1) * rows] = abuf[k].T

        product(u)
        c1(u).start()

    def stage1(u):
        c1(u).wait_recv()
        cur[u] = plus(prod[u % RING, pl.ds(home, 4)], c1in[u])
        send(y1, u)

        @pl.when(edge)
        def _():
            send(ch_z, u)

    def stage2(u):
        y1(u).wait_recv()
        cur[u, side] = plus(cur[u, side], y1in[u])

        @pl.when(edge)
        def _():
            send(ch_y, u)

        @pl.when(has_out)
        def _():
            ch_z(u).wait_recv()
            cur[u, 2:4] = plus(cur[u, 2:4], chz[u])

        @pl.when(inner)
        def _():
            send(in_z, u)

        @pl.when(jnp.logical_and(outer, has_out))
        def _():
            send(ch_z, u)

    def stage3(u):
        @pl.when(has_out)
        def _():
            ch_y(u).wait_recv()
            cur[u, side] = plus(cur[u, side], chy[u])

        @pl.when(inner)
        def _():
            send(in_y, u)
            in_z(u).wait_recv()
            cur[u, 2 + keep] = plus(cur[u, 2 + keep], inz[u])
            send(y_z, u)

        @pl.when(jnp.logical_and(outer, has_out))
        def _():
            send(ch_y, u)

    def stage4(u):
        @pl.when(inner)
        def _():
            in_y(u).wait_recv()
            res[u, home + side] = plus(cur[u, side], iny[u])
            send(r_y, u)
            send(y2, u)
            y_z(u).wait_recv()
            res[u, home + 2 + keep] = plus(cur[u, 2 + keep], yz[u])
            send(r_zh, u)

    def stage5(u):
        @pl.when(outer)
        def _():
            r_y(u).wait_recv()

            @pl.when(has_out)
            def _():
                send(r_y, u)

            send(y2, u)

        @pl.when(inner)
        def _():
            message(
                RZH, u, res.at[u, home + 3 - keep], res.at[u, home + 3 - keep], inward
            ).wait_recv()
            send(r_zf, u)
            send(s_z, u)

    def stage6(u):
        message(Y2, u, res.at[u, home + 1 - side], res.at[u, home + 1 - side], across).wait_recv()
        send(s_y, u)

        @pl.when(outer)
        def _():
            r_zf(u).wait_recv()

            @pl.when(has_out)
            def _():
                send(r_zf, u)

            send(s_z, u)

    def stage7(u):
        away = 4 - home
        message(SY, u, res.at[u, pl.ds(away, 2)], res.at[u, pl.ds(away, 2)], sibling).wait_recv()
        message(SZ, u, res.at[u, pl.ds(away + 2, 2)], res.at[u, pl.ds(away + 2, 2)], sibling).wait_recv()

        @pl.when(u >= 2)
        def _():
            for t in range(width // wide):
                up_copy(half, t, u % 2).wait()

        stage[u % 2] = res[u].reshape(width, wide)

        @pl.when(u < half)
        def _():
            for t in range(width // wide):
                down_copy(u, t).start()

        @pl.when(u >= half)
        def _():
            for t in range(width // wide):
                up_copy(u, t, u % 2).start()

    stages = (stage1, stage2, stage3, stage4, stage5, stage6, stage7)

    def one(i, carry):
        @pl.when(jnp.logical_and(i > 0, i < units))
        def _():
            compute(i)

        for work, lag in reversed(list(zip(stages, LAGS))):
            u = i - lag

            @pl.when(jnp.logical_and(u >= 0, u < units))
            def _():
                work(u)

        for s in range(steps):

            @pl.when(i == s + 1)
            def _():
                small_copy(s).wait_recv()
                sm[s + 1] = sm[s] + smin[s]
                if s + 1 < steps:
                    small_copy(s + 1).start()

        return carry

    df_copy.wait()
    x_wait(0)
    x_start(2)
    product(0)
    sm[0] = small_ref[...]

    @pl.when(has_out)
    def _():
        pl.semaphore_wait(barrier, steps + 2)

    @pl.when(edge)
    def _():
        pl.semaphore_wait(barrier, steps + 1)

    c1(0).start()
    small_copy(0).start()
    lax.fori_loop(0, units + LAGS[-1], one, 0)

    small_out[...] = sm[steps]
    for s in range(steps):
        small_copy(s).wait_send()

    def drain(u, carry):
        for make in (c1, y1, y2, s_y, s_z):
            make(u).wait_send()

        @pl.when(inner)
        def _():
            for make in (in_z, in_y, y_z, r_zh):
                make(u).wait_send()

        @pl.when(has_out)
        def _():
            for make in (r_y, r_zf):
                make(u).wait_send()

        @pl.when(outer)
        def _():
            for make in (ch_y, ch_z):
                make(u).wait_send()

        return carry

    lax.fori_loop(units - RING, units, drain, 0)
    for slot in range(2):
        for t in range(width // wide):
            up_copy(half, t, slot).wait()


def run_grads(dp, a, df, h, du, small):
    count, rows, width = a.shape
    blocks, fb = h.shape[0], h.shape[-1]
    wide = fb // 3
    half = blocks * 3
    units = 2 * half
    steps = dp.bit_length() - 1
    piece = width // 8
    hidden = blocks * fb
    any_spec = pl.BlockSpec(memory_space=pl.ANY)
    vmem = pl.BlockSpec(memory_space=pltpu.VMEM)
    shape = jax.ShapeDtypeStruct
    body = functools.partial(grads_kernel, dp, count, rows, width, units, wide, 3)
    return pl.pallas_call(
        body,
        out_shape=(shape((1, hidden, width), BF), shape((1, width, hidden), BF), shape(small.shape, F32)),
        in_specs=[any_spec] * 4 + [vmem],
        out_specs=(any_spec, any_spec, vmem),
        scratch_shapes=[
            pltpu.VMEM((width, count * rows), BF),
            pltpu.VMEM((count, rows, width), BF),
            pltpu.VMEM((count, rows, width), BF),
            pltpu.VMEM((3, count, rows, wide), BF),
            pltpu.VMEM((RING, 8, piece, wide), BF),
            pltpu.VMEM((units, 4, piece, wide), BF),
            pltpu.VMEM((units, 8, piece, wide), BF),
            pltpu.VMEM((2, width, wide), BF),
            pltpu.VMEM((units, 4, piece, wide), BF),
            pltpu.VMEM((units, piece, wide), BF),
            pltpu.VMEM((units, piece, wide), BF),
            pltpu.VMEM((units, piece, wide), BF),
            pltpu.VMEM((units, 2, piece, wide), BF),
            pltpu.VMEM((units, piece, wide), BF),
            pltpu.VMEM((units, piece, wide), BF),
            pltpu.VMEM((steps + 1,) + small.shape, F32),
            pltpu.VMEM((steps,) + small.shape, F32),
            pltpu.SemaphoreType.DMA((2,)),
            pltpu.SemaphoreType.DMA((3,)),
            pltpu.SemaphoreType.DMA((2, 3)),
            pltpu.SemaphoreType.DMA((KINDS, RING)),
            pltpu.SemaphoreType.DMA((KINDS, units)),
            pltpu.SemaphoreType.DMA((steps,)),
            pltpu.SemaphoreType.DMA((steps,)),
        ],
        compiler_params=pltpu.CompilerParams(
            collective_id=1, has_side_effects=True, vmem_limit_bytes=60 * 2**20
        ),
    )(a, df, h, du, small)


def widen_kernel(act, grad, down, up, small, act_out, grad_out, g1, b1, up_out, upb, down_out, bd, g2, b2):
    act_out[...] = act[...].astype(F32)
    grad_out[...] = grad[...].astype(F32)
    up_out[...] = up[...].astype(F32)
    down_out[...] = down[...].astype(F32)

    @pl.when(pl.program_id(0) == 0)
    def _():
        width = small.shape[-1]
        for n, out in enumerate((g1, b1, g2, b2, bd)):
            out[...] = small[n : n + 1, :]
        for b in range(upb.shape[-1] // width):
            upb[:, b * width : (b + 1) * width] = small[5 + b : 6 + b, :]


def run_widen(act, grad, down, up, small):
    count, rows, width = act.shape[1:]
    hidden = down.shape[1]
    grid = 4 * count
    token = pl.BlockSpec((1, 1, rows // 4, width), lambda i: (0, i // 4, i % 4, 0))
    tall = pl.BlockSpec((1, hidden // grid, width), lambda i: (0, i, 0))
    flat = pl.BlockSpec((1, width // grid, hidden), lambda i: (0, i, 0))

    def whole(*extent):
        return pl.BlockSpec(extent, lambda i: (0, 0))

    shape = jax.ShapeDtypeStruct
    row = shape((1, width), F32)
    line = whole(1, width)
    return pl.pallas_call(
        widen_kernel,
        grid=(grid,),
        in_specs=[token, token, tall, flat, whole(*small.shape)],
        out_specs=(token, token, line, line, flat, whole(1, hidden), tall, line, line, line),
        out_shape=(
            shape(act.shape, F32), shape(grad.shape, F32), row, row, shape(up.shape, F32),
            shape((1, hidden), F32), shape(down.shape, F32), row, row, row,
        ),
        compiler_params=pltpu.CompilerParams(
            dimension_semantics=("arbitrary",), vmem_limit_bytes=60 * 2**20
        ),
    )(act, grad, down, up, small)


def per_device(
    inputs, bucket, plan, cotangent, norm1_gain, norm1_bias, up_weight, up_bias,
    down_weight, down_bias, norm2_gain, norm2_bias,
):
    count, rows, width = inputs.shape
    hidden = up_weight.shape[-1]
    norms = (norm1_gain, norm1_bias, norm2_gain, norm2_bias, down_bias)
    activations, input_grad, h, du, a, df, small = run_layers(
        bucket, plan, norms, up_bias.reshape(-1, 1, width), inputs, cotangent, up_weight, down_weight
    )
    down_grad, up_grad, small = run_grads(lax.axis_size("dp"), a, df, h, du, small)
    return run_widen(activations, input_grad, down_grad, up_grad, small)


def solution(mesh):
    row = P("pipe", None)
    weight = P("pipe", None, None)
    tokens = P(None, "dp", None)
    result = P("pipe", None, "dp", None)
    return jax.shard_map(
        per_device,
        mesh=mesh,
        in_specs=(tokens, P(), P(), tokens, row, row, weight, row, weight, row, row, row),
        out_specs=(result, result, row, row, weight, row, weight, row, row, row),
        check_vma=False,
    )
```

```python
import functools
import math

import jax
import jax.numpy as jnp
import ml_dtypes
import numpy as np
from jax import lax
from jax.experimental import pallas as pl
from jax.experimental.pallas import tpu as pltpu
from jax.sharding import PartitionSpec as P

BF = jnp.bfloat16
F32 = jnp.float32
TANH_IN = math.sqrt(2.0 / math.pi)
TANH_CUBE = TANH_IN * 0.044715
EPS = 1e-6
CHUNKS = 4


def hidden_tables(width):
    position = np.arange(width)
    angle = 2.0 * np.pi * (np.outer(position, position) % width) / width
    pair = np.stack([np.cos(angle), np.sin(angle)]) / np.sqrt(width)
    return pair.astype(ml_dtypes.bfloat16)


def seq_tables(rows):
    position = np.arange(rows)
    found = []
    for length in (rows // 4, rows // 2, rows):
        same = position[:, None] // length == position[None, :] // length
        phase = (position[:, None] % length) * (position[None, :] % length) % length
        angle = 2.0 * np.pi * phase / length
        found.append(
            np.stack(
                [
                    np.where(same, np.cos(angle), 0.0) / np.sqrt(length),
                    np.where(same, -np.sin(angle), 0.0) / np.sqrt(length),
                ]
            )
        )
    return np.stack(found).astype(ml_dtypes.bfloat16)


def dot(left, right):
    return jnp.dot(left, right, preferred_element_type=F32)


def dot_t(left, right):
    return lax.dot_general(left, right, (((1,), (1,)), ((), ())), preferred_element_type=F32)


def fold8(values):
    return jnp.sum(values.reshape(-1, 8, values.shape[-1]), axis=0)


def layers_kernel(
    count, rows, width, blocks, fb,
    bucket, plan, g1_ref, b1_ref, g2_ref, b2_ref, bd_ref, upb_ref, in_hbm, cot_hbm, wu_hbm, wd_hbm, htab_hbm, stab_hbm,
    act_hbm, grad_hbm, h_hbm, du_hbm, a_hbm, df_hbm, small_ref,
    wu, wd, htab, stab, inbuf, recv, sendbuf, deriv, xh1, xh2, rstd,
    hst, pq, u0, u1, acc, alow, dlow, yst, xst, sums,
    w_sem, t_sem, o_sem, h_sem, send_sem, recv_sem, turn_sem,
):
    first = lax.axis_index("pipe") == 0
    partner = 1 - lax.axis_index("pipe")
    core = lax.axis_index("dp") % 2
    sibling = lax.axis_index("dp") + 1 - 2 * core
    last = blocks - 1

    def wu_copy(b):
        return pltpu.make_async_copy(wu_hbm.at[0, :, pl.ds(b * fb, fb)], wu.at[b], w_sem.at[b])

    def wd_copy(b):
        return pltpu.make_async_copy(wd_hbm.at[0, pl.ds(b * fb, fb), :], wd.at[b], w_sem.at[blocks + b])

    in_copy = pltpu.make_async_copy(in_hbm, inbuf, t_sem.at[0])
    cot_copy = pltpu.make_async_copy(cot_hbm, inbuf, t_sem.at[0])
    htab_copy = pltpu.make_async_copy(htab_hbm, htab, t_sem.at[1])
    stab_copy = pltpu.make_async_copy(stab_hbm, stab, t_sem.at[2])

    def start_weights():
        for b in range(blocks):
            wu_copy(b).start()
            wd_copy(b).start()

    @pl.when(first)
    def _():
        in_copy.start()

    htab_copy.start()
    stab_copy.start()

    @pl.when(jnp.logical_not(first))
    def _():
        start_weights()
        cot_copy.start()

    sums[...] = jnp.zeros_like(sums)

    barrier = pltpu.get_barrier_semaphore()
    pl.semaphore_signal(barrier, inc=1, device_id={"pipe": partner}, device_id_type=pl.DeviceIdType.MESH)
    pl.semaphore_signal(barrier, inc=1, device_id={"dp": sibling}, device_id_type=pl.DeviceIdType.MESH)
    pl.semaphore_wait(barrier, 2)

    span = rows // CHUNKS

    def chunk_copy(k, c):
        part = pl.ds(c * span, span)
        return pltpu.make_async_remote_copy(
            src_ref=sendbuf.at[k, part],
            dst_ref=recv.at[k, part],
            send_sem=send_sem.at[k, c],
            recv_sem=recv_sem.at[k, c],
            device_id={"pipe": partner},
            device_id_type=pl.DeviceIdType.MESH,
        )

    def act_copy(k):
        return pltpu.make_async_copy(yst, act_hbm.at[0, k], o_sem.at[0])

    def grad_copy(k):
        return pltpu.make_async_copy(xst, grad_hbm.at[0, k], o_sem.at[1])

    def a_copy(k):
        return pltpu.make_async_copy(alow, a_hbm.at[k], o_sem.at[2])

    def df_copy(k):
        return pltpu.make_async_copy(dlow, df_hbm.at[k], o_sem.at[3])

    def h_copy(k, b):
        return pltpu.make_async_copy(hst.at[b], h_hbm.at[b, k], h_sem.at[b])

    def du_copy(k, b):
        return pltpu.make_async_copy(hst.at[b], du_hbm.at[b, k], h_sem.at[b])

    def arrived(k, i):
        for c in range(i * CHUNKS // 2, (i + 1) * CHUNKS // 2):
            chunk_copy(k, c).wait_recv()

    def leave(k, i):
        for c in range(i * CHUNKS // 2, (i + 1) * CHUNKS // 2):
            chunk_copy(k, c).start()

    half = rows // 2
    halves = (slice(0, half), slice(half, rows))
    tiles = [[slice(r, r + span) for r in range(h.start, h.stop, span)] for h in halves]
    order = [(i, b) for i in range(2) for b in range(blocks)]
    buffers = (u0, u1)
    g1, b1, g2, b2, bd = (ref[...] for ref in (g1_ref, b1_ref, g2_ref, b2_ref, bd_ref))

    def normalized(values):
        centered = values - jnp.mean(values, axis=-1, keepdims=True)
        scale = lax.rsqrt(jnp.mean(centered * centered, axis=-1, keepdims=True) + EPS)
        return centered * scale, scale

    def norm_back(grad, gain, unit, scale):
        scaled = grad * gain
        mean_one = jnp.mean(scaled, axis=-1, keepdims=True)
        mean_two = jnp.mean(scaled * unit, axis=-1, keepdims=True)
        return scale * (scaled - mean_one - unit * mean_two)

    def pipelined(up, activate, down, before, after):
        before(0)
        up(*order[0], u0)
        for n, (i, b) in enumerate(order):
            if n + 1 < len(order):
                if order[n + 1][1] == 0:
                    before(order[n + 1][0])
                up(*order[n + 1], buffers[(n + 1) % 2])
            if n > 0:
                down(*order[n - 1])
            activate(i, b, buffers[n % 2])
            if n > 0 and order[n - 1][1] == last:
                after(order[n - 1][0])
        down(*order[-1])
        after(1)

    def forward(k, opening):
        source = plan[k]
        length = bucket[k]
        level = jnp.where(length == rows, 2, jnp.where(length * 2 == rows, 1, 0))

        if opening:
            htab_copy.wait()

            @pl.when(first)
            def _():
                in_copy.wait()
                start_weights()

        @pl.when(first)
        def _():
            recv[k] = inbuf[source]

        for i, part in enumerate(halves):

            @pl.when(jnp.logical_not(first))
            def _():
                arrived(k, i)

            pq[0, part] = dot(recv[k, part], htab[0]).astype(BF)
            pq[1, part] = dot(recv[k, part], htab[1]).astype(BF)

        if opening:
            stab_copy.wait()
        else:
            for b in range(blocks):
                h_copy(k, b).wait()
            a_copy(k).wait()
            act_copy(k).wait()

        for part in halves:
            mixed = dot(stab[level, 0, part, :], pq[0]) + dot(stab[level, 1, part, :], pq[1])
            unit, scale = normalized(recv[k, part, :].astype(F32) + mixed)
            xh1[k, part, :] = unit.astype(BF)
            rstd[k, part, 0:1] = scale
            value = unit * g1 + b1
            alow[part, :] = value.astype(BF)
            acc[part, :] = value + bd
        if opening:
            for b in range(blocks):
                wu_copy(b).wait()
                wd_copy(b).wait()

        def up(i, b, u):
            u[...] = dot(alow[halves[i], :], wu[b])

        def activate(i, b, u):
            pre = u[...] + upb_ref[b]
            square = pre * pre
            level_half = 0.5 * jnp.tanh(pre * (TANH_IN + TANH_CUBE * square)) + 0.5
            value = pre * level_half
            slope = level_half + value * (1.0 - level_half) * (2.0 * TANH_IN + 6.0 * TANH_CUBE * square)
            hst[b, halves[i], :] = value.astype(BF)
            deriv[k, b, halves[i], :] = slope.astype(BF)
            if i == 1:
                h_copy(k, b).start()

        def down(i, b):
            acc[halves[i], :] += dot(hst[b, halves[i], :], wd[b])

        def before(i):
            pass

        def after(i):
            for part in tiles[i]:
                unit, scale = normalized(acc[part, :])
                xh2[k, part, :] = unit.astype(BF)
                rstd[k, part, 1:2] = scale
                value = unit * g2 + b2
                rounded = value.astype(BF)
                yst[part, :] = rounded
                sendbuf[k, part, :] = rounded

            if i == 0:

                @pl.when(jnp.logical_and(first, core + k > 0))
                def _():
                    pl.semaphore_wait(turn_sem, 1)

            @pl.when(first)
            def _():
                leave(k, i)

            if i == 1:

                @pl.when(jnp.logical_and(first, k + core < count))
                def _():
                    for c in range(CHUNKS):
                        chunk_copy(k, c).wait_send()
                    pl.semaphore_signal(
                        turn_sem, inc=1, device_id={"dp": sibling}, device_id_type=pl.DeviceIdType.MESH
                    )

        pipelined(up, activate, down, before, after)
        a_copy(k).start()
        act_copy(k).start()

    def backward(k):
        length = bucket[k]
        level = jnp.where(length == rows, 2, jnp.where(length * 2 == rows, 1, 0))

        @pl.when(jnp.logical_and(k == 0, jnp.logical_not(first)))
        def _():
            cot_copy.wait()

        @pl.when(jnp.logical_and(first, k + core == count))
        def _():
            for c in range(CHUNKS):
                chunk_copy(k, c).wait_send()

        @pl.when(k > 0)
        def _():
            df_copy(k).wait()
            grad_copy(k).wait()

        for b in range(blocks):
            du_copy(k, b).wait()

        def before(i):
            @pl.when(first)
            def _():
                arrived(k, i)

            for part in tiles[i]:
                grad = jnp.where(first, recv[k, part, :], inbuf[k, part, :]).astype(F32)
                unit = xh2[k, part, :].astype(F32)
                back = norm_back(grad, g2, unit, rstd[k, part, 1:2])
                rounded = back.astype(BF)
                dlow[part, :] = rounded
                acc[part, :] = back
                sums[2] += fold8(grad * unit)
                sums[3] += fold8(grad)
                sums[4] += fold8(rounded.astype(F32))

        def up(i, b, u):
            u[...] = dot_t(dlow[halves[i], :], wd[b])

        def activate(i, b, u):
            rounded = (u[...] * deriv[k, b, halves[i], :].astype(F32)).astype(BF)
            hst[b, halves[i], :] = rounded
            sums[5 + b] += fold8(rounded.astype(F32))
            if i == 1:
                du_copy(k, b).start()

        def down(i, b):
            acc[halves[i], :] += dot_t(hst[b, halves[i], :], wu[b])

        def after(i):
            for part in tiles[i]:
                grad = acc[part, :]
                unit = xh1[k, part, :].astype(F32)
                back = norm_back(grad, g1, unit, rstd[k, part, 0:1])
                acc[part, :] = back
                recv[k, part, :] = back.astype(BF)
                sums[0] += fold8(grad * unit)
                sums[1] += fold8(grad)

        pipelined(up, activate, down, before, after)
        pq[0] = dot(stab[level, 0], recv[k]).astype(BF)
        pq[1] = dot(stab[level, 1], recv[k]).astype(BF)

        for i, part in enumerate(halves):
            value = acc[part, :] + dot(pq[0, part, :], htab[0]) + dot(pq[1, part, :], htab[1])
            rounded = value.astype(BF)
            xst[part, :] = rounded
            sendbuf[k, part, :] = rounded

            @pl.when(jnp.logical_not(first))
            def _():
                leave(k, i)

        df_copy(k).start()
        grad_copy(k).start()

    def one(step, carry):
        forwards = jnp.where(first, step < count, lax.rem(step, 2) == 0)
        k = jnp.where(first, lax.rem(step, count), step // 2)

        @pl.when(forwards)
        def _():
            forward(k, False)

        @pl.when(jnp.logical_not(forwards))
        def _():
            backward(k)

        return carry

    forward(0, True)
    lax.fori_loop(1, 2 * count, one, 0)

    end = count - 1

    for n in range(5 + blocks):
        small_ref[n : n + 1, :] = jnp.sum(sums[n], axis=0, keepdims=True)
    for n in range(5 + blocks, small_ref.shape[0]):
        small_ref[n : n + 1, :] = jnp.zeros((1, width), F32)
    act_copy(end).wait()
    grad_copy(end).wait()
    a_copy(end).wait()
    df_copy(end).wait()
    for b in range(blocks):
        du_copy(end, b).wait()

    @pl.when(jnp.logical_not(first))
    def _():
        for k in range(count):
            for c in range(CHUNKS):
                chunk_copy(k, c).wait_send()


def run_layers(bucket, plan, norms, up_bias, inputs, cotangent, up_weight, down_weight):
    count, rows, width = inputs.shape
    hidden = up_weight.shape[-1]
    fb = width
    blocks = hidden // fb
    htab = jnp.asarray(hidden_tables(width))
    stab = jnp.asarray(seq_tables(rows))
    any_spec = pl.BlockSpec(memory_space=pl.ANY)
    smem = pl.BlockSpec(memory_space=pltpu.SMEM)
    vmem = pl.BlockSpec(memory_space=pltpu.VMEM)
    shape = jax.ShapeDtypeStruct
    body = functools.partial(layers_kernel, count, rows, width, blocks, fb)
    flops = count * (12 * rows * width * hidden // 1 + 4 * rows * width * (2 * width + 2 * rows))
    return pl.pallas_call(
        body,
        out_shape=(
            shape((1, count, rows, width), BF),
            shape((1, count, rows, width), BF),
            shape((blocks, count, rows, fb), BF),
            shape((blocks, count, rows, fb), BF),
            shape((count, rows, width), BF),
            shape((count, rows, width), BF),
            shape((16, width), F32),
        ),
        in_specs=[smem, smem] + [vmem] * 6 + [any_spec] * 6,
        out_specs=(any_spec,) * 6 + (vmem,),
        scratch_shapes=[
            pltpu.VMEM((blocks, width, fb), BF),
            pltpu.VMEM((blocks, fb, width), BF),
            pltpu.VMEM((2, width, width), BF),
            pltpu.VMEM((3, 2, rows, rows), BF),
            pltpu.VMEM((count, rows, width), BF),
            pltpu.VMEM((count, rows, width), BF),
            pltpu.VMEM((count, rows, width), BF),
            pltpu.VMEM((count, blocks, rows, fb), BF),
            pltpu.VMEM((count, rows, width), BF),
            pltpu.VMEM((count, rows, width), BF),
            pltpu.VMEM((count, rows, 128), F32),
            pltpu.VMEM((blocks, rows, fb), BF),
            pltpu.VMEM((2, rows, width), BF),
            pltpu.VMEM((rows // 2, fb), F32),
            pltpu.VMEM((rows // 2, fb), F32),
            pltpu.VMEM((rows, width), F32),
            pltpu.VMEM((rows, width), BF),
            pltpu.VMEM((rows, width), BF),
            pltpu.VMEM((rows, width), BF),
            pltpu.VMEM((rows, width), BF),
            pltpu.VMEM((5 + blocks, 8, width), F32),
            pltpu.SemaphoreType.DMA((2 * blocks,)),
            pltpu.SemaphoreType.DMA((3,)),
            pltpu.SemaphoreType.DMA((4,)),
            pltpu.SemaphoreType.DMA((blocks,)),
            pltpu.SemaphoreType.DMA((count, CHUNKS)),
            pltpu.SemaphoreType.DMA((count, CHUNKS)),
            pltpu.SemaphoreType.REGULAR,
        ],
        compiler_params=pltpu.CompilerParams(
            collective_id=0, has_side_effects=True, vmem_limit_bytes=63 * 2**20
        ),
        cost_estimate=pl.CostEstimate(flops=flops, bytes_accessed=60 * 2**20, transcendentals=0),
    )(bucket, plan, *norms, up_bias, inputs, cotangent, up_weight, down_weight, htab, stab)


KINDS = 13
C1, Y1, CHY, INY, RY, Y2, CHZ, INZ, YZ, RZH, RZF, SY, SZ = range(KINDS)
RING = 4
LAGS = (1, 3, 5, 7, 9, 11, 12)


def grads_kernel(
    dp, count, rows, width, units, wide, per_block,
    a_hbm, df_hbm, h_hbm, du_hbm, small_ref,
    down_hbm, up_hbm, small_out,
    at, abuf, dfb, xb, prod, cur, res, stage, c1in, y1in, chy, iny, chz, inz, yz, sm, smin,
    in_sem, x_sem, out_sem, send_sem, recv_sem, sm_send, sm_recv,
):
    me = lax.axis_index("dp")
    n = dp // 4
    core = me % 2
    side = (me // 2) % 2
    z = me // 4
    low = z < n // 2
    inner = jnp.logical_or(z == n // 2 - 1, z == n // 2)
    outer = jnp.logical_not(inner)
    has_out = jnp.logical_and(z > 0, z < n - 1)
    edge = jnp.logical_not(has_out)
    toward = jnp.where(low, 4, -4)
    inward = me + toward
    outward = me - toward
    sibling = me + 1 - 2 * core
    across = me + 2 - 4 * side
    keep = jnp.where(low, 0, 1)
    half = units // 2
    steps = dp.bit_length() - 1
    home = core * 4

    def x_start(u):
        slot = u % 3
        j = u % half
        block = j // per_block
        part = pl.ds(pl.multiple_of((j % per_block) * wide, wide), wide)

        @pl.when(u < half)
        def _():
            pltpu.make_async_copy(h_hbm.at[block, :, :, part], xb.at[slot], x_sem.at[slot]).start()

        @pl.when(u >= half)
        def _():
            pltpu.make_async_copy(du_hbm.at[block, :, :, part], xb.at[slot], x_sem.at[slot]).start()

    def x_wait(u):
        slot = u % 3
        pltpu.make_async_copy(h_hbm.at[0, :, :, pl.ds(0, wide)], xb.at[slot], x_sem.at[slot]).wait()

    df_copy = pltpu.make_async_copy(df_hbm, dfb, in_sem.at[0])
    a_copy = pltpu.make_async_copy(a_hbm, abuf, in_sem.at[1])
    df_copy.start()
    x_start(0)
    x_start(1)
    a_copy.start()

    def partner(s):
        return me + 2**s - 2 ** (s + 1) * ((me // 2**s) % 2)

    barrier = pltpu.get_barrier_semaphore()
    for s in range(steps):
        pl.semaphore_signal(barrier, inc=1, device_id={"dp": partner(s)}, device_id_type=pl.DeviceIdType.MESH)
    pl.semaphore_signal(barrier, inc=1, device_id={"dp": inward}, device_id_type=pl.DeviceIdType.MESH)

    @pl.when(has_out)
    def _():
        pl.semaphore_signal(barrier, inc=1, device_id={"dp": outward}, device_id_type=pl.DeviceIdType.MESH)

    def small_copy(s):
        return pltpu.make_async_remote_copy(
            src_ref=sm.at[s], dst_ref=smin.at[s], send_sem=sm_send.at[s], recv_sem=sm_recv.at[s],
            device_id={"dp": partner(s)}, device_id_type=pl.DeviceIdType.MESH,
        )

    def message(kind, u, src, dst, target):
        return pltpu.make_async_remote_copy(
            src_ref=src, dst_ref=dst, send_sem=send_sem.at[kind, u % RING], recv_sem=recv_sem.at[kind, u],
            device_id={"dp": target}, device_id_type=pl.DeviceIdType.MESH,
        )

    def c1(u):
        return message(C1, u, prod.at[u % RING, pl.ds(4 - home, 4)], c1in.at[u], sibling)

    def y1(u):
        return message(Y1, u, cur.at[u, 1 - side], y1in.at[u], across)

    def ch_y(u):
        return message(CHY, u, cur.at[u, side], chy.at[u], inward)

    def in_y(u):
        return message(INY, u, cur.at[u, side], iny.at[u], inward)

    def r_y(u):
        return message(RY, u, res.at[u, home + side], res.at[u, home + side], outward)

    def y2(u):
        return message(Y2, u, res.at[u, home + side], res.at[u, home + side], across)

    def ch_z(u):
        return message(CHZ, u, cur.at[u, pl.ds(2, 2)], chz.at[u], inward)

    def in_z(u):
        return message(INZ, u, cur.at[u, 3 - keep], inz.at[u], inward)

    def y_z(u):
        return message(YZ, u, cur.at[u, 2 + keep], yz.at[u], across)

    def r_zh(u):
        return message(RZH, u, res.at[u, home + 2 + keep], res.at[u, home + 2 + keep], inward)

    def r_zf(u):
        return message(RZF, u, res.at[u, pl.ds(home + 2, 2)], res.at[u, pl.ds(home + 2, 2)], outward)

    def s_y(u):
        return message(SY, u, res.at[u, pl.ds(home, 2)], res.at[u, pl.ds(home, 2)], sibling)

    def s_z(u):
        return message(SZ, u, res.at[u, pl.ds(home + 2, 2)], res.at[u, pl.ds(home + 2, 2)], sibling)

    def down_copy(u, t):
        part = pl.ds(pl.multiple_of(u * wide, wide), wide)
        return pltpu.make_async_copy(
            stage.at[u % 2, pl.ds(t * wide, wide)], down_hbm.at[0, part, pl.ds(t * wide, wide)],
            out_sem.at[u % 2, t],
        )

    def up_copy(u, t, slot):
        part = pl.ds(pl.multiple_of((u - half) * wide, wide), wide)
        return pltpu.make_async_copy(
            stage.at[slot, pl.ds(t * wide, wide)], up_hbm.at[0, pl.ds(t * wide, wide), part],
            out_sem.at[slot, t],
        )

    def send(make, u):
        @pl.when(u >= RING)
        def _():
            make(u - RING).wait_send()

        make(u).start()

    def plus(left, right):
        return (left.astype(F32) + right.astype(F32)).astype(BF)

    def product(u):
        slot = u % RING
        block = xb.at[u % 3]

        @pl.when(u < half)
        def _():
            value = lax.dot_general(
                block[...].reshape(count * rows, wide), dfb[...].reshape(count * rows, width),
                (((0,), (0,)), ((), ())), preferred_element_type=F32,
            )
            value = jnp.concatenate([value[:, t : t + wide] for t in range(0, width, wide)], axis=0)
            prod[slot] = value.astype(BF).reshape(8, width // 8, wide)

        @pl.when(u >= half)
        def _():
            value = dot(at[...], block[...].reshape(count * rows, wide))
            prod[slot] = value.astype(BF).reshape(8, width // 8, wide)

    def compute(u):
        x_wait(u)

        @pl.when(u + 2 < units)
        def _():
            x_start(u + 2)

        @pl.when(u >= RING)
        def _():
            c1(u - RING).wait_send()

        @pl.when(u == 1)
        def _():
            a_copy.wait()

        for k in range(count):

            @pl.when(u == 2 * k + 2)
            def _():
                at[:, k * rows : (k + 1) * rows] = abuf[k].T

        product(u)
        c1(u).start()

    def stage1(u):
        c1(u).wait_recv()
        cur[u] = plus(prod[u % RING, pl.ds(home, 4)], c1in[u])
        send(y1, u)

        @pl.when(edge)
        def _():
            send(ch_z, u)

    def stage2(u):
        y1(u).wait_recv()
        cur[u, side] = plus(cur[u, side], y1in[u])

        @pl.when(edge)
        def _():
            send(ch_y, u)

        @pl.when(has_out)
        def _():
            ch_z(u).wait_recv()
            cur[u, 2:4] = plus(cur[u, 2:4], chz[u])

        @pl.when(inner)
        def _():
            send(in_z, u)

        @pl.when(jnp.logical_and(outer, has_out))
        def _():
            send(ch_z, u)

    def stage3(u):
        @pl.when(has_out)
        def _():
            ch_y(u).wait_recv()
            cur[u, side] = plus(cur[u, side], chy[u])

        @pl.when(inner)
        def _():
            send(in_y, u)
            in_z(u).wait_recv()
            cur[u, 2 + keep] = plus(cur[u, 2 + keep], inz[u])
            send(y_z, u)

        @pl.when(jnp.logical_and(outer, has_out))
        def _():
            send(ch_y, u)

    def stage4(u):
        @pl.when(inner)
        def _():
            in_y(u).wait_recv()
            res[u, home + side] = plus(cur[u, side], iny[u])
            send(r_y, u)
            send(y2, u)
            y_z(u).wait_recv()
            res[u, home + 2 + keep] = plus(cur[u, 2 + keep], yz[u])
            send(r_zh, u)

    def stage5(u):
        @pl.when(outer)
        def _():
            r_y(u).wait_recv()

            @pl.when(has_out)
            def _():
                send(r_y, u)

            send(y2, u)

        @pl.when(inner)
        def _():
            message(
                RZH, u, res.at[u, home + 3 - keep], res.at[u, home + 3 - keep], inward
            ).wait_recv()
            send(r_zf, u)
            send(s_z, u)

    def stage6(u):
        message(Y2, u, res.at[u, home + 1 - side], res.at[u, home + 1 - side], across).wait_recv()
        send(s_y, u)

        @pl.when(outer)
        def _():
            r_zf(u).wait_recv()

            @pl.when(has_out)
            def _():
                send(r_zf, u)

            send(s_z, u)

    def stage7(u):
        away = 4 - home
        message(SY, u, res.at[u, pl.ds(away, 2)], res.at[u, pl.ds(away, 2)], sibling).wait_recv()
        message(SZ, u, res.at[u, pl.ds(away + 2, 2)], res.at[u, pl.ds(away + 2, 2)], sibling).wait_recv()

        @pl.when(u >= 2)
        def _():
            for t in range(width // wide):
                up_copy(half, t, u % 2).wait()

        stage[u % 2] = res[u].reshape(width, wide)

        @pl.when(u < half)
        def _():
            for t in range(width // wide):
                down_copy(u, t).start()

        @pl.when(u >= half)
        def _():
            for t in range(width // wide):
                up_copy(u, t, u % 2).start()

    stages = (stage1, stage2, stage3, stage4, stage5, stage6, stage7)

    def one(i, carry):
        @pl.when(jnp.logical_and(i > 0, i < units))
        def _():
            compute(i)

        for work, lag in reversed(list(zip(stages, LAGS))):
            u = i - lag

            @pl.when(jnp.logical_and(u >= 0, u < units))
            def _():
                work(u)

        for s in range(steps):

            @pl.when(i == s + 1)
            def _():
                small_copy(s).wait_recv()
                sm[s + 1] = sm[s] + smin[s]
                if s + 1 < steps:
                    small_copy(s + 1).start()

        return carry

    df_copy.wait()
    x_wait(0)
    x_start(2)
    product(0)
    sm[0] = small_ref[...]

    @pl.when(has_out)
    def _():
        pl.semaphore_wait(barrier, steps + 2)

    @pl.when(edge)
    def _():
        pl.semaphore_wait(barrier, steps + 1)

    c1(0).start()
    small_copy(0).start()
    lax.fori_loop(0, units + LAGS[-1], one, 0)

    small_out[...] = sm[steps]
    for s in range(steps):
        small_copy(s).wait_send()

    def drain(u, carry):
        for make in (c1, y1, y2, s_y, s_z):
            make(u).wait_send()

        @pl.when(inner)
        def _():
            for make in (in_z, in_y, y_z, r_zh):
                make(u).wait_send()

        @pl.when(has_out)
        def _():
            for make in (r_y, r_zf):
                make(u).wait_send()

        @pl.when(outer)
        def _():
            for make in (ch_y, ch_z):
                make(u).wait_send()

        return carry

    lax.fori_loop(units - RING, units, drain, 0)
    for slot in range(2):
        for t in range(width // wide):
            up_copy(half, t, slot).wait()


def run_grads(dp, a, df, h, du, small):
    count, rows, width = a.shape
    blocks, fb = h.shape[0], h.shape[-1]
    wide = fb // 3
    half = blocks * 3
    units = 2 * half
    steps = dp.bit_length() - 1
    piece = width // 8
    hidden = blocks * fb
    any_spec = pl.BlockSpec(memory_space=pl.ANY)
    vmem = pl.BlockSpec(memory_space=pltpu.VMEM)
    shape = jax.ShapeDtypeStruct
    body = functools.partial(grads_kernel, dp, count, rows, width, units, wide, 3)
    return pl.pallas_call(
        body,
        out_shape=(shape((1, hidden, width), BF), shape((1, width, hidden), BF), shape(small.shape, F32)),
        in_specs=[any_spec] * 4 + [vmem],
        out_specs=(any_spec, any_spec, vmem),
        scratch_shapes=[
            pltpu.VMEM((width, count * rows), BF),
            pltpu.VMEM((count, rows, width), BF),
            pltpu.VMEM((count, rows, width), BF),
            pltpu.VMEM((3, count, rows, wide), BF),
            pltpu.VMEM((RING, 8, piece, wide), BF),
            pltpu.VMEM((units, 4, piece, wide), BF),
            pltpu.VMEM((units, 8, piece, wide), BF),
            pltpu.VMEM((2, width, wide), BF),
            pltpu.VMEM((units, 4, piece, wide), BF),
            pltpu.VMEM((units, piece, wide), BF),
            pltpu.VMEM((units, piece, wide), BF),
            pltpu.VMEM((units, piece, wide), BF),
            pltpu.VMEM((units, 2, piece, wide), BF),
            pltpu.VMEM((units, piece, wide), BF),
            pltpu.VMEM((units, piece, wide), BF),
            pltpu.VMEM((steps + 1,) + small.shape, F32),
            pltpu.VMEM((steps,) + small.shape, F32),
            pltpu.SemaphoreType.DMA((2,)),
            pltpu.SemaphoreType.DMA((3,)),
            pltpu.SemaphoreType.DMA((2, 3)),
            pltpu.SemaphoreType.DMA((KINDS, RING)),
            pltpu.SemaphoreType.DMA((KINDS, units)),
            pltpu.SemaphoreType.DMA((steps,)),
            pltpu.SemaphoreType.DMA((steps,)),
        ],
        compiler_params=pltpu.CompilerParams(
            collective_id=1, has_side_effects=True, vmem_limit_bytes=60 * 2**20
        ),
    )(a, df, h, du, small)


def widen_kernel(act, grad, down, up, small, act_out, grad_out, g1, b1, up_out, upb, down_out, bd, g2, b2):
    act_out[...] = act[...].astype(F32)
    grad_out[...] = grad[...].astype(F32)
    up_out[...] = up[...].astype(F32)
    down_out[...] = down[...].astype(F32)

    @pl.when(pl.program_id(0) == 0)
    def _():
        width = small.shape[-1]
        for n, out in enumerate((g1, b1, g2, b2, bd)):
            out[...] = small[n : n + 1, :]
        for b in range(upb.shape[-1] // width):
            upb[:, b * width : (b + 1) * width] = small[5 + b : 6 + b, :]


def run_widen(act, grad, down, up, small):
    count, rows, width = act.shape[1:]
    hidden = down.shape[1]
    grid = 4 * count
    token = pl.BlockSpec((1, 1, rows // 4, width), lambda i: (0, i // 4, i % 4, 0))
    tall = pl.BlockSpec((1, hidden // grid, width), lambda i: (0, i, 0))
    flat = pl.BlockSpec((1, width // grid, hidden), lambda i: (0, i, 0))

    def whole(*extent):
        return pl.BlockSpec(extent, lambda i: (0, 0))

    shape = jax.ShapeDtypeStruct
    row = shape((1, width), F32)
    line = whole(1, width)
    return pl.pallas_call(
        widen_kernel,
        grid=(grid,),
        in_specs=[token, token, tall, flat, whole(*small.shape)],
        out_specs=(token, token, line, line, flat, whole(1, hidden), tall, line, line, line),
        out_shape=(
            shape(act.shape, F32), shape(grad.shape, F32), row, row, shape(up.shape, F32),
            shape((1, hidden), F32), shape(down.shape, F32), row, row, row,
        ),
        compiler_params=pltpu.CompilerParams(
            dimension_semantics=("arbitrary",), vmem_limit_bytes=60 * 2**20
        ),
    )(act, grad, down, up, small)


def per_device(
    inputs, bucket, plan, cotangent, norm1_gain, norm1_bias, up_weight, up_bias,
    down_weight, down_bias, norm2_gain, norm2_bias,
):
    count, rows, width = inputs.shape
    hidden = up_weight.shape[-1]
    norms = (norm1_gain, norm1_bias, norm2_gain, norm2_bias, down_bias)
    activations, input_grad, h, du, a, df, small = run_layers(
        bucket, plan, norms, up_bias.reshape(-1, 1, width), inputs, cotangent, up_weight, down_weight
    )
    down_grad, up_grad, small = run_grads(lax.axis_size("dp"), a, df, h, du, small)
    return run_widen(activations, input_grad, down_grad, up_grad, small)


def solution(mesh):
    row = P("pipe", None)
    weight = P("pipe", None, None)
    tokens = P(None, "dp", None)
    result = P("pipe", None, "dp", None)
    return jax.shard_map(
        per_device,
        mesh=mesh,
        in_specs=(tokens, P(), P(), tokens, row, row, weight, row, weight, row, row, row),
        out_specs=(result, result, row, row, weight, row, weight, row, row, row),
        check_vma=False,
    )
```

```python
import functools
import math

import jax
import jax.numpy as jnp
import ml_dtypes
import numpy as np
from jax import lax
from jax.experimental import pallas as pl
from jax.experimental.pallas import tpu as pltpu
from jax.sharding import PartitionSpec as P

BF = jnp.bfloat16
F32 = jnp.float32
TANH_IN = math.sqrt(2.0 / math.pi)
TANH_CUBE = TANH_IN * 0.044715
EPS = 1e-6
CHUNKS = 4


def hidden_tables(width):
    position = np.arange(width)
    angle = 2.0 * np.pi * (np.outer(position, position) % width) / width
    pair = np.stack([np.cos(angle), np.sin(angle)]) / np.sqrt(width)
    return pair.astype(ml_dtypes.bfloat16)


def seq_tables(rows):
    position = np.arange(rows)
    found = []
    for length in (rows // 4, rows // 2, rows):
        same = position[:, None] // length == position[None, :] // length
        phase = (position[:, None] % length) * (position[None, :] % length) % length
        angle = 2.0 * np.pi * phase / length
        found.append(
            np.stack(
                [
                    np.where(same, np.cos(angle), 0.0) / np.sqrt(length),
                    np.where(same, -np.sin(angle), 0.0) / np.sqrt(length),
                ]
            )
        )
    return np.stack(found).astype(ml_dtypes.bfloat16)


def dot(left, right):
    return jnp.dot(left, right, preferred_element_type=F32)


def dot_t(left, right):
    return lax.dot_general(left, right, (((1,), (1,)), ((), ())), preferred_element_type=F32)


def fold8(values):
    return jnp.sum(values.reshape(-1, 8, values.shape[-1]), axis=0)


def layers_kernel(
    count, rows, width, blocks, fb,
    bucket, plan, g1_ref, b1_ref, g2_ref, b2_ref, bd_ref, upb_ref, in_hbm, cot_hbm, wu_hbm, wd_hbm, htab_hbm, stab_hbm,
    act_hbm, grad_hbm, h_hbm, du_hbm, a_hbm, df_hbm, small_ref,
    wu, wd, htab, stab, inbuf, recv, sendbuf, deriv, xh1, xh2, rstd,
    hst, pq, u0, u1, acc, alow, dlow, yst, xst, sums,
    w_sem, t_sem, o_sem, h_sem, send_sem, recv_sem, turn_sem,
):
    first = lax.axis_index("pipe") == 0
    partner = 1 - lax.axis_index("pipe")
    core = lax.axis_index("dp") % 2
    sibling = lax.axis_index("dp") + 1 - 2 * core
    last = blocks - 1

    def wu_copy(b):
        return pltpu.make_async_copy(wu_hbm.at[0, :, pl.ds(b * fb, fb)], wu.at[b], w_sem.at[b])

    def wd_copy(b):
        return pltpu.make_async_copy(wd_hbm.at[0, pl.ds(b * fb, fb), :], wd.at[b], w_sem.at[blocks + b])

    in_copy = pltpu.make_async_copy(in_hbm, inbuf, t_sem.at[0])
    cot_copy = pltpu.make_async_copy(cot_hbm, inbuf, t_sem.at[0])
    htab_copy = pltpu.make_async_copy(htab_hbm, htab, t_sem.at[1])
    stab_copy = pltpu.make_async_copy(stab_hbm, stab, t_sem.at[2])

    def start_weights():
        for b in range(blocks):
            wu_copy(b).start()
            wd_copy(b).start()

    @pl.when(first)
    def _():
        in_copy.start()

    htab_copy.start()
    stab_copy.start()

    @pl.when(jnp.logical_not(first))
    def _():
        start_weights()
        cot_copy.start()

    sums[...] = jnp.zeros_like(sums)

    barrier = pltpu.get_barrier_semaphore()
    pl.semaphore_signal(barrier, inc=1, device_id={"pipe": partner}, device_id_type=pl.DeviceIdType.MESH)
    pl.semaphore_signal(barrier, inc=1, device_id={"dp": sibling}, device_id_type=pl.DeviceIdType.MESH)
    pl.semaphore_wait(barrier, 2)

    span = rows // CHUNKS

    def chunk_copy(k, c):
        part = pl.ds(c * span, span)
        return pltpu.make_async_remote_copy(
            src_ref=sendbuf.at[k, part],
            dst_ref=recv.at[k, part],
            send_sem=send_sem.at[k, c],
            recv_sem=recv_sem.at[k, c],
            device_id={"pipe": partner},
            device_id_type=pl.DeviceIdType.MESH,
        )

    def act_copy(k):
        return pltpu.make_async_copy(yst, act_hbm.at[0, k], o_sem.at[0])

    def grad_copy(k):
        return pltpu.make_async_copy(xst, grad_hbm.at[0, k], o_sem.at[1])

    def a_copy(k):
        return pltpu.make_async_copy(alow, a_hbm.at[k], o_sem.at[2])

    def df_copy(k):
        return pltpu.make_async_copy(dlow, df_hbm.at[k], o_sem.at[3])

    def h_copy(k, b):
        return pltpu.make_async_copy(hst.at[b], h_hbm.at[b, k], h_sem.at[b])

    def du_copy(k, b):
        return pltpu.make_async_copy(hst.at[b], du_hbm.at[b, k], h_sem.at[b])

    def arrived(k, i):
        for c in range(i * CHUNKS // 2, (i + 1) * CHUNKS // 2):
            chunk_copy(k, c).wait_recv()

    def leave(k, i):
        for c in range(i * CHUNKS // 2, (i + 1) * CHUNKS // 2):
            chunk_copy(k, c).start()

    half = rows // 2
    halves = (slice(0, half), slice(half, rows))
    tiles = [[slice(r, r + span) for r in range(h.start, h.stop, span)] for h in halves]
    order = [(i, b) for i in range(2) for b in range(blocks)]
    buffers = (u0, u1)
    g1, b1, g2, b2, bd = (ref[...] for ref in (g1_ref, b1_ref, g2_ref, b2_ref, bd_ref))

    def normalized(values):
        centered = values - jnp.mean(values, axis=-1, keepdims=True)
        scale = lax.rsqrt(jnp.mean(centered * centered, axis=-1, keepdims=True) + EPS)
        return centered * scale, scale

    def norm_back(grad, gain, unit, scale):
        scaled = grad * gain
        mean_one = jnp.mean(scaled, axis=-1, keepdims=True)
        mean_two = jnp.mean(scaled * unit, axis=-1, keepdims=True)
        return scale * (scaled - mean_one - unit * mean_two)

    def pipelined(up, activate, down, before, after):
        before(0)
        up(*order[0], u0)
        for n, (i, b) in enumerate(order):
            if n + 1 < len(order):
                if order[n + 1][1] == 0:
                    before(order[n + 1][0])
                up(*order[n + 1], buffers[(n + 1) % 2])
            if n > 0:
                down(*order[n - 1])
            activate(i, b, buffers[n % 2])
            if n > 0 and order[n - 1][1] == last:
                after(order[n - 1][0])
        down(*order[-1])
        after(1)

    def forward(k, opening):
        source = plan[k]
        length = bucket[k]
        level = jnp.where(length == rows, 2, jnp.where(length * 2 == rows, 1, 0))

        if opening:
            htab_copy.wait()

            @pl.when(first)
            def _():
                in_copy.wait()
                start_weights()

        @pl.when(first)
        def _():
            recv[k] = inbuf[source]

        for i, part in enumerate(halves):

            @pl.when(jnp.logical_not(first))
            def _():
                arrived(k, i)

            pq[0, part] = dot(recv[k, part], htab[0]).astype(BF)
            pq[1, part] = dot(recv[k, part], htab[1]).astype(BF)

        if opening:
            stab_copy.wait()
        else:
            for b in range(blocks):
                h_copy(k, b).wait()
            a_copy(k).wait()
            act_copy(k).wait()

        for part in halves:
            mixed = dot(stab[level, 0, part, :], pq[0]) + dot(stab[level, 1, part, :], pq[1])
            unit, scale = normalized(recv[k, part, :].astype(F32) + mixed)
            xh1[k, part, :] = unit.astype(BF)
            rstd[k, part, 0:1] = scale
            value = unit * g1 + b1
            alow[part, :] = value.astype(BF)
            acc[part, :] = value + bd
        if opening:
            for b in range(blocks):
                wu_copy(b).wait()
                wd_copy(b).wait()

        def up(i, b, u):
            u[...] = dot(alow[halves[i], :], wu[b])

        def activate(i, b, u):
            pre = u[...] + upb_ref[b]
            square = pre * pre
            level_half = 0.5 * jnp.tanh(pre * (TANH_IN + TANH_CUBE * square)) + 0.5
            value = pre * level_half
            slope = level_half + value * (1.0 - level_half) * (2.0 * TANH_IN + 6.0 * TANH_CUBE * square)
            hst[b, halves[i], :] = value.astype(BF)
            deriv[k, b, halves[i], :] = slope.astype(BF)
            if i == 1:
                h_copy(k, b).start()

        def down(i, b):
            acc[halves[i], :] += dot(hst[b, halves[i], :], wd[b])

        def before(i):
            pass

        def after(i):
            for part in tiles[i]:
                unit, scale = normalized(acc[part, :])
                xh2[k, part, :] = unit.astype(BF)
                rstd[k, part, 1:2] = scale
                value = unit * g2 + b2
                rounded = value.astype(BF)
                yst[part, :] = rounded
                sendbuf[k, part, :] = rounded

            if i == 0:

                @pl.when(jnp.logical_and(first, core + k > 0))
                def _():
                    pl.semaphore_wait(turn_sem, 1)

            @pl.when(first)
            def _():
                leave(k, i)

            if i == 1:

                @pl.when(jnp.logical_and(first, k + core < count))
                def _():
                    for c in range(CHUNKS):
                        chunk_copy(k, c).wait_send()
                    pl.semaphore_signal(
                        turn_sem, inc=1, device_id={"dp": sibling}, device_id_type=pl.DeviceIdType.MESH
                    )

        pipelined(up, activate, down, before, after)
        a_copy(k).start()
        act_copy(k).start()

    def backward(k):
        length = bucket[k]
        level = jnp.where(length == rows, 2, jnp.where(length * 2 == rows, 1, 0))

        @pl.when(jnp.logical_and(k == 0, jnp.logical_not(first)))
        def _():
            cot_copy.wait()

        @pl.when(jnp.logical_and(first, k + core == count))
        def _():
            for c in range(CHUNKS):
                chunk_copy(k, c).wait_send()

        @pl.when(k > 0)
        def _():
            df_copy(k).wait()
            grad_copy(k).wait()

        for b in range(blocks):
            du_copy(k, b).wait()

        def before(i):
            @pl.when(first)
            def _():
                arrived(k, i)

            for part in tiles[i]:
                grad = jnp.where(first, recv[k, part, :], inbuf[k, part, :]).astype(F32)
                unit = xh2[k, part, :].astype(F32)
                back = norm_back(grad, g2, unit, rstd[k, part, 1:2])
                rounded = back.astype(BF)
                dlow[part, :] = rounded
                acc[part, :] = back
                sums[2] += fold8(grad * unit)
                sums[3] += fold8(grad)
                sums[4] += fold8(rounded.astype(F32))

        def up(i, b, u):
            u[...] = dot_t(dlow[halves[i], :], wd[b])

        def activate(i, b, u):
            rounded = (u[...] * deriv[k, b, halves[i], :].astype(F32)).astype(BF)
            hst[b, halves[i], :] = rounded
            sums[5 + b] += fold8(rounded.astype(F32))
            if i == 1:
                du_copy(k, b).start()

        def down(i, b):
            acc[halves[i], :] += dot_t(hst[b, halves[i], :], wu[b])

        def after(i):
            for part in tiles[i]:
                grad = acc[part, :]
                unit = xh1[k, part, :].astype(F32)
                back = norm_back(grad, g1, unit, rstd[k, part, 0:1])
                acc[part, :] = back
                recv[k, part, :] = back.astype(BF)
                sums[0] += fold8(grad * unit)
                sums[1] += fold8(grad)

        pipelined(up, activate, down, before, after)
        pq[0] = dot(stab[level, 0], recv[k]).astype(BF)
        pq[1] = dot(stab[level, 1], recv[k]).astype(BF)

        for i, part in enumerate(halves):
            value = acc[part, :] + dot(pq[0, part, :], htab[0]) + dot(pq[1, part, :], htab[1])
            rounded = value.astype(BF)
            xst[part, :] = rounded
            sendbuf[k, part, :] = rounded

            @pl.when(jnp.logical_not(first))
            def _():
                leave(k, i)

        df_copy(k).start()
        grad_copy(k).start()

    def one(step, carry):
        forwards = jnp.where(first, step < count, lax.rem(step, 2) == 0)
        k = jnp.where(first, lax.rem(step, count), step // 2)

        @pl.when(forwards)
        def _():
            forward(k, False)

        @pl.when(jnp.logical_not(forwards))
        def _():
            backward(k)

        return carry

    forward(0, True)
    lax.fori_loop(1, 2 * count, one, 0)

    end = count - 1

    for n in range(5 + blocks):
        small_ref[n : n + 1, :] = jnp.sum(sums[n], axis=0, keepdims=True)
    for n in range(5 + blocks, small_ref.shape[0]):
        small_ref[n : n + 1, :] = jnp.zeros((1, width), F32)
    act_copy(end).wait()
    grad_copy(end).wait()
    a_copy(end).wait()
    df_copy(end).wait()
    for b in range(blocks):
        du_copy(end, b).wait()

    @pl.when(jnp.logical_not(first))
    def _():
        for k in range(count):
            for c in range(CHUNKS):
                chunk_copy(k, c).wait_send()


def run_layers(bucket, plan, norms, up_bias, inputs, cotangent, up_weight, down_weight):
    count, rows, width = inputs.shape
    hidden = up_weight.shape[-1]
    fb = width
    blocks = hidden // fb
    htab = jnp.asarray(hidden_tables(width))
    stab = jnp.asarray(seq_tables(rows))
    any_spec = pl.BlockSpec(memory_space=pl.ANY)
    smem = pl.BlockSpec(memory_space=pltpu.SMEM)
    vmem = pl.BlockSpec(memory_space=pltpu.VMEM)
    shape = jax.ShapeDtypeStruct
    body = functools.partial(layers_kernel, count, rows, width, blocks, fb)
    flops = count * (12 * rows * width * hidden // 1 + 4 * rows * width * (2 * width + 2 * rows))
    return pl.pallas_call(
        body,
        out_shape=(
            shape((1, count, rows, width), BF),
            shape((1, count, rows, width), BF),
            shape((blocks, count, rows, fb), BF),
            shape((blocks, count, rows, fb), BF),
            shape((count, rows, width), BF),
            shape((count, rows, width), BF),
            shape((16, width), F32),
        ),
        in_specs=[smem, smem] + [vmem] * 6 + [any_spec] * 6,
        out_specs=(any_spec,) * 6 + (vmem,),
        scratch_shapes=[
            pltpu.VMEM((blocks, width, fb), BF),
            pltpu.VMEM((blocks, fb, width), BF),
            pltpu.VMEM((2, width, width), BF),
            pltpu.VMEM((3, 2, rows, rows), BF),
            pltpu.VMEM((count, rows, width), BF),
            pltpu.VMEM((count, rows, width), BF),
            pltpu.VMEM((count, rows, width), BF),
            pltpu.VMEM((count, blocks, rows, fb), BF),
            pltpu.VMEM((count, rows, width), BF),
            pltpu.VMEM((count, rows, width), BF),
            pltpu.VMEM((count, rows, 128), F32),
            pltpu.VMEM((blocks, rows, fb), BF),
            pltpu.VMEM((2, rows, width), BF),
            pltpu.VMEM((rows // 2, fb), F32),
            pltpu.VMEM((rows // 2, fb), F32),
            pltpu.VMEM((rows, width), F32),
            pltpu.VMEM((rows, width), BF),
            pltpu.VMEM((rows, width), BF),
            pltpu.VMEM((rows, width), BF),
            pltpu.VMEM((rows, width), BF),
            pltpu.VMEM((5 + blocks, 8, width), F32),
            pltpu.SemaphoreType.DMA((2 * blocks,)),
            pltpu.SemaphoreType.DMA((3,)),
            pltpu.SemaphoreType.DMA((4,)),
            pltpu.SemaphoreType.DMA((blocks,)),
            pltpu.SemaphoreType.DMA((count, CHUNKS)),
            pltpu.SemaphoreType.DMA((count, CHUNKS)),
            pltpu.SemaphoreType.REGULAR,
        ],
        compiler_params=pltpu.CompilerParams(
            collective_id=0, has_side_effects=True, vmem_limit_bytes=63 * 2**20
        ),
        cost_estimate=pl.CostEstimate(flops=flops, bytes_accessed=60 * 2**20, transcendentals=0),
    )(bucket, plan, *norms, up_bias, inputs, cotangent, up_weight, down_weight, htab, stab)


KINDS = 13
C1, Y1, CHY, INY, RY, Y2, CHZ, INZ, YZ, RZH, RZF, SY, SZ = range(KINDS)
RING = 4
LAGS = (1, 3, 5, 7, 9, 11, 12)


def grads_kernel(
    dp, count, rows, width, units, wide, per_block,
    a_hbm, df_hbm, h_hbm, du_hbm, small_ref,
    down_hbm, up_hbm, small_out,
    at, abuf, dfb, xb, prod, cur, res, stage, c1in, y1in, chy, iny, chz, inz, yz, sm, smin,
    in_sem, x_sem, out_sem, send_sem, recv_sem, sm_send, sm_recv,
):
    me = lax.axis_index("dp")
    n = dp // 4
    core = me % 2
    side = (me // 2) % 2
    z = me // 4
    low = z < n // 2
    inner = jnp.logical_or(z == n // 2 - 1, z == n // 2)
    outer = jnp.logical_not(inner)
    has_out = jnp.logical_and(z > 0, z < n - 1)
    edge = jnp.logical_not(has_out)
    toward = jnp.where(low, 4, -4)
    inward = me + toward
    outward = me - toward
    sibling = me + 1 - 2 * core
    across = me + 2 - 4 * side
    keep = jnp.where(low, 0, 1)
    half = units // 2
    steps = dp.bit_length() - 1
    home = core * 4

    def x_start(u):
        slot = u % 3
        j = u % half
        block = j // per_block
        part = pl.ds(pl.multiple_of((j % per_block) * wide, wide), wide)

        @pl.when(u < half)
        def _():
            pltpu.make_async_copy(h_hbm.at[block, :, :, part], xb.at[slot], x_sem.at[slot]).start()

        @pl.when(u >= half)
        def _():
            pltpu.make_async_copy(du_hbm.at[block, :, :, part], xb.at[slot], x_sem.at[slot]).start()

    def x_wait(u):
        slot = u % 3
        pltpu.make_async_copy(h_hbm.at[0, :, :, pl.ds(0, wide)], xb.at[slot], x_sem.at[slot]).wait()

    df_copy = pltpu.make_async_copy(df_hbm, dfb, in_sem.at[0])
    a_copy = pltpu.make_async_copy(a_hbm, abuf, in_sem.at[1])
    df_copy.start()
    x_start(0)
    x_start(1)
    a_copy.start()

    def partner(s):
        return me + 2**s - 2 ** (s + 1) * ((me // 2**s) % 2)

    barrier = pltpu.get_barrier_semaphore()
    for s in range(steps):
        pl.semaphore_signal(barrier, inc=1, device_id={"dp": partner(s)}, device_id_type=pl.DeviceIdType.MESH)
    pl.semaphore_signal(barrier, inc=1, device_id={"dp": inward}, device_id_type=pl.DeviceIdType.MESH)

    @pl.when(has_out)
    def _():
        pl.semaphore_signal(barrier, inc=1, device_id={"dp": outward}, device_id_type=pl.DeviceIdType.MESH)

    def small_copy(s):
        return pltpu.make_async_remote_copy(
            src_ref=sm.at[s], dst_ref=smin.at[s], send_sem=sm_send.at[s], recv_sem=sm_recv.at[s],
            device_id={"dp": partner(s)}, device_id_type=pl.DeviceIdType.MESH,
        )

    def message(kind, u, src, dst, target):
        return pltpu.make_async_remote_copy(
            src_ref=src, dst_ref=dst, send_sem=send_sem.at[kind, u % RING], recv_sem=recv_sem.at[kind, u],
            device_id={"dp": target}, device_id_type=pl.DeviceIdType.MESH,
        )

    def c1(u):
        return message(C1, u, prod.at[u % RING, pl.ds(4 - home, 4)], c1in.at[u], sibling)

    def y1(u):
        return message(Y1, u, cur.at[u, 1 - side], y1in.at[u], across)

    def ch_y(u):
        return message(CHY, u, cur.at[u, side], chy.at[u], inward)

    def in_y(u):
        return message(INY, u, cur.at[u, side], iny.at[u], inward)

    def r_y(u):
        return message(RY, u, res.at[u, home + side], res.at[u, home + side], outward)

    def y2(u):
        return message(Y2, u, res.at[u, home + side], res.at[u, home + side], across)

    def ch_z(u):
        return message(CHZ, u, cur.at[u, pl.ds(2, 2)], chz.at[u], inward)

    def in_z(u):
        return message(INZ, u, cur.at[u, 3 - keep], inz.at[u], inward)

    def y_z(u):
        return message(YZ, u, cur.at[u, 2 + keep], yz.at[u], across)

    def r_zh(u):
        return message(RZH, u, res.at[u, home + 2 + keep], res.at[u, home + 2 + keep], inward)

    def r_zf(u):
        return message(RZF, u, res.at[u, pl.ds(home + 2, 2)], res.at[u, pl.ds(home + 2, 2)], outward)

    def s_y(u):
        return message(SY, u, res.at[u, pl.ds(home, 2)], res.at[u, pl.ds(home, 2)], sibling)

    def s_z(u):
        return message(SZ, u, res.at[u, pl.ds(home + 2, 2)], res.at[u, pl.ds(home + 2, 2)], sibling)

    def down_copy(u, t):
        part = pl.ds(pl.multiple_of(u * wide, wide), wide)
        return pltpu.make_async_copy(
            stage.at[u % 2, pl.ds(t * wide, wide)], down_hbm.at[0, part, pl.ds(t * wide, wide)],
            out_sem.at[u % 2, t],
        )

    def up_copy(u, t, slot):
        part = pl.ds(pl.multiple_of((u - half) * wide, wide), wide)
        return pltpu.make_async_copy(
            stage.at[slot, pl.ds(t * wide, wide)], up_hbm.at[0, pl.ds(t * wide, wide), part],
            out_sem.at[slot, t],
        )

    def send(make, u):
        @pl.when(u >= RING)
        def _():
            make(u - RING).wait_send()

        make(u).start()

    def plus(left, right):
        return (left.astype(F32) + right.astype(F32)).astype(BF)

    def product(u):
        slot = u % RING
        block = xb.at[u % 3]

        @pl.when(u < half)
        def _():
            value = lax.dot_general(
                block[...].reshape(count * rows, wide), dfb[...].reshape(count * rows, width),
                (((0,), (0,)), ((), ())), preferred_element_type=F32,
            )
            value = jnp.concatenate([value[:, t : t + wide] for t in range(0, width, wide)], axis=0)
            prod[slot] = value.astype(BF).reshape(8, width // 8, wide)

        @pl.when(u >= half)
        def _():
            value = dot(at[...], block[...].reshape(count * rows, wide))
            prod[slot] = value.astype(BF).reshape(8, width // 8, wide)

    def compute(u):
        x_wait(u)

        @pl.when(u + 2 < units)
        def _():
            x_start(u + 2)

        @pl.when(u >= RING)
        def _():
            c1(u - RING).wait_send()

        @pl.when(u == 1)
        def _():
            a_copy.wait()

        for k in range(count):

            @pl.when(u == 2 * k + 2)
            def _():
                at[:, k * rows : (k + 1) * rows] = abuf[k].T

        product(u)
        c1(u).start()

    def stage1(u):
        c1(u).wait_recv()
        cur[u] = plus(prod[u % RING, pl.ds(home, 4)], c1in[u])
        send(y1, u)

        @pl.when(edge)
        def _():
            send(ch_z, u)

    def stage2(u):
        y1(u).wait_recv()
        cur[u, side] = plus(cur[u, side], y1in[u])

        @pl.when(edge)
        def _():
            send(ch_y, u)

        @pl.when(has_out)
        def _():
            ch_z(u).wait_recv()
            cur[u, 2:4] = plus(cur[u, 2:4], chz[u])

        @pl.when(inner)
        def _():
            send(in_z, u)

        @pl.when(jnp.logical_and(outer, has_out))
        def _():
            send(ch_z, u)

    def stage3(u):
        @pl.when(has_out)
        def _():
            ch_y(u).wait_recv()
            cur[u, side] = plus(cur[u, side], chy[u])

        @pl.when(inner)
        def _():
            send(in_y, u)
            in_z(u).wait_recv()
            cur[u, 2 + keep] = plus(cur[u, 2 + keep], inz[u])
            send(y_z, u)

        @pl.when(jnp.logical_and(outer, has_out))
        def _():
            send(ch_y, u)

    def stage4(u):
        @pl.when(inner)
        def _():
            in_y(u).wait_recv()
            res[u, home + side] = plus(cur[u, side], iny[u])
            send(r_y, u)
            send(y2, u)
            y_z(u).wait_recv()
            res[u, home + 2 + keep] = plus(cur[u, 2 + keep], yz[u])
            send(r_zh, u)

    def stage5(u):
        @pl.when(outer)
        def _():
            r_y(u).wait_recv()

            @pl.when(has_out)
            def _():
                send(r_y, u)

            send(y2, u)

        @pl.when(inner)
        def _():
            message(
                RZH, u, res.at[u, home + 3 - keep], res.at[u, home + 3 - keep], inward
            ).wait_recv()
            send(r_zf, u)
            send(s_z, u)

    def stage6(u):
        message(Y2, u, res.at[u, home + 1 - side], res.at[u, home + 1 - side], across).wait_recv()
        send(s_y, u)

        @pl.when(outer)
        def _():
            r_zf(u).wait_recv()

            @pl.when(has_out)
            def _():
                send(r_zf, u)

            send(s_z, u)

    def stage7(u):
        away = 4 - home
        message(SY, u, res.at[u, pl.ds(away, 2)], res.at[u, pl.ds(away, 2)], sibling).wait_recv()
        message(SZ, u, res.at[u, pl.ds(away + 2, 2)], res.at[u, pl.ds(away + 2, 2)], sibling).wait_recv()

        @pl.when(u >= 2)
        def _():
            for t in range(width // wide):
                up_copy(half, t, u % 2).wait()

        stage[u % 2] = res[u].reshape(width, wide)

        @pl.when(u < half)
        def _():
            for t in range(width // wide):
                down_copy(u, t).start()

        @pl.when(u >= half)
        def _():
            for t in range(width // wide):
                up_copy(u, t, u % 2).start()

    stages = (stage1, stage2, stage3, stage4, stage5, stage6, stage7)

    def one(i, carry):
        @pl.when(jnp.logical_and(i > 0, i < units))
        def _():
            compute(i)

        for work, lag in reversed(list(zip(stages, LAGS))):
            u = i - lag

            @pl.when(jnp.logical_and(u >= 0, u < units))
            def _():
                work(u)

        for s in range(steps):

            @pl.when(i == s + 1)
            def _():
                small_copy(s).wait_recv()
                sm[s + 1] = sm[s] + smin[s]
                if s + 1 < steps:
                    small_copy(s + 1).start()

        return carry

    df_copy.wait()
    x_wait(0)
    x_start(2)
    product(0)
    sm[0] = small_ref[...]

    @pl.when(has_out)
    def _():
        pl.semaphore_wait(barrier, steps + 2)

    @pl.when(edge)
    def _():
        pl.semaphore_wait(barrier, steps + 1)

    c1(0).start()
    small_copy(0).start()
    lax.fori_loop(0, units + LAGS[-1], one, 0)

    small_out[...] = sm[steps]
    for s in range(steps):
        small_copy(s).wait_send()

    def drain(u, carry):
        for make in (c1, y1, y2, s_y, s_z):
            make(u).wait_send()

        @pl.when(inner)
        def _():
            for make in (in_z, in_y, y_z, r_zh):
                make(u).wait_send()

        @pl.when(has_out)
        def _():
            for make in (r_y, r_zf):
                make(u).wait_send()

        @pl.when(outer)
        def _():
            for make in (ch_y, ch_z):
                make(u).wait_send()

        return carry

    lax.fori_loop(units - RING, units, drain, 0)
    for slot in range(2):
        for t in range(width // wide):
            up_copy(half, t, slot).wait()


def run_grads(dp, a, df, h, du, small):
    count, rows, width = a.shape
    blocks, fb = h.shape[0], h.shape[-1]
    wide = fb // 3
    half = blocks * 3
    units = 2 * half
    steps = dp.bit_length() - 1
    piece = width // 8
    hidden = blocks * fb
    any_spec = pl.BlockSpec(memory_space=pl.ANY)
    vmem = pl.BlockSpec(memory_space=pltpu.VMEM)
    shape = jax.ShapeDtypeStruct
    body = functools.partial(grads_kernel, dp, count, rows, width, units, wide, 3)
    return pl.pallas_call(
        body,
        out_shape=(shape((1, hidden, width), BF), shape((1, width, hidden), BF), shape(small.shape, F32)),
        in_specs=[any_spec] * 4 + [vmem],
        out_specs=(any_spec, any_spec, vmem),
        scratch_shapes=[
            pltpu.VMEM((width, count * rows), BF),
            pltpu.VMEM((count, rows, width), BF),
            pltpu.VMEM((count, rows, width), BF),
            pltpu.VMEM((3, count, rows, wide), BF),
            pltpu.VMEM((RING, 8, piece, wide), BF),
            pltpu.VMEM((units, 4, piece, wide), BF),
            pltpu.VMEM((units, 8, piece, wide), BF),
            pltpu.VMEM((2, width, wide), BF),
            pltpu.VMEM((units, 4, piece, wide), BF),
            pltpu.VMEM((units, piece, wide), BF),
            pltpu.VMEM((units, piece, wide), BF),
            pltpu.VMEM((units, piece, wide), BF),
            pltpu.VMEM((units, 2, piece, wide), BF),
            pltpu.VMEM((units, piece, wide), BF),
            pltpu.VMEM((units, piece, wide), BF),
            pltpu.VMEM((steps + 1,) + small.shape, F32),
            pltpu.VMEM((steps,) + small.shape, F32),
            pltpu.SemaphoreType.DMA((2,)),
            pltpu.SemaphoreType.DMA((3,)),
            pltpu.SemaphoreType.DMA((2, 3)),
            pltpu.SemaphoreType.DMA((KINDS, RING)),
            pltpu.SemaphoreType.DMA((KINDS, units)),
            pltpu.SemaphoreType.DMA((steps,)),
            pltpu.SemaphoreType.DMA((steps,)),
        ],
        compiler_params=pltpu.CompilerParams(
            collective_id=1, has_side_effects=True, vmem_limit_bytes=52 * 2**20
        ),
    )(a, df, h, du, small)


def widen_kernel(act, grad, down, up, small, act_out, grad_out, g1, b1, up_out, upb, down_out, bd, g2, b2):
    act_out[...] = act[...].astype(F32)
    grad_out[...] = grad[...].astype(F32)
    up_out[...] = up[...].astype(F32)
    down_out[...] = down[...].astype(F32)

    @pl.when(pl.program_id(0) == 0)
    def _():
        width = small.shape[-1]
        for n, out in enumerate((g1, b1, g2, b2, bd)):
            out[...] = small[n : n + 1, :]
        for b in range(upb.shape[-1] // width):
            upb[:, b * width : (b + 1) * width] = small[5 + b : 6 + b, :]


def run_widen(act, grad, down, up, small):
    count, rows, width = act.shape[1:]
    hidden = down.shape[1]
    grid = 4 * count
    token = pl.BlockSpec((1, 1, rows // 4, width), lambda i: (0, i // 4, i % 4, 0))
    tall = pl.BlockSpec((1, hidden // grid, width), lambda i: (0, i, 0))
    flat = pl.BlockSpec((1, width // grid, hidden), lambda i: (0, i, 0))

    def whole(*extent):
        return pl.BlockSpec(extent, lambda i: (0, 0))

    shape = jax.ShapeDtypeStruct
    row = shape((1, width), F32)
    line = whole(1, width)
    return pl.pallas_call(
        widen_kernel,
        grid=(grid,),
        in_specs=[token, token, tall, flat, whole(*small.shape)],
        out_specs=(token, token, line, line, flat, whole(1, hidden), tall, line, line, line),
        out_shape=(
            shape(act.shape, F32), shape(grad.shape, F32), row, row, shape(up.shape, F32),
            shape((1, hidden), F32), shape(down.shape, F32), row, row, row,
        ),
        compiler_params=pltpu.CompilerParams(
            dimension_semantics=("arbitrary",), vmem_limit_bytes=12 * 2**20
        ),
    )(act, grad, down, up, small)


def per_device(
    inputs, bucket, plan, cotangent, norm1_gain, norm1_bias, up_weight, up_bias,
    down_weight, down_bias, norm2_gain, norm2_bias,
):
    count, rows, width = inputs.shape
    hidden = up_weight.shape[-1]
    norms = (norm1_gain, norm1_bias, norm2_gain, norm2_bias, down_bias)
    activations, input_grad, h, du, a, df, small = run_layers(
        bucket, plan, norms, up_bias.reshape(-1, 1, width), inputs, cotangent, up_weight, down_weight
    )
    down_grad, up_grad, small = run_grads(lax.axis_size("dp"), a, df, h, du, small)
    return run_widen(activations, input_grad, down_grad, up_grad, small)


def solution(mesh):
    row = P("pipe", None)
    weight = P("pipe", None, None)
    tokens = P(None, "dp", None)
    result = P("pipe", None, "dp", None)
    return jax.shard_map(
        per_device,
        mesh=mesh,
        in_specs=(tokens, P(), P(), tokens, row, row, weight, row, weight, row, row, row),
        out_specs=(result, result, row, row, weight, row, weight, row, row, row),
        check_vma=False,
    )
```
